32 devices in a mesh: dp: 8 (over z, x), tensor: 4 (over y, core).
Axes of the slice: x: 2, y: 2, z: 4, core: 2. Of those that a mesh axis runs over, the one named last changes fastest.
Arguments:
- hidden_in: bfloat16 [16384, 768], P(('dp', 'tensor')), may hold values from -6 to 6
- w_qkv: bfloat16 [3, 768, 768], P(None, 'dp', 'tensor'), may hold values from -0.21875 to 0.21875
- b_qkv: bfloat16 [3, 768], P(None, 'tensor'), may hold values from -1.5 to 1.5
- w_out: bfloat16 [768, 768], P('tensor', 'dp'), may hold values from -3.5 to 3.5
- b_out: bfloat16 [768], P('dp'), may hold values from -1.5 to 1.5
- w_fc: bfloat16 [768, 3072], P('dp', 'tensor'), may hold values from -0.21875 to 0.21875
- b_fc: bfloat16 [3072], P('tensor'), may hold values from -2.5 to 2.5
- w_fc2: bfloat16 [3072, 768], P('tensor', 'dp'), may hold values from -0.109375 to 0.109375
- b_fc2: bfloat16 [768], P('dp'), may hold values from -1.5 to 1.5
- ln1_gain: bfloat16 [768], P('dp'), may hold values from 0.25 to 1.75
- ln1_bias: bfloat16 [768], P('dp'), may hold values from -1.5 to 1.5
- ln2_gain: bfloat16 [768], P('dp'), may hold values from 0.25 to 1.75
- ln2_bias: bfloat16 [768], P('dp'), may hold values from -1.5 to 1.5
- segment_ids: int32 [16384], P('dp'), may hold values from 0 to 24, as said below
- positions: int32 [16384], P('dp'), may hold values from 0 to 1533, as said below
- cotangent: bfloat16 [16384, 768], P(('dp', 'tensor')), may hold values from -6 to 6
Outputs:
- layer_out: bfloat16 [16384, 768], P(('dp', 'tensor'))
- d_hidden_in: bfloat16 [16384, 768], P(('dp', 'tensor'))
- d_w_qkv: float32 [3, 768, 768], P(None, 'dp', 'tensor')
- d_b_qkv: float32 [3, 768], P(None, 'tensor')
- d_w_out: float32 [768, 768], P('tensor', 'dp')
- d_b_out: float32 [768], P('dp')
- d_w_fc: float32 [768, 3072], P('dp', 'tensor')
- d_b_fc: float32 [3072], P('tensor')
- d_w_fc2: float32 [3072, 768], P('tensor', 'dp')
- d_b_fc2: float32 [768], P('dp')
- d_ln1_gain: float32 [768], P('dp')
- d_ln1_bias: float32 [768], P('dp')
- d_ln2_gain: float32 [768], P('dp')
- d_ln2_bias: float32 [768], P('dp')
The draws below stay inside these ranges and needn't reach their ends.
Inputs may be any that keep to these rules, and one draw needn't show every extreme that they name: `segment_ids`: document numbers along the whole stream start at 0 and never fall; every document lies within the token ranges of two neighbouring blocks of 2048 tokens (blocks aligned from the stream's start), and every border between two such blocks lies inside a document. Of a document that crosses such a border, at most 767 tokens lie in the block before the border and at most as many in the block after it; some document has exactly that many on both sides. `positions`: A token's position counts from 0 at the first token of its document and rises by one per token.
All inputs are finite; a program needn't handle non-finite values.
Results may differ from the reference program's by a relative error of at most 0.0099.
Values may be sent and summed in bfloat16 or wider, within the bound.
No kernel may reach another device: no remote copies, remote signals or barrier semaphores. Data moves between devices by JAX's collectives and lax.ppermute only.
A program may use at most 192 MiB of HBM per device.

```python
import jax
import jax.numpy as jnp
from jax import lax

D = 768
HEADS = 12
HEAD_DIM = 64
ROT = 16
FF = 3072
TOK_DEV = 2048
TOKENS = 16384


def doc_layout(key, block_count, block_len):
    key_list = jax.random.split(key, 4)
    lower_len = block_len // 8
    upper_len = 3 * block_len // 8
    head_len = jax.random.randint(key_list[0], (block_count,), lower_len, upper_len)
    tail_len = jax.random.randint(key_list[1], (block_count,), lower_len, upper_len)
    longest = jax.random.randint(key_list[3], (), 0, block_count - 1)
    tail_len = tail_len.at[longest].set(upper_len - 1)
    head_len = head_len.at[longest + 1].set(upper_len - 1)
    middle = jax.random.randint(key_list[2], (block_count,), head_len + lower_len, block_len - tail_len - lower_len + 1)
    places = jnp.arange(block_len, dtype=jnp.int32)[None, :]
    border = (places == head_len[:, None]) | (places == (block_len - tail_len)[:, None])
    border = border | (places == middle[:, None])
    border = border.reshape(-1)
    segment = jnp.cumsum(border.astype(jnp.int32))
    tok_index = jnp.arange(block_count * block_len, dtype=jnp.int32)
    starts = lax.cummax(jnp.where(border, tok_index, 0), axis=0)
    return (segment.astype(jnp.int32), (tok_index - starts).astype(jnp.int32))


def draw_segment_ids(key, part):
    return doc_layout(key, TOKENS // TOK_DEV, TOK_DEV)[0]


def draw_positions(key, part):
    return doc_layout(key, TOKENS // TOK_DEV, TOK_DEV)[1]


def with_spikes(values, stream_key, source, target, blocks, factor):
    owner, partner = [(jnp.arange(values.shape[position]) // (values.shape[position] // blocks)).reshape([-1 if axis == position else 1 for axis in range(values.ndim)]) for position in (source, target)]
    chosen = jax.random.permutation(stream_key, blocks)[partner]
    strong = (owner == chosen) | (owner == (partner + blocks // 2) % blocks)
    return jnp.where(strong, factor * values, values)


def block_scale(stream_key, dims, pieces, smallest, top_value):
    loudness, own = 1.0, jax.random.fold_in(stream_key, 6)
    for axis_at, blocks in pieces:
        draws = jnp.exp(jax.random.uniform(jax.random.fold_in(own, axis_at), (blocks,), jnp.float32, smallest / len(pieces), top_value / len(pieces)))
        loudness = loudness * jnp.repeat(draws, dims[axis_at] // blocks).reshape([-1 if axis == axis_at else 1 for axis in range(len(dims))])
    return loudness


def centred(stream_key, extent, deviation, bound, cuts=(), held_as=jnp.bfloat16):
    entries = jax.random.normal(stream_key, extent, jnp.float32) * deviation
    if len(cuts) > 0:
        entries = block_scale(stream_key, extent, cuts, -0.22, 0.18) * entries
    return jnp.clip(entries, min=-bound, max=bound).astype(held_as)


def bell_draw_with(stream_key, dims, width, limit, shards, heavy, held_as=jnp.bfloat16):
    array = width * jax.random.normal(stream_key, dims, jnp.float32)
    if shards:
        array = array * block_scale(stream_key, dims, shards, -0.22, 0.18)
    return jnp.clip(with_spikes(array, jax.random.fold_in(stream_key, 3), *heavy), -limit, limit).astype(held_as)


def setup_inputs(seed: int = 0) -> dict:
    keys = jax.random.split(jax.random.key(seed), 17)
    return {
        "hidden_in": centred(keys[0], (TOKENS, D), 1.0, 6.0, ((0, 32),)),
        "w_qkv": centred(keys[1], (3, D, D), D ** -0.5, 0.21875, ((1, 8), (2, 4))),
        "b_qkv": centred(keys[2], (3, D), 0.3, 1.5, ((1, 4),)),
        "w_out": centred(keys[3], (D, D), (max(D // 256, 2)) ** -0.5, 3.5, ((0, 4), (1, 8))),
        "b_out": centred(keys[4], (D,), 0.3, 1.5, ((0, 8),)),
        "w_fc": centred(keys[5], (D, FF), D ** -0.5, 0.21875, ((0, 8), (1, 4))),
        "b_fc": centred(keys[6], (FF,), 0.5, 2.5, ((0, 4),)),
        "w_fc2": centred(keys[7], (FF, D), FF ** -0.5, 0.109375, ((0, 4), (1, 8))),
        "b_fc2": centred(keys[8], (D,), 0.3, 1.5, ((0, 8),)),
        "ln1_gain": jnp.clip(1.0 + 0.15 * jax.random.normal(keys[9], (D,), jnp.float32), 0.25, 1.75).astype(jnp.bfloat16),
        "ln1_bias": centred(keys[10], (D,), 0.3, 1.5, ((0, 8),)),
        "ln2_gain": jnp.clip(1.0 + 0.15 * jax.random.normal(keys[11], (D,), jnp.float32), 0.25, 1.75).astype(jnp.bfloat16),
        "ln2_bias": centred(keys[12], (D,), 0.3, 1.5, ((0, 8),)),
        "segment_ids": draw_segment_ids(jax.random.fold_in(keys[16], 71), 0),
        "positions": draw_positions(jax.random.fold_in(keys[16], 71), 0),
        "cotangent": bell_draw_with(keys[15], (TOKENS, D), 1.0, 6.0, ((0, 32),), (0, 1, 32, 2.75)),
    }


@jax.custom_vjp
def low(v):
    return lax.optimization_barrier(v.astype(jnp.bfloat16)).astype(jnp.float32)

@jax.custom_vjp
def low_back(v):
    return v

def low_keep(v):
    return (low(v), None)

def low_pass(kept, grad):
    return (grad,)

def back_keep(v):
    return (v, None)

def back_low(kept, grad):
    return (low(grad),)
low.defvjp(low_keep, low_pass)
low_back.defvjp(back_keep, back_low)
norm_eps = 1e-05
big_negative = -1e+30
rope_base = 10000.0
highest = lax.Precision.HIGHEST

def rope_tables(positions, rot_dims):
    freq_idx = jnp.arange(0, rot_dims, 2, dtype=jnp.float32)
    inverse = rope_base ** (-freq_idx / rot_dims)
    angles = positions.astype(jnp.float32)[:, None] * inverse[None, :]
    angles = jnp.concatenate([angles, angles], axis=1)
    return (jnp.cos(angles)[:, None, :], jnp.sin(angles)[:, None, :])

def rope_apply(values, cos_table, sin_table, rot_dims):
    half_dims = rot_dims // 2
    rotated = values[..., :rot_dims]
    turned = jnp.concatenate([-rotated[..., half_dims:], rotated[..., :half_dims]], axis=-1)
    return jnp.concatenate([rotated * cos_table + turned * sin_table, values[..., rot_dims:]], axis=-1)

def layer_norm(row_vals, gain_vec, shift_vec):
    center = row_vals - lax.optimization_barrier(jnp.mean(row_vals, axis=-1, keepdims=True))
    inv_std = lax.rsqrt(lax.optimization_barrier(jnp.mean(center * center, axis=-1, keepdims=True)) + norm_eps)
    return center * inv_std * gain_vec + shift_vec

def attend_item(block_in):
    query_blk, keys_blk, values_blk, seg_query, seg_keys, idx_query, idx_keys = block_in
    raw_scores = jnp.einsum('qd,kd->qk', query_blk, keys_blk, precision=highest)
    scores = low_back(raw_scores * HEAD_DIM ** (-0.5))
    allowed = (seg_query[:, None] == seg_keys[None, :]) & (idx_keys[None, :] <= idx_query[:, None])
    scores = jnp.where(allowed, scores, big_negative)
    prob_rows = low(jax.nn.softmax(scores, axis=-1))
    return jnp.einsum('qk,kd->qd', prob_rows, values_blk, precision=highest)

def layer_forward(hidden_in, w_qkv, b_qkv, w_out, b_out, w_fc, b_fc, w_fc2, b_fc2, ln1_gain, ln1_bias, ln2_gain, ln2_bias, segment_ids, positions):
    total_rows = hidden_in.shape[0]
    block_count = total_rows // TOK_DEV
    normed_one = low(layer_norm(hidden_in, ln1_gain, ln1_bias))
    normed_two = low(layer_norm(hidden_in, ln2_gain, ln2_bias))
    projected = low_back(jnp.einsum('td,pde->tpe', normed_one, w_qkv, precision=highest) + b_qkv[None])
    cos_table, sin_table = rope_tables(positions, ROT)
    queries = low(rope_apply(projected[:, 0].reshape(total_rows, HEADS, HEAD_DIM), cos_table, sin_table, ROT))
    keys_all = low(rope_apply(projected[:, 1].reshape(total_rows, HEADS, HEAD_DIM), cos_table, sin_table, ROT))
    values_all = low(projected[:, 2].reshape(total_rows, HEADS, HEAD_DIM))
    zero_blk = jnp.zeros((TOK_DEV, HEADS, HEAD_DIM), jnp.float32)

    def pair_blocks(padded):
        earlier = padded[:-TOK_DEV].reshape((block_count, TOK_DEV) + padded.shape[1:])
        current = padded[TOK_DEV:].reshape((block_count, TOK_DEV) + padded.shape[1:])
        return jnp.concatenate([earlier, current], axis=1)

    def head_items(blocks):
        return jnp.transpose(blocks, (0, 2, 1, 3)).reshape(block_count * HEADS, blocks.shape[1], HEAD_DIM)
    keys_pair = head_items(pair_blocks(jnp.concatenate([zero_blk, keys_all], axis=0)))
    values_pair = head_items(pair_blocks(jnp.concatenate([zero_blk, values_all], axis=0)))
    query_items = head_items(queries.reshape(block_count, TOK_DEV, HEADS, HEAD_DIM))
    tok_index = jnp.arange(total_rows, dtype=jnp.int32)
    seg_pad = jnp.concatenate([jnp.full((TOK_DEV,), -1, jnp.int32), segment_ids.astype(jnp.int32)])
    idx_pad = jnp.concatenate([tok_index[:TOK_DEV] - TOK_DEV, tok_index])
    seg_query = jnp.repeat(segment_ids.astype(jnp.int32).reshape(block_count, TOK_DEV), HEADS, axis=0)
    seg_keys = jnp.repeat(pair_blocks(seg_pad), HEADS, axis=0)
    idx_query = jnp.repeat(tok_index.reshape(block_count, TOK_DEV), HEADS, axis=0)
    idx_keys = jnp.repeat(pair_blocks(idx_pad), HEADS, axis=0)
    attended = lax.map(jax.checkpoint(attend_item), (query_items, keys_pair, values_pair, seg_query, seg_keys, idx_query, idx_keys))
    attended = jnp.transpose(attended.reshape(block_count, HEADS, TOK_DEV, HEAD_DIM), (0, 2, 1, 3))
    attended = low(low_back(attended.reshape(total_rows, D)))
    attn_branch = jnp.dot(attended, w_out, precision=highest)
    pre_act = low_back(jnp.dot(normed_two, w_fc, precision=highest) + b_fc)
    activated = low(jax.nn.gelu(pre_act, approximate=False))
    mlp_branch = jnp.dot(activated, w_fc2, precision=highest)
    return hidden_in + attn_branch + mlp_branch + b_out + b_fc2

def reference(hidden_in, w_qkv, b_qkv, w_out, b_out, w_fc, b_fc, w_fc2, b_fc2, ln1_gain, ln1_bias, ln2_gain, ln2_bias, segment_ids, positions, cotangent):
    floats = tuple((member.astype(jnp.float32) for member in (hidden_in, w_qkv, b_qkv, w_out, b_out, w_fc, b_fc, w_fc2, b_fc2, ln1_gain, ln1_bias, ln2_gain, ln2_bias)))

    def forward_fn(*params):
        return layer_forward(*params, segment_ids, positions)
    layer_out, pullback = jax.vjp(forward_fn, *floats)
    gradients = pullback(cotangent.astype(jnp.float32))
    return (layer_out.astype(jnp.bfloat16), gradients[0].astype(jnp.bfloat16), gradients[1], gradients[2], gradients[3], gradients[4], gradients[5], gradients[6], gradients[7], gradients[8], gradients[9], gradients[10], gradients[11], gradients[12])
```

```python
import functools

import jax
import jax.numpy as jnp
from jax import lax
from jax.experimental import pallas as pl
from jax.experimental.pallas import tpu as pltpu
from jax.sharding import PartitionSpec as P

HEAD_DIM = 64
ROT = 16
BLK = 256

norm_eps = 1e-05
big_negative = -1e30
rope_base = 10000.0

f32 = jnp.float32
bf16 = jnp.bfloat16


def mm(a, b, ca, cb):
    return lax.dot_general(a, b, (((ca,), (cb,)), ((), ())), preferred_element_type=f32)


def passed_along(block, axis, distance):
    devices = range(lax.axis_size(axis))
    route = [(i - distance, i) for i in devices if i - distance in devices]
    return lax.ppermute(block, axis, route)


def swapped(block, axis, bit):
    route = [(i, i ^ bit) for i in range(lax.axis_size(axis))]
    return lax.ppermute(block, axis, route)


def key_mask(chunk, lo_row, hi_row, shape):
    idx = chunk * BLK + lax.broadcasted_iota(jnp.int32, shape, 0)
    return (idx >= lo_row) & (idx <= hi_row)


def attn_fwd_kernel(heads, halo, first_ref, q_ref, k_ref, v_ref, lo_ref, o_ref, lse_ref):
    i = pl.program_id(0)
    first = first_ref[i]
    last = i + halo // BLK
    lo_row = lo_ref[...]
    hi_row = halo + i * BLK + lax.broadcasted_iota(jnp.int32, (1, BLK), 1)

    def step(c, carry):
        cols = pl.ds(pl.multiple_of(c * BLK, BLK), BLK)
        ok = key_mask(c, lo_row, hi_row, (BLK, BLK))
        out = []
        for h in range(heads):
            top, total, acc = carry[h]
            feats = pl.ds(h * HEAD_DIM, HEAD_DIM)
            s = mm(k_ref[feats, cols], q_ref[feats, :], 0, 0)
            s = jnp.where(ok, s, big_negative)
            new_top = jnp.maximum(top, jnp.max(s, axis=0, keepdims=True))
            keep = jnp.exp(top - new_top)
            p = jnp.exp(s - new_top)
            total = total * keep + jnp.sum(p, axis=0, keepdims=True)
            acc = acc * keep + mm(v_ref[feats, cols], p.astype(bf16), 1, 0)
            out.append((new_top, total, acc))
        return tuple(out)

    start = tuple(
        (
            jnp.full((1, BLK), big_negative, f32),
            jnp.zeros((1, BLK), f32),
            jnp.zeros((HEAD_DIM, BLK), f32),
        )
        for _ in range(heads)
    )
    done = lax.fori_loop(first, last + 1, step, start)
    for h in range(heads):
        top, total, acc = done[h]
        o_ref[pl.ds(h * HEAD_DIM, HEAD_DIM), :] = (acc / total).astype(bf16)
        lse_ref[pl.ds(h, 1), :] = top + jnp.log(total)


def attn_bwd_kernel(
    heads, halo, first_ref, q_ref, k_ref, v_ref, lo_ref, o_ref, lse_ref, do_ref, dq_ref, dk_ref, dv_ref
):
    i = pl.program_id(0)
    first = first_ref[i]
    last = i + halo // BLK

    @pl.when(i == 0)
    def _():
        dk_ref[...] = jnp.zeros_like(dk_ref)
        dv_ref[...] = jnp.zeros_like(dv_ref)

    lo_row = lo_ref[...]
    hi_row = halo + i * BLK + lax.broadcasted_iota(jnp.int32, (1, BLK), 1)
    dq_ref[...] = jnp.zeros_like(dq_ref)
    deltas = []
    for h in range(heads):
        feats = pl.ds(h * HEAD_DIM, HEAD_DIM)
        prod = do_ref[feats, :].astype(f32) * o_ref[feats, :].astype(f32)
        deltas.append(jnp.sum(prod, axis=0, keepdims=True))

    def step(c, carry):
        cols = pl.ds(pl.multiple_of(c * BLK, BLK), BLK)
        ok = key_mask(c, lo_row, hi_row, (BLK, BLK))
        for h in range(heads):
            feats = pl.ds(h * HEAD_DIM, HEAD_DIM)
            s = mm(k_ref[feats, cols], q_ref[feats, :], 0, 0)
            p = jnp.exp(jnp.where(ok, s, big_negative) - lse_ref[pl.ds(h, 1), :])
            dp = mm(v_ref[feats, cols], do_ref[feats, :], 0, 0)
            ds = (p * (dp - deltas[h])).astype(bf16)
            dv_ref[feats, cols] += mm(do_ref[feats, :], p.astype(bf16), 1, 1)
            dk_ref[feats, cols] += mm(q_ref[feats, :], ds, 1, 1)
            dq_ref[feats, :] += mm(k_ref[feats, cols], ds, 1, 0)
        return carry

    lax.fori_loop(first, last + 1, step, 0)
    dq_ref[...] = dq_ref[...] * HEAD_DIM ** (-0.5)


def attention_specs(feat, tokens, key_count):
    col = lambda i, *_: (0, i)
    whole = lambda i, *_: (0, 0)
    q_spec = pl.BlockSpec((feat, BLK), col)
    kv_spec = pl.BlockSpec((feat, key_count), whole)
    lo_spec = pl.BlockSpec((1, BLK), col)
    lse_spec = pl.BlockSpec((8, BLK), col)
    return q_spec, kv_spec, lo_spec, lse_spec


def attention_forward(first, q, k, v, lo, halo):
    feat, tokens = q.shape
    heads = feat // HEAD_DIM
    q_spec, kv_spec, lo_spec, lse_spec = attention_specs(feat, tokens, k.shape[1])
    return pl.pallas_call(
        functools.partial(attn_fwd_kernel, heads, halo),
        grid_spec=pltpu.PrefetchScalarGridSpec(
            num_scalar_prefetch=1,
            grid=(tokens // BLK,),
            in_specs=[q_spec, kv_spec, kv_spec, lo_spec],
            out_specs=[q_spec, lse_spec],
        ),
        out_shape=[
            jax.ShapeDtypeStruct((feat, tokens), bf16),
            jax.ShapeDtypeStruct((8, tokens), f32),
        ],
        compiler_params=pltpu.CompilerParams(vmem_limit_bytes=48 * 1024 * 1024),
        cost_estimate=pl.CostEstimate(
            flops=4 * feat * tokens * 1024, bytes_accessed=8 * feat * tokens, transcendentals=heads * tokens * 1024
        ),
        name="attention_forward",
    )(first, q, k, v, lo)


def attention_backward(first, q, k, v, lo, o, lse, do, halo):
    feat, tokens = q.shape
    heads = feat // HEAD_DIM
    q_spec, kv_spec, lo_spec, lse_spec = attention_specs(feat, tokens, k.shape[1])
    return pl.pallas_call(
        functools.partial(attn_bwd_kernel, heads, halo),
        grid_spec=pltpu.PrefetchScalarGridSpec(
            num_scalar_prefetch=1,
            grid=(tokens // BLK,),
            in_specs=[q_spec, kv_spec, kv_spec, lo_spec, q_spec, lse_spec, q_spec],
            out_specs=[q_spec, kv_spec, kv_spec],
        ),
        out_shape=[
            jax.ShapeDtypeStruct((feat, tokens), f32),
            jax.ShapeDtypeStruct(k.shape, f32),
            jax.ShapeDtypeStruct(k.shape, f32),
        ],
        compiler_params=pltpu.CompilerParams(vmem_limit_bytes=48 * 1024 * 1024),
        cost_estimate=pl.CostEstimate(
            flops=10 * feat * tokens * 1024, bytes_accessed=20 * feat * tokens, transcendentals=heads * tokens * 1024
        ),
        name="attention_backward",
    )(first, q, k, v, lo, o, lse, do)


def rope_tables(positions):
    freq_idx = jnp.arange(0, ROT, 2, dtype=f32)
    inverse = rope_base ** (-freq_idx / ROT)
    angles = inverse[:, None] * positions.astype(f32)[None, :]
    return jnp.cos(angles), jnp.sin(angles)


def rope_rows(x, cos_t, sin_t):
    half = ROT // 2
    feat, tokens = x.shape
    x = x.reshape(feat // HEAD_DIM, HEAD_DIM, tokens)
    a, b = x[:, :half], x[:, half:ROT]
    x = jnp.concatenate([a * cos_t - b * sin_t, b * cos_t + a * sin_t, x[:, ROT:]], axis=1)
    return x.reshape(feat, tokens)


def norm_stats(row_vals):
    center = row_vals - jnp.mean(row_vals, axis=-1, keepdims=True)
    inv_std = lax.rsqrt(jnp.mean(center * center, axis=-1, keepdims=True) + norm_eps)
    return (center * inv_std, inv_std)


def gelu_exact(pre_vals):
    return jax.nn.gelu(pre_vals, approximate=False)


def gather_rows(block):
    n = lax.axis_size("tensor")
    rank = lax.axis_index("tensor")
    count = block.shape[0]
    parts = {0: block}
    bit = n // 2
    while bit:
        for at in list(parts):
            parts[at ^ bit] = swapped(parts[at], "tensor", bit)
        bit //= 2
    whole = jnp.zeros((n * count,) + block.shape[1:], block.dtype)
    for at, part in parts.items():
        whole = lax.dynamic_update_slice_in_dim(whole, part, (rank ^ at) * count, 0)
    return whole


def scatter_rows(partial_sum):
    n = lax.axis_size("tensor")
    rank = lax.axis_index("tensor")
    count = partial_sum.shape[0] // n
    parts = {
        at: lax.dynamic_slice_in_dim(partial_sum, (rank ^ at) * count, count, 0) for at in range(n)
    }
    bit = 1
    while bit < n:
        kept = {}
        for at in parts:
            if not at & bit:
                came = swapped(parts[at | bit], "tensor", bit)
                kept[at] = parts[at].astype(f32) + came.astype(f32)
        bit *= 2
        parts = kept if bit >= n else {at: v.astype(bf16) for at, v in kept.items()}
    return parts[0]


def summed_over(vec, axis):
    n = lax.axis_size(axis)
    bit = 1
    while bit < n:
        vec = vec + swapped(vec, axis, bit)
        bit *= 2
    return vec


def body(
    hidden_in,
    w_qkv,
    b_qkv,
    w_out,
    b_out,
    w_fc,
    b_fc,
    w_fc2,
    b_fc2,
    ln1_gain,
    ln1_bias,
    ln2_gain,
    ln2_bias,
    segment_ids,
    positions,
    cotangent,
):
    local_dim = w_qkv.shape[2]
    ff = w_fc.shape[1]
    own_count = hidden_in.shape[0]
    own_dims = w_fc.shape[0]
    seq_len = positions.shape[0]
    halo = seq_len * 3 // 8
    qkv_dim = 3 * local_dim

    vectors = jnp.stack([b_out, b_fc2, ln1_gain, ln1_bias, ln2_gain, ln2_bias], axis=1)
    vectors = jnp.pad(vectors, ((0, 0), (0, 122)))
    packed = jnp.concatenate(
        [
            w_fc,
            w_fc2.T,
            jnp.transpose(w_qkv, (1, 0, 2)).reshape(own_dims, qkv_dim),
            w_out.T,
            vectors,
        ],
        axis=1,
    )
    rows_all = gather_rows(hidden_in)
    grads_all = gather_rows(cotangent)
    packed_all = lax.all_gather(packed, "dp", axis=0, tiled=True)
    fc_w = packed_all[:, :ff]
    fc2_w = packed_all[:, ff : 2 * ff]
    qkv_w = packed_all[:, 2 * ff : 2 * ff + qkv_dim]
    out_w = packed_all[:, 2 * ff + qkv_dim : 2 * ff + qkv_dim + local_dim]
    vecs = packed_all[:, 2 * ff + qkv_dim + local_dim :][:, :6].astype(f32).T
    out_bias, fc2_bias, gain_first, bias_first, gain_second, bias_second = [vecs[j] for j in range(6)]

    normed, inv_std = norm_stats(rows_all.astype(f32))
    normed_one = (normed * gain_first + bias_first).astype(bf16)
    normed_two = (normed * gain_second + bias_second).astype(bf16)

    cos_t, sin_t = rope_tables(positions)
    projected = mm(qkv_w, normed_one, 0, 1) + b_qkv.astype(f32).reshape(qkv_dim, 1)
    queries = (rope_rows(projected[:local_dim], cos_t, sin_t) * HEAD_DIM ** (-0.5)).astype(bf16)
    keys_own = rope_rows(projected[local_dim : 2 * local_dim], cos_t, sin_t).astype(bf16)
    values_own = projected[2 * local_dim :].astype(bf16)
    left = passed_along(jnp.concatenate([keys_own[:, -halo:], values_own[:, -halo:]], axis=0), "dp", 1)
    keys_all = jnp.concatenate([left[:local_dim], keys_own], axis=1)
    values_all = jnp.concatenate([left[local_dim:], values_own], axis=1)

    lo = halo + jnp.arange(seq_len, dtype=jnp.int32) - positions
    first = lo[::BLK] // BLK
    lo_row = lo.reshape(1, seq_len)

    attended, lse = attention_forward(first, queries, keys_all, values_all, lo_row, halo)

    pre_act = mm(normed_two, fc_w, 1, 0) + b_fc.astype(f32)
    activated = gelu_exact(pre_act).astype(bf16)
    branch = mm(attended, out_w, 0, 1) + mm(activated, fc2_w, 1, 1)
    summed = scatter_rows(branch.astype(bf16))
    layer_out = (hidden_in.astype(f32) + summed + out_bias + fc2_bias).astype(bf16)

    res_bias_grad = jnp.sum(grads_all.astype(f32), axis=0)
    attended_grad = mm(out_w, grads_all, 0, 1).astype(bf16)
    out_w_grad = mm(grads_all, attended, 0, 1)
    fc2_w_grad = mm(grads_all, activated, 0, 0)
    act_grad = mm(grads_all, fc2_w, 1, 0)
    gelu_pull = jax.vjp(gelu_exact, pre_act)[1]
    pre_grad = gelu_pull(act_grad)[0].astype(bf16)
    fc_b_grad = jnp.sum(pre_grad.astype(f32), axis=0)
    fc_w_grad = mm(normed_two, pre_grad, 0, 0)
    two_grad = mm(pre_grad, fc_w, 1, 1)
    early = jnp.concatenate([fc_w_grad, fc2_w_grad, out_w_grad], axis=1).astype(bf16)
    early_own = lax.psum_scatter(early, "dp", scatter_dimension=0, tiled=True).astype(f32)

    query_grad, key_grad, value_grad = attention_backward(
        first, queries, keys_all, values_all, lo_row, attended, lse, attended_grad, halo
    )
    back = passed_along(
        jnp.concatenate([key_grad[:, :halo], value_grad[:, :halo]], axis=0).astype(bf16), "dp", -1
    )
    back = jnp.pad(back.astype(f32), ((0, 0), (seq_len - halo, 0)))
    key_total = key_grad[:, halo:] + back[:local_dim]
    value_total = value_grad[:, halo:] + back[local_dim:]
    proj_grad = jnp.concatenate(
        [rope_rows(query_grad, cos_t, -sin_t), rope_rows(key_total, cos_t, -sin_t), value_total], axis=0
    ).astype(bf16)
    qkv_b_grad = jnp.sum(proj_grad.astype(f32), axis=1)
    qkv_w_grad = mm(normed_one, proj_grad, 0, 1).astype(bf16)
    one_grad = mm(proj_grad, qkv_w, 0, 1)
    qkv_own = lax.psum_scatter(qkv_w_grad, "dp", scatter_dimension=0, tiled=True).astype(f32)

    both = scatter_rows((one_grad * gain_first + two_grad * gain_second).astype(bf16))
    normed_own, inv_own = norm_stats(hidden_in.astype(f32))
    input_grad = cotangent.astype(f32) + inv_own * (
        both
        - jnp.mean(both, axis=-1, keepdims=True)
        - normed_own * jnp.mean(both * normed_own, axis=-1, keepdims=True)
    )

    norm_rows = jnp.stack(
        [
            jnp.sum(one_grad * normed, axis=0),
            jnp.sum(one_grad, axis=0),
            jnp.sum(two_grad * normed, axis=0),
            jnp.sum(two_grad, axis=0),
        ]
    )
    norm_rows = summed_over(norm_rows, "tensor")
    width = res_bias_grad.shape[0]
    fc_rows = jnp.pad(fc_b_grad, (0, -ff % width)).reshape(-1, width)
    qkv_rows = jnp.pad(qkv_b_grad, (0, -qkv_dim % width)).reshape(-1, width)
    small = jnp.concatenate([norm_rows, res_bias_grad[None], fc_rows, qkv_rows], axis=0)
    small = summed_over(small, "dp")
    own = lax.dynamic_slice_in_dim(small[:5], lax.axis_index("dp") * own_dims, own_dims, 1)
    fc_b_total = small[5 : 5 + fc_rows.shape[0]].reshape(-1)[:ff]
    qkv_b_total = small[5 + fc_rows.shape[0] :].reshape(-1)[:qkv_dim].reshape(3, local_dim)
    return (
        layer_out,
        input_grad.astype(bf16),
        jnp.transpose(qkv_own.reshape(own_dims, 3, local_dim), (1, 0, 2)),
        qkv_b_total,
        early_own[:, 2 * ff :].T,
        own[4],
        early_own[:, :ff],
        fc_b_total,
        early_own[:, ff : 2 * ff].T,
        own[4],
        own[0],
        own[1],
        own[2],
        own[3],
    )


def solution(mesh):
    in_specs = (
        P(("dp", "tensor"), None),
        P(None, "dp", "tensor"),
        P(None, "tensor"),
        P("tensor", "dp"),
        P("dp"),
        P("dp", "tensor"),
        P("tensor"),
        P("tensor", "dp"),
        P("dp"),
        P("dp"),
        P("dp"),
        P("dp"),
        P("dp"),
        P("dp"),
        P("dp"),
        P(("dp", "tensor"), None),
    )
    out_specs = (
        P(("dp", "tensor"), None),
        P(("dp", "tensor"), None),
        P(None, "dp", "tensor"),
        P(None, "tensor"),
        P("tensor", "dp"),
        P("dp"),
        P("dp", "tensor"),
        P("tensor"),
        P("tensor", "dp"),
        P("dp"),
        P("dp"),
        P("dp"),
        P("dp"),
        P("dp"),
    )
    return jax.shard_map(body, mesh=mesh, in_specs=in_specs, out_specs=out_specs, check_vma=False)
```

```python
import functools

import jax
import jax.numpy as jnp
from jax import lax
from jax.experimental import pallas as pl
from jax.experimental.pallas import tpu as pltpu
from jax.sharding import PartitionSpec as P

HEAD_DIM = 64
ROT = 16
BLK = 256
SLOTS = (0, 2, 1, 3)

norm_eps = 1e-05
big_negative = -1e30
rope_base = 10000.0
inv_sqrt_two = 0.7071067811865476
inv_sqrt_two_pi = 0.3989422804014327

f32 = jnp.float32
bf16 = jnp.bfloat16


def mm(a, b, ca, cb):
    return lax.dot_general(a, b, (((ca,), (cb,)), ((), ())), preferred_element_type=f32)


def params(**kw):
    return pltpu.CompilerParams(vmem_limit_bytes=56 * 1024 * 1024, **kw)


def cost(flops, moved, exps=0):
    return pl.CostEstimate(flops=int(flops), bytes_accessed=int(moved), transcendentals=int(exps))


def shaped(shape, dtype):
    return jax.ShapeDtypeStruct(shape, dtype)


def passed_along(block, axis, distance):
    devices = range(lax.axis_size(axis))
    route = [(i - distance, i) for i in devices if i - distance in devices]
    return lax.ppermute(block, axis, route)


def swapped(block, axis, bit):
    route = [(i, i ^ bit) for i in range(lax.axis_size(axis))]
    return lax.ppermute(block, axis, route)


def ring_order(n):
    return list(range(0, n, 2)) + list(range(n - 1, 0, -2))


def ring_gather(block, axis):
    n = lax.axis_size(axis)
    if n > 8:
        return [lax.all_gather(block, axis, axis=0, tiled=True)], jnp.zeros((1,), jnp.int32)
    ring = ring_order(n)
    ahead = [(ring[r], ring[(r + 1) % n]) for r in range(n)]
    behind = [(b, a) for a, b in ahead]
    table = []
    for device in range(n):
        at = ring.index(device)
        row = [device]
        for step in range(1, n // 2 + 1):
            row.append(ring[(at - step) % n])
            if step < n - step:
                row.append(ring[(at + step) % n])
        table.append(row)
    pieces = [block]
    from_left = from_right = block
    for step in range(1, n // 2 + 1):
        from_left = lax.ppermute(from_left, axis, ahead)
        pieces.append(from_left)
        if step < n - step:
            from_right = lax.ppermute(from_right, axis, behind)
            pieces.append(from_right)
    return pieces, jnp.asarray(table, jnp.int32)[lax.axis_index(axis)]


def gather_rows(block):
    far = swapped(block, "tensor", 2)
    near = swapped(block, "tensor", 1)
    both = swapped(far, "tensor", 1)
    return jnp.concatenate([block, far, near, both], axis=0)


def scatter_rows(keep, send):
    count = keep.shape[0] // 2
    came = swapped(send, "tensor", 1)
    other = (keep[count:].astype(f32) + came[count:].astype(f32)).astype(bf16)
    far = swapped(other, "tensor", 2)
    return keep[:count].astype(f32) + came[:count].astype(f32) + far.astype(f32)


def summed_over(vec, axis):
    n = lax.axis_size(axis)
    bit = 1
    while bit < n:
        vec = vec + swapped(vec, axis, bit)
        bit *= 2
    return vec


def assemble(piece_refs, owner_ref, out_ref):
    for n, ref in enumerate(piece_refs):
        rows = ref.shape[0]
        out_ref[pl.ds(pl.multiple_of(owner_ref[n] * rows, rows), rows), :] = ref[...]


def norm_rows(x):
    center = x - jnp.mean(x, axis=-1, keepdims=True)
    inv_std = lax.rsqrt(jnp.mean(center * center, axis=-1, keepdims=True) + norm_eps)
    return center * inv_std


def ff_kernel(pieces, owner_ref, x_ref, g_ref, b_ref, *refs):
    fc_refs, fc2_refs = refs[:pieces], refs[pieces : 2 * pieces]
    out_ref, u_ref, grads_ref, vec_ref, small_ref = refs[2 * pieces : 2 * pieces + 5]
    packed, fc2_w, fc_acc, fc2_acc = refs[2 * pieces + 5 :]
    step = pl.program_id(0)
    ff = fc2_w.shape[1]

    @pl.when(step == 0)
    def _():
        assemble(fc_refs, owner_ref, packed)
        assemble(fc2_refs, owner_ref, fc2_w)
        vec_ref[...] = packed[:, ff:].astype(f32).T[:8]
        fc_acc[...] = jnp.zeros_like(fc_acc)
        fc2_acc[...] = jnp.zeros_like(fc2_acc)
        small_ref[...] = jnp.zeros_like(small_ref)

    fc_w = packed[:, :ff]
    gain, shift = vec_ref[4:5, :], vec_ref[5:6, :]
    normed = norm_rows(x_ref[...].astype(f32))
    normed_two = (normed * gain + shift).astype(bf16)
    pre = mm(normed_two, fc_w, 1, 0) + b_ref[...]
    cdf = 0.5 + 0.5 * lax.erf(pre * inv_sqrt_two)
    act = (pre * cdf).astype(bf16)
    slope = cdf + pre * (jnp.exp(-0.5 * pre * pre) * inv_sqrt_two_pi)
    out_ref[...] = mm(act, fc2_w[...], 1, 1).astype(bf16)
    g = g_ref[...]
    pre_grad = (mm(g, fc2_w[...], 1, 0) * slope).astype(bf16)
    two_grad = mm(pre_grad, fc_w, 1, 1)
    u_ref[...] = (two_grad * gain).astype(bf16)
    fc_acc[...] += mm(normed_two, pre_grad, 0, 0)
    fc2_acc[...] += mm(g, act, 0, 0)
    small_ref[0:1, :] += jnp.sum(two_grad * normed, axis=0, keepdims=True)
    small_ref[1:2, :] += jnp.sum(two_grad, axis=0, keepdims=True)
    small_ref[2:3, :] += jnp.sum(g.astype(f32), axis=0, keepdims=True)
    small_ref[3:4, :] += jnp.sum(pre_grad.astype(f32), axis=0, keepdims=True)

    @pl.when(step == pl.num_programs(0) - 1)
    def _():
        grads_ref[:, :ff] = fc_acc[...].astype(bf16)
        grads_ref[:, ff:] = fc2_acc[...].astype(bf16)


def feed_forward(owner, x, g, b_fc, fc_pieces, fc2_pieces, ff):
    tokens, dim = x.shape
    rows = tokens // 4
    spec = pl.BlockSpec((rows, dim), lambda s, *_: (s, 0))
    whole = lambda shape: pl.BlockSpec(shape, lambda s, *_: (0, 0))
    return pl.pallas_call(
        functools.partial(ff_kernel, len(fc_pieces)),
        grid_spec=pltpu.PrefetchScalarGridSpec(
            num_scalar_prefetch=1,
            grid=(4,),
            in_specs=[spec, spec, whole((1, ff))] + [whole(p.shape) for p in fc_pieces + fc2_pieces],
            out_specs=[spec, spec, whole((dim, 2 * ff)), whole((8, dim)), whole((8, dim))],
            scratch_shapes=[
                pltpu.VMEM((dim, fc_pieces[0].shape[1]), bf16),
                pltpu.VMEM((dim, ff), bf16),
                pltpu.VMEM((dim, ff), f32),
                pltpu.VMEM((dim, ff), f32),
            ],
        ),
        out_shape=[
            shaped((tokens, dim), bf16),
            shaped((tokens, dim), bf16),
            shaped((dim, 2 * ff), bf16),
            shaped((8, dim), f32),
            shaped((8, dim), f32),
        ],
        compiler_params=params(),
        cost_estimate=cost(12 * tokens * dim * ff, 8 * tokens * dim + 8 * dim * ff, 2 * tokens * ff),
        name="feed_forward",
    )(owner, x, g, b_fc, *fc_pieces, *fc2_pieces)


def turned(x, cos_t, sin_t):
    half = ROT // 2
    out = []
    for h in range(x.shape[0] // HEAD_DIM):
        a = x[h * HEAD_DIM : h * HEAD_DIM + half]
        b = x[h * HEAD_DIM + half : h * HEAD_DIM + ROT]
        out += [a * cos_t - b * sin_t, b * cos_t + a * sin_t, x[h * HEAD_DIM + ROT : (h + 1) * HEAD_DIM]]
    return jnp.concatenate(out, axis=0)


def project_kernel(pieces, owner_ref, place_ref, x_ref, g_ref, vec_ref, b_ref, cos_ref, sin_ref, *refs):
    w_refs = refs[:pieces]
    normed_ref, q_ref, k_ref, v_ref, do_ref, wt_ref, packed = refs[pieces:]
    feat = q_ref.shape[0]

    @pl.when(pl.program_id(0) == 0)
    def _():
        assemble(w_refs, owner_ref, packed)
        wt_ref[...] = packed[...].astype(f32).T.astype(bf16)

    normed = norm_rows(x_ref[...].astype(f32))
    normed_one = (normed * vec_ref[2:3, :] + vec_ref[3:4, :]).astype(bf16)
    normed_ref[...] = normed_one
    proj = mm(wt_ref[: 3 * feat, :], normed_one, 1, 1) + b_ref[...]
    cos_t, sin_t = cos_ref[...], sin_ref[...]
    q_ref[...] = (turned(proj[:feat], cos_t, sin_t) * HEAD_DIM ** (-0.5)).astype(bf16)
    k_ref[...] = turned(proj[feat : 2 * feat], cos_t, sin_t).astype(bf16)
    v_ref[...] = proj[2 * feat :].astype(bf16)
    do_ref[...] = mm(wt_ref[3 * feat :, :], g_ref[...], 1, 1).astype(bf16)


def project(owner, places, x, g, vec, b_col, cos_t, sin_t, pieces, feat):
    tokens, dim = x.shape
    rows = tokens // 4
    spec = pl.BlockSpec((rows, dim), lambda s, *_: (s, 0))
    placed = lambda r: pl.BlockSpec((r, rows), lambda s, owner, place: (0, place[s]))
    whole = lambda shape: pl.BlockSpec(shape, lambda s, *_: (0, 0))
    width = pieces[0].shape[1]
    return pl.pallas_call(
        functools.partial(project_kernel, len(pieces)),
        grid_spec=pltpu.PrefetchScalarGridSpec(
            num_scalar_prefetch=2,
            grid=(4,),
            in_specs=[spec, spec, whole(vec.shape), whole(b_col.shape), placed(ROT // 2), placed(ROT // 2)]
            + [whole(p.shape) for p in pieces],
            out_specs=[spec, placed(feat), placed(feat), placed(feat), placed(feat), whole((width, dim))],
            scratch_shapes=[pltpu.VMEM((dim, width), bf16)],
        ),
        out_shape=[shaped((tokens, dim), bf16)]
        + [shaped((feat, tokens), bf16)] * 4
        + [shaped((width, dim), bf16)],
        compiler_params=params(),
        cost_estimate=cost(8 * tokens * dim * feat, 6 * tokens * dim + 4 * dim * width),
        name="project",
    )(owner, places, x, g, vec, b_col, cos_t, sin_t, *pieces)


def key_mask(chunk, lo_row, hi_row, shape):
    idx = chunk * BLK + lax.broadcasted_iota(jnp.int32, shape, 0)
    return (idx >= lo_row) & (idx <= hi_row)


def attn_fwd_kernel(heads, halo, first_ref, q_ref, k_ref, v_ref, left_ref, lo_ref, o_ref, lse_ref, keys, values):
    i = pl.program_id(0)
    first = first_ref[i]
    last = i + halo // BLK
    feat = k_ref.shape[0]

    @pl.when(i == 0)
    def _():
        keys[:, :halo] = left_ref[:feat, :]
        keys[:, halo:] = k_ref[...]
        values[:, :halo] = left_ref[feat:, :]
        values[:, halo:] = v_ref[...]

    lo_row = lo_ref[...]
    hi_row = halo + i * BLK + lax.broadcasted_iota(jnp.int32, (1, BLK), 1)

    def step(c, carry):
        cols = pl.ds(pl.multiple_of(c * BLK, BLK), BLK)
        ok = key_mask(c, lo_row, hi_row, (BLK, BLK))
        out = []
        for h in range(heads):
            top, total, acc = carry[h]
            feats = pl.ds(h * HEAD_DIM, HEAD_DIM)
            s = mm(keys[feats, cols], q_ref[feats, :], 0, 0)
            s = jnp.where(ok, s, big_negative)
            new_top = jnp.maximum(top, jnp.max(s, axis=0, keepdims=True))
            kept = jnp.exp(top - new_top)
            p = jnp.exp(s - new_top)
            total = total * kept + jnp.sum(p, axis=0, keepdims=True)
            acc = acc * kept + mm(values[feats, cols], p.astype(bf16), 1, 0)
            out.append((new_top, total, acc))
        return tuple(out)

    start = tuple(
        (
            jnp.full((1, BLK), big_negative, f32),
            jnp.zeros((1, BLK), f32),
            jnp.zeros((HEAD_DIM, BLK), f32),
        )
        for _ in range(heads)
    )
    done = lax.fori_loop(first, last + 1, step, start)
    for h in range(heads):
        top, total, acc = done[h]
        o_ref[pl.ds(h * HEAD_DIM, HEAD_DIM), :] = (acc / total).astype(bf16)
        lse_ref[pl.ds(h, 1), :] = top + jnp.log(total)


def attention_forward(first, q, k, v, left, lo, halo):
    feat, tokens = q.shape
    heads = feat // HEAD_DIM
    col = lambda i, *_: (0, i)
    whole = lambda shape: pl.BlockSpec(shape, lambda i, *_: (0, 0))
    q_spec = pl.BlockSpec((feat, BLK), col)
    return pl.pallas_call(
        functools.partial(attn_fwd_kernel, heads, halo),
        grid_spec=pltpu.PrefetchScalarGridSpec(
            num_scalar_prefetch=1,
            grid=(tokens // BLK,),
            in_specs=[q_spec, whole(k.shape), whole(v.shape), whole(left.shape), pl.BlockSpec((1, BLK), col)],
            out_specs=[q_spec, pl.BlockSpec((8, BLK), col)],
            scratch_shapes=[pltpu.VMEM((feat, halo + tokens), bf16)] * 2,
        ),
        out_shape=[shaped((feat, tokens), bf16), shaped((8, tokens), f32)],
        compiler_params=params(),
        cost_estimate=cost(16 * feat * tokens * 1024, 8 * feat * tokens, heads * tokens * 1024),
        name="attention_forward",
    )(first, q, k, v, left, lo)


def attn_bwd_step(heads, c, base, q_ref, k_ref, v_ref, do_ref, lse_ref, lo_row, hi_row, deltas, dq_ref, dk_ref, dv_ref):
    cols = pl.ds(pl.multiple_of((c - base) * BLK, BLK), BLK)
    ok = key_mask(c, lo_row, hi_row, (BLK, BLK))
    for h in range(heads):
        feats = pl.ds(h * HEAD_DIM, HEAD_DIM)
        s = mm(k_ref[feats, cols], q_ref[feats, :], 0, 0)
        p = jnp.exp(jnp.where(ok, s, big_negative) - lse_ref[pl.ds(h, 1), :])
        dp = mm(v_ref[feats, cols], do_ref[feats, :], 0, 0)
        ds = (p * (dp - deltas[h])).astype(bf16)
        dv_ref[feats, cols] += mm(do_ref[feats, :], p.astype(bf16), 1, 1)
        dk_ref[feats, cols] += mm(q_ref[feats, :], ds, 1, 1)
        dq_ref[feats, :] += mm(k_ref[feats, cols], ds, 1, 0)


def row_deltas(heads, o_ref, do_ref):
    deltas = []
    for h in range(heads):
        feats = pl.ds(h * HEAD_DIM, HEAD_DIM)
        prod = do_ref[feats, :].astype(f32) * o_ref[feats, :].astype(f32)
        deltas.append(jnp.sum(prod, axis=0, keepdims=True))
    return deltas


def halo_bwd_kernel(heads, halo, first_ref, q_ref, left_ref, lo_ref, o_ref, lse_ref, do_ref, dq_ref, back_ref, dk, dv):
    i = pl.program_id(0)
    feat = q_ref.shape[0]

    @pl.when(i == 0)
    def _():
        dk[...] = jnp.zeros_like(dk)
        dv[...] = jnp.zeros_like(dv)

    lo_row = lo_ref[...]
    hi_row = jnp.full((1, BLK), halo, jnp.int32)
    dq_ref[...] = jnp.zeros_like(dq_ref)
    deltas = row_deltas(heads, o_ref, do_ref)
    k_ref, v_ref = left_ref.at[:feat, :], left_ref.at[feat:, :]

    def step(c, carry):
        attn_bwd_step(
            heads, c, 0, q_ref, k_ref, v_ref, do_ref, lse_ref, lo_row, hi_row, deltas, dq_ref, dk, dv
        )
        return carry

    lax.fori_loop(first_ref[i], halo // BLK, step, 0)

    @pl.when(i == pl.num_programs(0) - 1)
    def _():
        back_ref[:feat, :] = dk[...].astype(bf16)
        back_ref[feat:, :] = dv[...].astype(bf16)


def own_bwd_kernel(
    heads, halo, first_ref, q_ref, k_ref, v_ref, lo_ref, o_ref, lse_ref, do_ref, part_ref, dq_ref, dk_ref, dv_ref
):
    i = pl.program_id(0)
    base = halo // BLK

    @pl.when(i == 0)
    def _():
        dk_ref[...] = jnp.zeros_like(dk_ref)
        dv_ref[...] = jnp.zeros_like(dv_ref)

    @pl.when(i < base)
    def _():
        dq_ref[...] = part_ref[...]

    @pl.when(i >= base)
    def _():
        dq_ref[...] = jnp.zeros_like(dq_ref)

    lo_row = lo_ref[...]
    hi_row = halo + i * BLK + lax.broadcasted_iota(jnp.int32, (1, BLK), 1)
    deltas = row_deltas(heads, o_ref, do_ref)

    def step(c, carry):
        attn_bwd_step(
            heads, c, base, q_ref, k_ref, v_ref, do_ref, lse_ref, lo_row, hi_row, deltas, dq_ref, dk_ref, dv_ref
        )
        return carry

    lax.fori_loop(jnp.maximum(first_ref[i], base), i + base + 1, step, 0)
    dq_ref[...] = dq_ref[...] * HEAD_DIM ** (-0.5)


def attention_backward(first, q, k, v, left, lo, o, lse, do, halo):
    feat, tokens = q.shape
    heads = feat // HEAD_DIM
    col = lambda i, *_: (0, i)
    whole = lambda shape: pl.BlockSpec(shape, lambda i, *_: (0, 0))
    q_spec = pl.BlockSpec((feat, BLK), col)
    lo_spec = pl.BlockSpec((1, BLK), col)
    lse_spec = pl.BlockSpec((8, BLK), col)
    dq_part, back = pl.pallas_call(
        functools.partial(halo_bwd_kernel, heads, halo),
        grid_spec=pltpu.PrefetchScalarGridSpec(
            num_scalar_prefetch=1,
            grid=(halo // BLK,),
            in_specs=[q_spec, whole(left.shape), lo_spec, q_spec, lse_spec, q_spec],
            out_specs=[q_spec, whole(left.shape)],
            scratch_shapes=[pltpu.VMEM((feat, halo), f32)] * 2,
        ),
        out_shape=[shaped((feat, halo), f32), shaped(left.shape, bf16)],
        compiler_params=params(),
        cost_estimate=cost(20 * feat * halo * 512, 20 * feat * halo, heads * halo * 512),
        name="attention_backward_left",
    )(first, q, left, lo, o, lse, do)
    back = passed_along(back, "dp", -1)
    part_spec = pl.BlockSpec((feat, BLK), lambda i, *_: (0, jnp.minimum(i, halo // BLK - 1)))
    dq, dk, dv = pl.pallas_call(
        functools.partial(own_bwd_kernel, heads, halo),
        grid_spec=pltpu.PrefetchScalarGridSpec(
            num_scalar_prefetch=1,
            grid=(tokens // BLK,),
            in_specs=[
                q_spec,
                whole(k.shape),
                whole(v.shape),
                lo_spec,
                q_spec,
                lse_spec,
                q_spec,
                part_spec,
            ],
            out_specs=[q_spec, whole(k.shape), whole(v.shape)],
        ),
        out_shape=[shaped((feat, tokens), f32)] * 3,
        compiler_params=params(),
        cost_estimate=cost(40 * feat * tokens * 1024, 20 * feat * tokens, heads * tokens * 1024),
        name="attention_backward_own",
    )(first, q, k, v, lo, o, lse, do, dq_part)
    return dq, dk, dv, back


def keep_send_specs(rows, dim):
    keep = pl.BlockSpec((rows, dim), lambda s, *_: (jnp.minimum(s, 1), 0))
    send = pl.BlockSpec((rows, dim), lambda s, *_: (jnp.maximum(s - 2, 0), 0))
    return keep, send


def put_rows(keep_ref, send_ref, value):
    s = pl.program_id(0)

    @pl.when(s < 2)
    def _():
        keep_ref[...] = value

    @pl.when(s >= 2)
    def _():
        send_ref[...] = value


def out_kernel(place_ref, o_ref, ff_ref, w_ref, keep_ref, send_ref):
    total = mm(o_ref[...], w_ref[...], 0, 0) + ff_ref[...].astype(f32)
    put_rows(keep_ref, send_ref, total.astype(bf16))


def branch_out(places, o, ff_out, out_w):
    feat, tokens = o.shape
    dim = out_w.shape[1]
    rows = tokens // 4
    keep, send = keep_send_specs(rows, dim)
    return pl.pallas_call(
        out_kernel,
        grid_spec=pltpu.PrefetchScalarGridSpec(
            num_scalar_prefetch=1,
            grid=(4,),
            in_specs=[
                pl.BlockSpec((feat, rows), lambda s, place: (0, place[s])),
                pl.BlockSpec((rows, dim), lambda s, *_: (s, 0)),
                pl.BlockSpec((feat, dim), lambda s, *_: (0, 0)),
            ],
            out_specs=[keep, send],
        ),
        out_shape=[shaped((tokens // 2, dim), bf16)] * 2,
        compiler_params=params(),
        cost_estimate=cost(2 * feat * tokens * dim, 4 * tokens * dim),
        name="branch_out",
    )(places, o, ff_out, out_w)


def tail_kernel(
    halo,
    place_ref,
    chunk_ref,
    dq_ref,
    dk_ref,
    dv_ref,
    back_ref,
    o_ref,
    x_ref,
    g_ref,
    n1_ref,
    u2_ref,
    wt_ref,
    vec_ref,
    cos_ref,
    sin_ref,
    keep_ref,
    send_ref,
    wkeep_ref,
    wsend_ref,
    small_ref,
    bias_ref,
    acc,
    late,
):
    s = pl.program_id(0)
    feat, rows = dq_ref.shape
    tokens = late.shape[1]

    @pl.when(s == 0)
    def _():
        late[:, : tokens - halo] = jnp.zeros((2 * feat, tokens - halo), bf16)
        late[:, tokens - halo :] = back_ref[...]
        acc[...] = jnp.zeros_like(acc)
        small_ref[...] = jnp.zeros_like(small_ref)
        bias_ref[...] = jnp.zeros_like(bias_ref)

    cols = pl.ds(pl.multiple_of(place_ref[s] * rows, rows), rows)
    cos_t, sin_t = cos_ref[...], -sin_ref[...]
    dq = turned(dq_ref[...], cos_t, sin_t)
    dk = turned(dk_ref[...] + late[:feat, cols].astype(f32), cos_t, sin_t)
    dv = dv_ref[...] + late[feat:, cols].astype(f32)
    grad = jnp.concatenate([dq, dk, dv], axis=0).astype(bf16)
    bias_ref[...] += jnp.sum(grad.astype(f32), axis=1, keepdims=True)
    one_grad = mm(grad, wt_ref[: 3 * feat, :], 0, 0)
    put_rows(keep_ref, send_ref, (one_grad * vec_ref[2:3, :] + u2_ref[...].astype(f32)).astype(bf16))
    acc[: 3 * feat, :] += mm(grad, n1_ref[...], 1, 0)
    acc[3 * feat :, :] += mm(o_ref[...], g_ref[...], 1, 0)
    normed = norm_rows(x_ref[...].astype(f32))
    small_ref[0:1, :] += jnp.sum(one_grad * normed, axis=0, keepdims=True)
    small_ref[1:2, :] += jnp.sum(one_grad, axis=0, keepdims=True)

    @pl.when(s == pl.num_programs(0) - 1)
    def _():
        acc_t = acc[...].T
        acc[...] = acc_t
        count = wkeep_ref.shape[0]
        parts = chunk_ref.shape[0] // 2
        size = count // parts
        for n in range(parts):
            at = pl.ds(pl.multiple_of(chunk_ref[n] * size, size), size)
            wkeep_ref[n * size : (n + 1) * size, :] = acc[at, :].astype(bf16)
            at = pl.ds(pl.multiple_of(chunk_ref[parts + n] * size, size), size)
            wsend_ref[n * size : (n + 1) * size, :] = acc[at, :].astype(bf16)


def tail(places, chunks, dq, dk, dv, back, o, x, g, n1, u2, wt, vec, cos_t, sin_t, halo):
    feat, tokens = dq.shape
    dim = x.shape[1]
    width = wt.shape[0]
    rows = tokens // 4
    spec = pl.BlockSpec((rows, dim), lambda s, *_: (s, 0))
    placed = lambda r: pl.BlockSpec((r, rows), lambda s, place, chunk: (0, place[s]))
    whole = lambda shape: pl.BlockSpec(shape, lambda s, *_: (0, 0))
    keep, send = keep_send_specs(rows, dim)
    return pl.pallas_call(
        functools.partial(tail_kernel, halo),
        grid_spec=pltpu.PrefetchScalarGridSpec(
            num_scalar_prefetch=2,
            grid=(4,),
            in_specs=[placed(feat)] * 3
            + [whole(back.shape), placed(feat), spec, spec, spec, spec, whole(wt.shape), whole(vec.shape)]
            + [placed(ROT // 2)] * 2,
            out_specs=[
                keep,
                send,
                whole((dim // 2, width)),
                whole((dim // 2, width)),
                whole((8, dim)),
                whole((3 * feat, 1)),
            ],
            scratch_shapes=[pltpu.VMEM((width, dim), f32), pltpu.VMEM((2 * feat, tokens), bf16)],
        ),
        out_shape=[shaped((tokens // 2, dim), bf16)] * 2
        + [shaped((dim // 2, width), bf16)] * 2
        + [shaped((8, dim), f32), shaped((3 * feat, 1), f32)],
        compiler_params=params(),
        cost_estimate=cost(14 * feat * tokens * dim, 14 * tokens * dim + 6 * dim * width),
        name="tail",
    )(places, chunks, dq, dk, dv, back, o, x, g, n1, u2, wt, vec, cos_t, sin_t)


def rope_tables(positions):
    freq_idx = jnp.arange(0, ROT, 2, dtype=f32)
    inverse = rope_base ** (-freq_idx / ROT)
    angles = inverse[:, None] * positions.astype(f32)[None, :]
    return jnp.cos(angles), jnp.sin(angles)


def late_chunks():
    n = lax.axis_size("dp")
    rank = lax.axis_index("dp")
    if n > 8:
        return jnp.arange(2, dtype=jnp.int32)
    mine = jnp.stack([rank ^ (2 * k) for k in range(n // 2)])
    return jnp.concatenate([mine, mine ^ 1]).astype(jnp.int32)


def late_scatter(keep, send):
    n = lax.axis_size("dp")
    if n > 8:
        whole = jnp.concatenate([keep, send], axis=0)
        return lax.psum_scatter(whole, "dp", scatter_dimension=0, tiled=True).astype(f32)
    size = keep.shape[0] * 2 // n
    total = keep.astype(f32) + swapped(send, "dp", 1).astype(f32)
    low = total.astype(bf16)
    own = total[:size]
    for k in range(1, n // 2):
        own = own + swapped(low[k * size : (k + 1) * size], "dp", 2 * k).astype(f32)
    return own


def body(
    hidden_in,
    w_qkv,
    b_qkv,
    w_out,
    b_out,
    w_fc,
    b_fc,
    w_fc2,
    b_fc2,
    ln1_gain,
    ln1_bias,
    ln2_gain,
    ln2_bias,
    segment_ids,
    positions,
    cotangent,
):
    local_dim = w_qkv.shape[2]
    ff = w_fc.shape[1]
    own_dims = w_fc.shape[0]
    seq_len = positions.shape[0]
    halo = seq_len * 3 // 8
    qkv_dim = 3 * local_dim
    rank = lax.axis_index("tensor")
    places = jnp.stack([rank ^ at for at in SLOTS]).astype(jnp.int32)

    vectors = jnp.stack([b_out, b_fc2, ln1_gain, ln1_bias, ln2_gain, ln2_bias], axis=1)
    vectors = jnp.pad(vectors, ((0, 0), (0, 122)))
    first_block = jnp.concatenate([w_fc, vectors], axis=1)
    third_block = jnp.concatenate(
        [jnp.transpose(w_qkv, (1, 0, 2)).reshape(own_dims, qkv_dim), w_out.T], axis=1
    )
    x_all = gather_rows(hidden_in)
    fc_pieces, owner = ring_gather(first_block, "dp")
    fc2_pieces, _ = ring_gather(w_fc2.T, "dp")
    g_all = gather_rows(cotangent)
    attn_pieces, _ = ring_gather(third_block, "dp")

    cos_t, sin_t = rope_tables(positions)
    lo = halo + jnp.arange(seq_len, dtype=jnp.int32) - positions
    first = lo[::BLK] // BLK
    lo_row = lo.reshape(1, seq_len)

    ff_out, u_two, ff_grads, vec, ff_small = feed_forward(
        owner, x_all, g_all, b_fc.astype(f32).reshape(1, ff), fc_pieces, fc2_pieces, ff
    )
    ff_own = lax.psum_scatter(ff_grads, "dp", scatter_dimension=0, tiled=True).astype(f32)

    normed_one, q, k, v, do, wt = project(
        owner, places, x_all, g_all, vec, b_qkv.astype(f32).reshape(qkv_dim, 1), cos_t, sin_t, attn_pieces, local_dim
    )
    left = passed_along(jnp.concatenate([k[:, -halo:], v[:, -halo:]], axis=0), "dp", 1)
    o, lse = attention_forward(first, q, k, v, left, lo_row, halo)
    summed = scatter_rows(*branch_out(places, o, ff_out, wt[qkv_dim:]))
    layer_out = (hidden_in.astype(f32) + summed + vec[0] + vec[1]).astype(bf16)

    dq, dk, dv, back = attention_backward(first, q, k, v, left, lo_row, o, lse, do, halo)
    u_keep, u_send, w_keep, w_send, one_small, qkv_bias = tail(
        places, late_chunks(), dq, dk, dv, back, o, x_all, g_all, normed_one, u_two, wt, vec, cos_t, sin_t, halo
    )
    late_own = late_scatter(w_keep, w_send)
    both = scatter_rows(u_keep, u_send)
    normed_own = hidden_in.astype(f32)
    normed_own = normed_own - jnp.mean(normed_own, axis=-1, keepdims=True)
    inv_own = lax.rsqrt(jnp.mean(normed_own * normed_own, axis=-1, keepdims=True) + norm_eps)
    normed_own = normed_own * inv_own
    input_grad = cotangent.astype(f32) + inv_own * (
        both
        - jnp.mean(both, axis=-1, keepdims=True)
        - normed_own * jnp.mean(both * normed_own, axis=-1, keepdims=True)
    )

    width = x_all.shape[1]
    dp_rank = lax.axis_index("dp")
    two_rows = summed_over(ff_small[:2], "tensor")
    early = summed_over(jnp.concatenate([two_rows, ff_small[2:4]], axis=0), "dp")
    one_rows = summed_over(one_small[:2], "tensor")
    qkv_rows = jnp.pad(qkv_bias[:, 0], (0, -qkv_dim % width)).reshape(-1, width)
    last = summed_over(jnp.concatenate([one_rows, qkv_rows], axis=0), "dp")
    own_early = lax.dynamic_slice_in_dim(early[:3], dp_rank * own_dims, own_dims, 1)
    own_late = lax.dynamic_slice_in_dim(last[:2], dp_rank * own_dims, own_dims, 1)
    qkv_b_total = last[2:].reshape(-1)[:qkv_dim].reshape(3, local_dim)
    return (
        layer_out,
        input_grad.astype(bf16),
        jnp.transpose(late_own[:, :qkv_dim].reshape(own_dims, 3, local_dim), (1, 0, 2)),
        qkv_b_total,
        late_own[:, qkv_dim:].T,
        own_early[2],
        ff_own[:, :ff],
        early[3],
        ff_own[:, ff:].T,
        own_early[2],
        own_late[0],
        own_late[1],
        own_early[0],
        own_early[1],
    )


def solution(mesh):
    in_specs = (
        P(("dp", "tensor"), None),
        P(None, "dp", "tensor"),
        P(None, "tensor"),
        P("tensor", "dp"),
        P("dp"),
        P("dp", "tensor"),
        P("tensor"),
        P("tensor", "dp"),
        P("dp"),
        P("dp"),
        P("dp"),
        P("dp"),
        P("dp"),
        P("dp"),
        P("dp"),
        P(("dp", "tensor"), None),
    )
    out_specs = (
        P(("dp", "tensor"), None),
        P(("dp", "tensor"), None),
        P(None, "dp", "tensor"),
        P(None, "tensor"),
        P("tensor", "dp"),
        P("dp"),
        P("dp", "tensor"),
        P("tensor"),
        P("tensor", "dp"),
        P("dp"),
        P("dp"),
        P("dp"),
        P("dp"),
        P("dp"),
    )
    return jax.shard_map(body, mesh=mesh, in_specs=in_specs, out_specs=out_specs, check_vma=False)
```

```python
import functools

import jax
import jax.numpy as jnp
from jax import lax
from jax.experimental import pallas as pl
from jax.experimental.pallas import tpu as pltpu
from jax.sharding import PartitionSpec as P

HEAD_DIM = 64
ROT = 16
BLK = 256
SLOTS = (0, 2, 1, 3)

norm_eps = 1e-05
big_negative = -1e30
rope_base = 10000.0
inv_sqrt_two = 0.7071067811865476
inv_sqrt_two_pi = 0.3989422804014327

f32 = jnp.float32
bf16 = jnp.bfloat16


def mm(a, b, ca, cb):
    return lax.dot_general(a, b, (((ca,), (cb,)), ((), ())), preferred_element_type=f32)


def params(**kw):
    return pltpu.CompilerParams(vmem_limit_bytes=56 * 1024 * 1024, **kw)


def cost(flops, moved, exps=0):
    return pl.CostEstimate(flops=int(flops), bytes_accessed=int(moved), transcendentals=int(exps))


def shaped(shape, dtype):
    return jax.ShapeDtypeStruct(shape, dtype)


def passed_along(block, axis, distance):
    devices = range(lax.axis_size(axis))
    route = [(i - distance, i) for i in devices if i - distance in devices]
    return lax.ppermute(block, axis, route)


def swapped(block, axis, bit):
    route = [(i, i ^ bit) for i in range(lax.axis_size(axis))]
    return lax.ppermute(block, axis, route)


def ring_order(n):
    return list(range(0, n, 2)) + list(range(n - 1, 0, -2))


def ring_gather(block, axis):
    n = lax.axis_size(axis)
    rows = block.shape[0]
    if n > 8:
        return [lax.all_gather(block, axis, axis=0, tiled=True)], jnp.zeros((1,), jnp.int32)
    ring = ring_order(n)
    ahead = [(ring[r], ring[(r + 1) % n]) for r in range(n)]
    behind = [(b, a) for a, b in ahead]
    table = []
    for device in range(n):
        at = ring.index(device)
        row = [device * rows]
        for step in range(1, n // 2):
            row.append(ring[(at - step) % n] * rows)
            row.append(ring[(at + step) % n] * rows)
        row.append(ring[(at + n // 2) % n] * rows)
        row.append(ring[(at + n // 2) % n] * rows + rows // 2)
        table.append(row)
    pieces = [block]
    from_left = from_right = block
    for step in range(1, n // 2):
        from_left = lax.ppermute(from_left, axis, ahead)
        from_right = lax.ppermute(from_right, axis, behind)
        pieces += [from_left, from_right]
    pieces.append(lax.ppermute(from_left[: rows // 2], axis, ahead))
    pieces.append(lax.ppermute(from_right[rows // 2 :], axis, behind))
    return pieces, jnp.asarray(table, jnp.int32)[lax.axis_index(axis)]


def gather_rows(block):
    far = swapped(block, "tensor", 2)
    near = swapped(block, "tensor", 1)
    both = swapped(far, "tensor", 1)
    return jnp.concatenate([block, far, near, both], axis=0)


def scatter_near(keep, send):
    count = keep.shape[0] // 2
    came = swapped(send, "tensor", 1)
    other = (keep[count:].astype(f32) + came[count:].astype(f32)).astype(bf16)
    return keep[:count], came[:count], other


def scatter_far(own, came, other):
    return own.astype(f32) + came.astype(f32) + swapped(other, "tensor", 2).astype(f32)


def tied(*arrays):
    return lax.optimization_barrier(arrays)


def summed_over(vec, axis):
    n = lax.axis_size(axis)
    bit = 1
    while bit < n:
        vec = vec + swapped(vec, axis, bit)
        bit *= 2
    return vec


def assemble(piece_refs, start_ref, first, out_ref):
    columns = pl.ds(first, out_ref.shape[1])
    for n, ref in enumerate(piece_refs):
        rows = ref.shape[0]
        out_ref[pl.ds(pl.multiple_of(start_ref[n], rows), rows), :] = ref[:, columns]


def norm_rows(x):
    center = x - jnp.mean(x, axis=-1, keepdims=True)
    inv_std = lax.rsqrt(jnp.mean(center * center, axis=-1, keepdims=True) + norm_eps)
    return center * inv_std


def ff_kernel(pieces, start_ref, x_ref, g_ref, b_ref, vec_ref, *refs):
    w_refs = refs[:pieces]
    out_ref, u_ref, grads_ref, small_ref = refs[pieces : pieces + 4]
    fc_w, fc2_w, fc_acc, fc2_acc = refs[pieces + 4 :]
    step = pl.program_id(0)
    ff = fc2_w.shape[1]

    @pl.when(step == 0)
    def _():
        assemble(w_refs, start_ref, 0, fc_w)
        assemble(w_refs, start_ref, ff, fc2_w)
        fc_acc[...] = jnp.zeros_like(fc_acc)
        fc2_acc[...] = jnp.zeros_like(fc2_acc)
        small_ref[...] = jnp.zeros_like(small_ref)

    gain, shift = vec_ref[4:5, :], vec_ref[5:6, :]
    normed = norm_rows(x_ref[...].astype(f32))
    normed_two = (normed * gain + shift).astype(bf16)
    pre = mm(normed_two, fc_w[...], 1, 0) + b_ref[...]
    cdf = 0.5 + 0.5 * lax.erf(pre * inv_sqrt_two)
    act = (pre * cdf).astype(bf16)
    slope = cdf + pre * (jnp.exp(-0.5 * pre * pre) * inv_sqrt_two_pi)
    out_ref[...] = mm(act, fc2_w[...], 1, 1).astype(bf16)
    g = g_ref[...]
    pre_grad = (mm(g, fc2_w[...], 1, 0) * slope).astype(bf16)
    two_grad = mm(pre_grad, fc_w[...], 1, 1)
    u_ref[...] = (two_grad * gain).astype(bf16)
    fc_acc[...] += mm(normed_two, pre_grad, 0, 0)
    fc2_acc[...] += mm(g, act, 0, 0)
    small_ref[0:1, :] += jnp.sum(two_grad * normed, axis=0, keepdims=True)
    small_ref[1:2, :] += jnp.sum(two_grad, axis=0, keepdims=True)
    small_ref[2:3, :] += jnp.sum(g.astype(f32), axis=0, keepdims=True)
    small_ref[3:4, :] += jnp.sum(pre_grad.astype(f32), axis=0, keepdims=True)

    @pl.when(step == pl.num_programs(0) - 1)
    def _():
        grads_ref[:, :ff] = fc_acc[...].astype(bf16)
        grads_ref[:, ff:] = fc2_acc[...].astype(bf16)


def feed_forward(starts, x, g, b_fc, vec, pieces, ff):
    tokens, dim = x.shape
    rows = tokens // 4
    spec = pl.BlockSpec((rows, dim), lambda s, *_: (s, 0))
    whole = lambda shape: pl.BlockSpec(shape, lambda s, *_: (0, 0))
    return pl.pallas_call(
        functools.partial(ff_kernel, len(pieces)),
        grid_spec=pltpu.PrefetchScalarGridSpec(
            num_scalar_prefetch=1,
            grid=(4,),
            in_specs=[spec, spec, whole((1, ff)), whole(vec.shape)] + [whole(p.shape) for p in pieces],
            out_specs=[spec, spec, whole((dim, 2 * ff)), whole((8, dim))],
            scratch_shapes=[pltpu.VMEM((dim, ff), bf16)] * 2 + [pltpu.VMEM((dim, ff), f32)] * 2,
        ),
        out_shape=[
            shaped((tokens, dim), bf16),
            shaped((tokens, dim), bf16),
            shaped((dim, 2 * ff), bf16),
            shaped((8, dim), f32),
        ],
        compiler_params=params(),
        cost_estimate=cost(12 * tokens * dim * ff, 8 * tokens * dim + 8 * dim * ff, 2 * tokens * ff),
        name="feed_forward",
    )(starts, x, g, b_fc, vec, *pieces)


def turned(x, cos_t, sin_t):
    half = ROT // 2
    out = []
    for h in range(x.shape[0] // HEAD_DIM):
        a = x[h * HEAD_DIM : h * HEAD_DIM + half]
        b = x[h * HEAD_DIM + half : h * HEAD_DIM + ROT]
        out += [a * cos_t - b * sin_t, b * cos_t + a * sin_t, x[h * HEAD_DIM + ROT : (h + 1) * HEAD_DIM]]
    return jnp.concatenate(out, axis=0)


def project_kernel(pieces, first, start_ref, place_ref, x_ref, g_ref, b_ref, cos_ref, sin_ref, *refs):
    w_refs = refs[:pieces]
    q_ref, k_ref, v_ref, do_ref, wt_ref, vec_ref, packed = refs[pieces:]
    feat = q_ref.shape[0]
    width = wt_ref.shape[0]

    @pl.when(pl.program_id(0) == 0)
    def _():
        assemble(w_refs, start_ref, first, packed)
        wt_ref[...] = packed[:, :width].astype(f32).T.astype(bf16)
        vec_ref[...] = packed[:, width:].astype(f32).T[:8]

    normed = norm_rows(x_ref[...].astype(f32))
    normed_one = (normed * vec_ref[2:3, :] + vec_ref[3:4, :]).astype(bf16)
    proj = mm(wt_ref[: 3 * feat, :], normed_one, 1, 1) + b_ref[...]
    cos_t, sin_t = cos_ref[...], sin_ref[...]
    q_ref[...] = (turned(proj[:feat], cos_t, sin_t) * HEAD_DIM ** (-0.5)).astype(bf16)
    k_ref[...] = turned(proj[feat : 2 * feat], cos_t, sin_t).astype(bf16)
    v_ref[...] = proj[2 * feat :].astype(bf16)
    do_ref[...] = mm(wt_ref[3 * feat :, :], g_ref[...], 1, 1).astype(bf16)


def project(starts, places, x, g, b_col, cos_t, sin_t, pieces, first, feat):
    tokens, dim = x.shape
    rows = tokens // 4
    width = 4 * feat
    spec = pl.BlockSpec((rows, dim), lambda s, *_: (s, 0))
    placed = lambda r: pl.BlockSpec((r, rows), lambda s, start, place: (0, place[s]))
    whole = lambda shape: pl.BlockSpec(shape, lambda s, *_: (0, 0))
    return pl.pallas_call(
        functools.partial(project_kernel, len(pieces), first),
        grid_spec=pltpu.PrefetchScalarGridSpec(
            num_scalar_prefetch=2,
            grid=(4,),
            in_specs=[spec, spec, whole(b_col.shape), placed(ROT // 2), placed(ROT // 2)]
            + [whole(p.shape) for p in pieces],
            out_specs=[placed(feat)] * 4 + [whole((width, dim)), whole((8, dim))],
            scratch_shapes=[pltpu.VMEM((dim, width + 128), bf16)],
        ),
        out_shape=[shaped((feat, tokens), bf16)] * 4 + [shaped((width, dim), bf16), shaped((8, dim), f32)],
        compiler_params=params(),
        cost_estimate=cost(8 * tokens * dim * feat, 6 * tokens * dim + 4 * dim * width),
        name="project",
    )(starts, places, x, g, b_col, cos_t, sin_t, *pieces)


def key_mask(chunk, lo_row, hi_row):
    idx = chunk * BLK + lax.broadcasted_iota(jnp.int32, (BLK, BLK), 0)
    return jnp.where((idx >= lo_row) & (idx <= hi_row), 0.0, big_negative)


def attn_fwd_kernel(heads, halo, first_ref, q_ref, k_ref, v_ref, left_ref, lo_ref, o_ref, lse_ref, keys, values):
    i = pl.program_id(0)
    first = first_ref[i]
    last = i + halo // BLK
    feat = k_ref.shape[0]

    @pl.when(i == 0)
    def _():
        keys[:, :halo] = left_ref[:feat, :]
        keys[:, halo:] = k_ref[...]
        values[:, :halo] = left_ref[feat:, :]
        values[:, halo:] = v_ref[...]

    lo_row = lo_ref[...]
    hi_row = halo + i * BLK + lax.broadcasted_iota(jnp.int32, (1, BLK), 1)

    def step(c, carry):
        cols = pl.ds(pl.multiple_of(c * BLK, BLK), BLK)
        mask = key_mask(c, lo_row, hi_row)
        hs = range(heads)
        feats = [pl.ds(h * HEAD_DIM, HEAD_DIM) for h in hs]
        s = [mm(keys[feats[h], cols], q_ref[feats[h], :], 0, 0) + mask for h in hs]
        tops = [jnp.maximum(carry[h][0], jnp.max(s[h], axis=0, keepdims=True)) for h in hs]
        p = [jnp.exp(s[h] - tops[h]) for h in hs]
        pv = [mm(values[feats[h], cols], p[h].astype(bf16), 1, 0) for h in hs]
        kept = [jnp.exp(carry[h][0] - tops[h]) for h in hs]
        return tuple(
            (
                tops[h],
                carry[h][1] * kept[h] + jnp.sum(p[h], axis=0, keepdims=True),
                carry[h][2] * kept[h] + pv[h],
            )
            for h in hs
        )

    start = tuple(
        (
            jnp.full((1, BLK), big_negative, f32),
            jnp.zeros((1, BLK), f32),
            jnp.zeros((HEAD_DIM, BLK), f32),
        )
        for _ in range(heads)
    )
    done = lax.fori_loop(first, last + 1, step, start)
    for h in range(heads):
        top, total, acc = done[h]
        o_ref[pl.ds(h * HEAD_DIM, HEAD_DIM), :] = (acc / total).astype(bf16)
        lse_ref[pl.ds(h, 1), :] = top + jnp.log(total)


def attention_forward(first, q, k, v, left, lo, halo):
    feat, tokens = q.shape
    heads = feat // HEAD_DIM
    col = lambda i, *_: (0, i)
    whole = lambda shape: pl.BlockSpec(shape, lambda i, *_: (0, 0))
    q_spec = pl.BlockSpec((feat, BLK), col)
    return pl.pallas_call(
        functools.partial(attn_fwd_kernel, heads, halo),
        grid_spec=pltpu.PrefetchScalarGridSpec(
            num_scalar_prefetch=1,
            grid=(tokens // BLK,),
            in_specs=[q_spec, whole(k.shape), whole(v.shape), whole(left.shape), pl.BlockSpec((1, BLK), col)],
            out_specs=[q_spec, pl.BlockSpec((8, BLK), col)],
            scratch_shapes=[pltpu.VMEM((feat, halo + tokens), bf16)] * 2,
        ),
        out_shape=[shaped((feat, tokens), bf16), shaped((8, tokens), f32)],
        compiler_params=params(),
        cost_estimate=cost(16 * feat * tokens * 1024, 8 * feat * tokens, heads * tokens * 1024),
        name="attention_forward",
    )(first, q, k, v, left, lo)


def attn_bwd_step(heads, c, base, q_ref, k_ref, v_ref, do_ref, lse_ref, lo_row, hi_row, deltas, dq_ref, dk_ref, dv_ref):
    cols = pl.ds(pl.multiple_of((c - base) * BLK, BLK), BLK)
    mask = key_mask(c, lo_row, hi_row)
    hs = range(heads)
    feats = [pl.ds(h * HEAD_DIM, HEAD_DIM) for h in hs]
    s = [mm(k_ref[feats[h], cols], q_ref[feats[h], :], 0, 0) + mask for h in hs]
    dp = [mm(v_ref[feats[h], cols], do_ref[feats[h], :], 0, 0) for h in hs]
    p = [jnp.exp(s[h] - lse_ref[pl.ds(h, 1), :]) for h in hs]
    ds = [(p[h] * (dp[h] - deltas[h])).astype(bf16) for h in hs]
    dv = [mm(do_ref[feats[h], :], p[h].astype(bf16), 1, 1) for h in hs]
    dk = [mm(q_ref[feats[h], :], ds[h], 1, 1) for h in hs]
    dq = [mm(k_ref[feats[h], cols], ds[h], 1, 0) for h in hs]
    for h in hs:
        dv_ref[feats[h], cols] += dv[h]
        dk_ref[feats[h], cols] += dk[h]
        dq_ref[feats[h], :] += dq[h]


def row_deltas(heads, o_ref, do_ref):
    deltas = []
    for h in range(heads):
        feats = pl.ds(h * HEAD_DIM, HEAD_DIM)
        prod = do_ref[feats, :].astype(f32) * o_ref[feats, :].astype(f32)
        deltas.append(jnp.sum(prod, axis=0, keepdims=True))
    return deltas


def halo_bwd_kernel(heads, halo, first_ref, q_ref, left_ref, lo_ref, o_ref, lse_ref, do_ref, dq_ref, back_ref, dk, dv):
    i = pl.program_id(0)
    feat = q_ref.shape[0]

    @pl.when(i == 0)
    def _():
        dk[...] = jnp.zeros_like(dk)
        dv[...] = jnp.zeros_like(dv)

    lo_row = lo_ref[...]
    hi_row = jnp.full((1, BLK), halo, jnp.int32)
    dq_ref[...] = jnp.zeros_like(dq_ref)
    deltas = row_deltas(heads, o_ref, do_ref)
    k_ref, v_ref = left_ref.at[:feat, :], left_ref.at[feat:, :]

    def step(c, carry):
        attn_bwd_step(
            heads, c, 0, q_ref, k_ref, v_ref, do_ref, lse_ref, lo_row, hi_row, deltas, dq_ref, dk, dv
        )
        return carry

    lax.fori_loop(first_ref[i], halo // BLK, step, 0)

    @pl.when(i == pl.num_programs(0) - 1)
    def _():
        back_ref[:feat, :] = dk[...].astype(bf16)
        back_ref[feat:, :] = dv[...].astype(bf16)


def own_bwd_kernel(
    heads, halo, first_ref, q_ref, k_ref, v_ref, lo_ref, o_ref, lse_ref, do_ref, part_ref, dq_ref, dk_ref, dv_ref
):
    i = pl.program_id(0)
    base = halo // BLK

    @pl.when(i == 0)
    def _():
        dk_ref[...] = jnp.zeros_like(dk_ref)
        dv_ref[...] = jnp.zeros_like(dv_ref)

    @pl.when(i < base)
    def _():
        dq_ref[...] = part_ref[...]

    @pl.when(i >= base)
    def _():
        dq_ref[...] = jnp.zeros_like(dq_ref)

    lo_row = lo_ref[...]
    hi_row = halo + i * BLK + lax.broadcasted_iota(jnp.int32, (1, BLK), 1)
    deltas = row_deltas(heads, o_ref, do_ref)

    def step(c, carry):
        attn_bwd_step(
            heads, c, base, q_ref, k_ref, v_ref, do_ref, lse_ref, lo_row, hi_row, deltas, dq_ref, dk_ref, dv_ref
        )
        return carry

    lax.fori_loop(jnp.maximum(first_ref[i], base), i + base + 1, step, 0)
    dq_ref[...] = dq_ref[...] * HEAD_DIM ** (-0.5)


def backward_left(first, q, left, lo, o, lse, do, halo):
    feat, tokens = q.shape
    heads = feat // HEAD_DIM
    col = lambda i, *_: (0, i)
    whole = lambda shape: pl.BlockSpec(shape, lambda i, *_: (0, 0))
    q_spec = pl.BlockSpec((feat, BLK), col)
    return pl.pallas_call(
        functools.partial(halo_bwd_kernel, heads, halo),
        grid_spec=pltpu.PrefetchScalarGridSpec(
            num_scalar_prefetch=1,
            grid=(halo // BLK,),
            in_specs=[
                q_spec,
                whole(left.shape),
                pl.BlockSpec((1, BLK), col),
                q_spec,
                pl.BlockSpec((8, BLK), col),
                q_spec,
            ],
            out_specs=[q_spec, whole(left.shape)],
            scratch_shapes=[pltpu.VMEM((feat, halo), f32)] * 2,
        ),
        out_shape=[shaped((feat, halo), f32), shaped(left.shape, bf16)],
        compiler_params=params(),
        cost_estimate=cost(40 * feat * halo * 512, 20 * feat * halo, heads * halo * 512),
        name="attention_backward_left",
    )(first, q, left, lo, o, lse, do)


def backward_own(first, q, k, v, lo, o, lse, do, dq_part, halo):
    feat, tokens = q.shape
    heads = feat // HEAD_DIM
    col = lambda i, *_: (0, i)
    whole = lambda shape: pl.BlockSpec(shape, lambda i, *_: (0, 0))
    q_spec = pl.BlockSpec((feat, BLK), col)
    part_spec = pl.BlockSpec((feat, BLK), lambda i, *_: (0, jnp.minimum(i, halo // BLK - 1)))
    return pl.pallas_call(
        functools.partial(own_bwd_kernel, heads, halo),
        grid_spec=pltpu.PrefetchScalarGridSpec(
            num_scalar_prefetch=1,
            grid=(tokens // BLK,),
            in_specs=[
                q_spec,
                whole(k.shape),
                whole(v.shape),
                pl.BlockSpec((1, BLK), col),
                q_spec,
                pl.BlockSpec((8, BLK), col),
                q_spec,
                part_spec,
            ],
            out_specs=[q_spec, whole(k.shape), whole(v.shape)],
        ),
        out_shape=[shaped((feat, tokens), f32)] * 3,
        compiler_params=params(),
        cost_estimate=cost(40 * feat * tokens * 1024, 20 * feat * tokens, heads * tokens * 1024),
        name="attention_backward_own",
    )(first, q, k, v, lo, o, lse, do, dq_part)


def keep_send_specs(rows, dim):
    keep = pl.BlockSpec((rows, dim), lambda s, *_: (jnp.minimum(s, 1), 0))
    send = pl.BlockSpec((rows, dim), lambda s, *_: (jnp.maximum(s - 2, 0), 0))
    return keep, send


def put_rows(keep_ref, send_ref, value):
    s = pl.program_id(0)

    @pl.when(s < 2)
    def _():
        keep_ref[...] = value

    @pl.when(s >= 2)
    def _():
        send_ref[...] = value


def put_chunks(chunk_ref, keep_ref, send_ref, value):
    parts = chunk_ref.shape[0] // 2
    size = keep_ref.shape[0] // parts
    for half, ref in enumerate((keep_ref, send_ref)):
        for n in range(parts):
            at = pl.ds(pl.multiple_of(chunk_ref[half * parts + n] * size, size), size)
            ref[n * size : (n + 1) * size, :] = value[at, :].astype(bf16)


def out_kernel(place_ref, chunk_ref, o_ref, ff_ref, g_ref, w_ref, keep_ref, send_ref, wkeep_ref, wsend_ref, acc, acc_t):
    s = pl.program_id(0)

    @pl.when(s == 0)
    def _():
        acc[...] = jnp.zeros_like(acc)

    total = mm(o_ref[...], w_ref[...], 0, 0) + ff_ref[...].astype(f32)
    put_rows(keep_ref, send_ref, total.astype(bf16))
    acc[...] += mm(o_ref[...], g_ref[...], 1, 0)

    @pl.when(s == pl.num_programs(0) - 1)
    def _():
        acc_t[...] = acc[...].T
        put_chunks(chunk_ref, wkeep_ref, wsend_ref, acc_t)


def branch_out(places, chunks, o, ff_out, g, out_w):
    feat, tokens = o.shape
    dim = out_w.shape[1]
    rows = tokens // 4
    keep, send = keep_send_specs(rows, dim)
    spec = pl.BlockSpec((rows, dim), lambda s, *_: (s, 0))
    whole = lambda shape: pl.BlockSpec(shape, lambda s, *_: (0, 0))
    return pl.pallas_call(
        out_kernel,
        grid_spec=pltpu.PrefetchScalarGridSpec(
            num_scalar_prefetch=2,
            grid=(4,),
            in_specs=[
                pl.BlockSpec((feat, rows), lambda s, place, chunk: (0, place[s])),
                spec,
                spec,
                whole((feat, dim)),
            ],
            out_specs=[keep, send, whole((dim // 2, feat)), whole((dim // 2, feat))],
            scratch_shapes=[pltpu.VMEM((feat, dim), f32), pltpu.VMEM((dim, feat), f32)],
        ),
        out_shape=[shaped((tokens // 2, dim), bf16)] * 2 + [shaped((dim // 2, feat), bf16)] * 2,
        compiler_params=params(),
        cost_estimate=cost(4 * feat * tokens * dim, 6 * tokens * dim),
        name="branch_out",
    )(places, chunks, o, ff_out, g, out_w)


def input_grad_kernel(
    halo,
    place_ref,
    dq_ref,
    dk_ref,
    dv_ref,
    back_ref,
    x_ref,
    u2_ref,
    wt_ref,
    vec_ref,
    cos_ref,
    sin_ref,
    keep_ref,
    send_ref,
    grad_ref,
    small_ref,
    bias_ref,
    late,
):
    s = pl.program_id(0)
    feat, rows = dq_ref.shape
    tokens = late.shape[1]

    @pl.when(s == 0)
    def _():
        late[:, : tokens - halo] = jnp.zeros((2 * feat, tokens - halo), bf16)
        late[:, tokens - halo :] = back_ref[...]
        small_ref[...] = jnp.zeros_like(small_ref)
        bias_ref[...] = jnp.zeros_like(bias_ref)

    cols = pl.ds(pl.multiple_of(place_ref[s] * rows, rows), rows)
    cos_t, sin_t = cos_ref[...], -sin_ref[...]
    dq = turned(dq_ref[...], cos_t, sin_t)
    dk = turned(dk_ref[...] + late[:feat, cols].astype(f32), cos_t, sin_t)
    dv = dv_ref[...] + late[feat:, cols].astype(f32)
    grad = jnp.concatenate([dq, dk, dv], axis=0).astype(bf16)
    grad_ref[...] = grad
    bias_ref[...] += jnp.sum(grad.astype(f32), axis=1, keepdims=True)
    one_grad = mm(grad, wt_ref[: 3 * feat, :], 0, 0)
    put_rows(keep_ref, send_ref, (one_grad * vec_ref[2:3, :] + u2_ref[...].astype(f32)).astype(bf16))
    normed = norm_rows(x_ref[...].astype(f32))
    small_ref[0:1, :] += jnp.sum(one_grad * normed, axis=0, keepdims=True)
    small_ref[1:2, :] += jnp.sum(one_grad, axis=0, keepdims=True)


def input_gradient(places, dq, dk, dv, back, x, u2, wt, vec, cos_t, sin_t, halo):
    feat, tokens = dq.shape
    dim = x.shape[1]
    rows = tokens // 4
    spec = pl.BlockSpec((rows, dim), lambda s, *_: (s, 0))
    placed = lambda r: pl.BlockSpec((r, rows), lambda s, place: (0, place[s]))
    whole = lambda shape: pl.BlockSpec(shape, lambda s, *_: (0, 0))
    keep, send = keep_send_specs(rows, dim)
    return pl.pallas_call(
        functools.partial(input_grad_kernel, halo),
        grid_spec=pltpu.PrefetchScalarGridSpec(
            num_scalar_prefetch=1,
            grid=(4,),
            in_specs=[placed(feat)] * 3
            + [whole(back.shape), spec, spec, whole(wt.shape), whole(vec.shape)]
            + [placed(ROT // 2)] * 2,
            out_specs=[keep, send, placed(3 * feat), whole((8, dim)), whole((3 * feat, 1))],
            scratch_shapes=[pltpu.VMEM((2 * feat, tokens), bf16)],
        ),
        out_shape=[shaped((tokens // 2, dim), bf16)] * 2
        + [shaped((3 * feat, tokens), bf16), shaped((8, dim), f32), shaped((3 * feat, 1), f32)],
        compiler_params=params(),
        cost_estimate=cost(12 * feat * tokens * dim, 10 * tokens * dim),
        name="input_gradient",
    )(places, dq, dk, dv, back, x, u2, wt, vec, cos_t, sin_t)


def weight_grad_kernel(place_ref, chunk_ref, grad_ref, x_ref, vec_ref, wkeep_ref, wsend_ref, acc, acc_t):
    s = pl.program_id(0)

    @pl.when(s == 0)
    def _():
        acc[...] = jnp.zeros_like(acc)

    normed = norm_rows(x_ref[...].astype(f32))
    normed_one = (normed * vec_ref[2:3, :] + vec_ref[3:4, :]).astype(bf16)
    acc[...] += mm(grad_ref[...], normed_one, 1, 0)

    @pl.when(s == pl.num_programs(0) - 1)
    def _():
        acc_t[...] = acc[...].T
        put_chunks(chunk_ref, wkeep_ref, wsend_ref, acc_t)


def weight_gradient(places, chunks, grad, x, vec):
    width, tokens = grad.shape
    dim = x.shape[1]
    rows = tokens // 4
    whole = lambda shape: pl.BlockSpec(shape, lambda s, *_: (0, 0))
    return pl.pallas_call(
        weight_grad_kernel,
        grid_spec=pltpu.PrefetchScalarGridSpec(
            num_scalar_prefetch=2,
            grid=(4,),
            in_specs=[
                pl.BlockSpec((width, rows), lambda s, place, chunk: (0, place[s])),
                pl.BlockSpec((rows, dim), lambda s, *_: (s, 0)),
                whole(vec.shape),
            ],
            out_specs=[whole((dim // 2, width))] * 2,
            scratch_shapes=[pltpu.VMEM((width, dim), f32), pltpu.VMEM((dim, width), f32)],
        ),
        out_shape=[shaped((dim // 2, width), bf16)] * 2,
        compiler_params=params(),
        cost_estimate=cost(4 * width * tokens * dim, 4 * tokens * dim),
        name="weight_gradient",
    )(places, chunks, grad, x, vec)


def rope_tables(positions):
    freq_idx = jnp.arange(0, ROT, 2, dtype=f32)
    inverse = rope_base ** (-freq_idx / ROT)
    angles = inverse[:, None] * positions.astype(f32)[None, :]
    return jnp.cos(angles), jnp.sin(angles)


def late_chunks():
    n = lax.axis_size("dp")
    rank = lax.axis_index("dp")
    if n > 8:
        return jnp.arange(2, dtype=jnp.int32)
    mine = jnp.stack([rank ^ (2 * k) for k in range(n // 2)])
    return jnp.concatenate([mine, mine ^ 1]).astype(jnp.int32)


def late_near(keep, send):
    n = lax.axis_size("dp")
    if n > 8:
        whole = jnp.concatenate([keep, send], axis=0)
        return lax.psum_scatter(whole, "dp", scatter_dimension=0, tiled=True).astype(f32)
    return keep.astype(f32) + swapped(send, "dp", 1).astype(f32)


def late_far(total, dtype):
    n = lax.axis_size("dp")
    if n > 8:
        return total
    size = total.shape[0] * 2 // n
    low = total.astype(dtype)
    own = total[:size]
    for k in range(1, n // 2):
        own = own + swapped(low[k * size : (k + 1) * size], "dp", 2 * k).astype(f32)
    return own


def body(
    hidden_in,
    w_qkv,
    b_qkv,
    w_out,
    b_out,
    w_fc,
    b_fc,
    w_fc2,
    b_fc2,
    ln1_gain,
    ln1_bias,
    ln2_gain,
    ln2_bias,
    segment_ids,
    positions,
    cotangent,
):
    local_dim = w_qkv.shape[2]
    ff = w_fc.shape[1]
    own_dims = w_fc.shape[0]
    seq_len = positions.shape[0]
    halo = seq_len * 3 // 8
    qkv_dim = 3 * local_dim
    rank = lax.axis_index("tensor")
    places = jnp.stack([rank ^ at for at in SLOTS]).astype(jnp.int32)

    vectors = jnp.stack([b_out, b_fc2, ln1_gain, ln1_bias, ln2_gain, ln2_bias], axis=1)
    vectors = jnp.pad(vectors, ((0, 0), (0, 122)))
    block = jnp.concatenate(
        [
            w_fc,
            w_fc2.T,
            jnp.transpose(w_qkv, (1, 0, 2)).reshape(own_dims, qkv_dim),
            w_out.T,
            vectors,
        ],
        axis=1,
    )
    pieces, starts = ring_gather(block, "dp")
    x_all = gather_rows(hidden_in)
    g_all = gather_rows(cotangent)

    cos_t, sin_t = rope_tables(positions)
    lo = halo + jnp.arange(seq_len, dtype=jnp.int32) - positions
    first = lo[::BLK] // BLK
    lo_row = lo.reshape(1, seq_len)

    q, k, v, do, wt, vec = project(
        starts, places, x_all, g_all, b_qkv.astype(f32).reshape(qkv_dim, 1), cos_t, sin_t, pieces, 2 * ff, local_dim
    )
    left = passed_along(jnp.concatenate([k[:, -halo:], v[:, -halo:]], axis=0), "dp", 1)
    ff_out, u_two, ff_grads, ff_small = feed_forward(
        starts, x_all, g_all, b_fc.astype(f32).reshape(1, ff), vec, pieces, ff
    )
    ff_own = lax.psum_scatter(ff_grads, "dp", scatter_dimension=0, tiled=True).astype(f32)
    q, ff_out = tied(q, ff_out)

    o, lse = attention_forward(first, q, k, v, left, lo_row, halo)
    chunks = late_chunks()
    out_keep, out_send, ow_keep, ow_send = branch_out(places, chunks, o, ff_out, g_all, wt[qkv_dim:])
    own_o, came_o, other_o = scatter_near(out_keep, out_send)
    ow_near = late_near(ow_keep, ow_send)
    do, out_keep = tied(do, out_keep)
    dq_part, back = backward_left(first, q, left, lo_row, o, lse, do, halo)
    dq_part, back, other_o, ow_near = tied(dq_part, back, other_o, ow_near)
    far_o = swapped(other_o, "tensor", 2)
    back = passed_along(back, "dp", -1)
    ow_own = late_far(ow_near, bf16)
    dq, dk, dv = backward_own(first, q, k, v, lo_row, o, lse, do, dq_part, halo)
    back, dq, far_o, ow_own = tied(back, dq, far_o, ow_own)
    summed = own_o.astype(f32) + came_o.astype(f32) + far_o.astype(f32)
    layer_out = (hidden_in.astype(f32) + summed + vec[0] + vec[1]).astype(bf16)

    u_keep, u_send, proj_grad, one_small, qkv_bias = input_gradient(
        places, dq, dk, dv, back, x_all, u_two, wt, vec, cos_t, sin_t, halo
    )
    own_u, came_u, other_u = scatter_near(u_keep, u_send)
    w_keep, w_send = weight_gradient(places, chunks, proj_grad, x_all, vec)

    n = lax.axis_size("dp")
    dims = x_all.shape[1]
    mine = jnp.concatenate([one_small[:2], ff_small[:3]], axis=0).reshape(5, n, own_dims)
    mine = jnp.pad(jnp.transpose(mine, (1, 0, 2)), ((0, 0), (0, 0), (0, 128 - own_dims)))
    fc_rows = ff_small[3].reshape(-1, 128)
    qkv_rows = jnp.pad(qkv_bias[:, 0], (0, -qkv_dim % 128)).reshape(-1, 128)
    shared = jnp.concatenate([fc_rows, qkv_rows], axis=0)
    small = jnp.concatenate([mine, jnp.broadcast_to(shared, (n,) + shared.shape)], axis=1)
    w_send, small, _ = tied(w_send, small, other_u)
    w_near = late_near(w_keep, w_send)
    if n > 8:
        small_near = lax.psum_scatter(small, "dp", scatter_dimension=0, tiled=True)
    else:
        small = jnp.take(small, chunks, axis=0)
        small_near = late_near(small[: n // 2], small[n // 2 :])
    w_near, small_near = tied(w_near, small_near)
    both = scatter_far(own_u, came_u, other_u)
    small_own = late_far(small_near, f32)[0]
    late_own = late_far(w_near, bf16)
    late_own, ff_own = tied(late_own, ff_own)
    norm_grads = summed_over(small_own[:4], "tensor")[:, :own_dims]
    fc_count = fc_rows.shape[0]
    fc_b_total = small_own[5 : 5 + fc_count].reshape(-1)
    qkv_b_total = small_own[5 + fc_count :].reshape(-1)[:qkv_dim].reshape(3, local_dim)
    out_b_total = small_own[4, :own_dims]

    normed_own = hidden_in.astype(f32)
    normed_own = normed_own - jnp.mean(normed_own, axis=-1, keepdims=True)
    inv_own = lax.rsqrt(jnp.mean(normed_own * normed_own, axis=-1, keepdims=True) + norm_eps)
    normed_own = normed_own * inv_own
    input_grad = cotangent.astype(f32) + inv_own * (
        both
        - jnp.mean(both, axis=-1, keepdims=True)
        - normed_own * jnp.mean(both * normed_own, axis=-1, keepdims=True)
    )
    return (
        layer_out,
        input_grad.astype(bf16),
        jnp.transpose(late_own.reshape(own_dims, 3, local_dim), (1, 0, 2)),
        qkv_b_total,
        ow_own.T,
        out_b_total,
        ff_own[:, :ff],
        fc_b_total,
        ff_own[:, ff:].T,
        out_b_total,
        norm_grads[0],
        norm_grads[1],
        norm_grads[2],
        norm_grads[3],
    )


def solution(mesh):
    in_specs = (
        P(("dp", "tensor"), None),
        P(None, "dp", "tensor"),
        P(None, "tensor"),
        P("tensor", "dp"),
        P("dp"),
        P("dp", "tensor"),
        P("tensor"),
        P("tensor", "dp"),
        P("dp"),
        P("dp"),
        P("dp"),
        P("dp"),
        P("dp"),
        P("dp"),
        P("dp"),
        P(("dp", "tensor"), None),
    )
    out_specs = (
        P(("dp", "tensor"), None),
        P(("dp", "tensor"), None),
        P(None, "dp", "tensor"),
        P(None, "tensor"),
        P("tensor", "dp"),
        P("dp"),
        P("dp", "tensor"),
        P("tensor"),
        P("tensor", "dp"),
        P("dp"),
        P("dp"),
        P("dp"),
        P("dp"),
        P("dp"),
    )
    return jax.shard_map(body, mesh=mesh, in_specs=in_specs, out_specs=out_specs, check_vma=False)
```

```python
import functools

import jax
import jax.numpy as jnp
from jax import lax
from jax.experimental import pallas as pl
from jax.experimental.pallas import tpu as pltpu
from jax.sharding import PartitionSpec as P

HEAD_DIM = 64
ROT = 16
BLK = 256
SLOTS = (0, 2, 1, 3)

norm_eps = 1e-05
big_negative = -1e30
rope_base = 10000.0
inv_sqrt_two = 0.7071067811865476
inv_sqrt_two_pi = 0.3989422804014327

f32 = jnp.float32
bf16 = jnp.bfloat16


def mm(a, b, ca, cb):
    return lax.dot_general(a, b, (((ca,), (cb,)), ((), ())), preferred_element_type=f32)


def params(**kw):
    return pltpu.CompilerParams(vmem_limit_bytes=56 * 1024 * 1024, **kw)


def cost(flops, moved, exps=0):
    return pl.CostEstimate(flops=int(flops), bytes_accessed=int(moved), transcendentals=int(exps))


def shaped(shape, dtype):
    return jax.ShapeDtypeStruct(shape, dtype)


def passed_along(block, axis, distance):
    devices = range(lax.axis_size(axis))
    route = [(i - distance, i) for i in devices if i - distance in devices]
    return lax.ppermute(block, axis, route)


def swapped(block, axis, bit):
    route = [(i, i ^ bit) for i in range(lax.axis_size(axis))]
    return lax.ppermute(block, axis, route)


def ring_order(n):
    return list(range(0, n, 2)) + list(range(n - 1, 0, -2))


def ring_gather(block, axis, early, late):
    n = lax.axis_size(axis)
    rows = block.shape[0]
    if n > 8:
        return [lax.all_gather(block, axis, axis=0, tiled=True)], jnp.zeros((1,), jnp.int32), early, late
    ring = ring_order(n)
    ahead = [(ring[r], ring[(r + 1) % n]) for r in range(n)]
    behind = [(b, a) for a, b in ahead]
    table = []
    for device in range(n):
        at = ring.index(device)
        row = [device * rows]
        for step in range(1, n // 2):
            row.append(ring[(at - step) % n] * rows)
            row.append(ring[(at + step) % n] * rows)
        row.append(ring[(at + n // 2) % n] * rows)
        row.append(ring[(at + n // 2) % n] * rows + rows // 2)
        table.append(row)
    pieces = [block]
    from_left = from_right = block
    for step in range(1, n // 2):
        from_left = lax.ppermute(from_left, axis, ahead)
        from_right = lax.ppermute(from_right, axis, behind)
        if step == n // 2 - 1:
            from_left, from_right, early = tied(from_left, from_right, early)
        else:
            from_left, from_right = tied(from_left, from_right)
        pieces += [from_left, from_right]
    from_left = lax.ppermute(from_left[: rows // 2], axis, ahead)
    from_right = lax.ppermute(from_right[rows // 2 :], axis, behind)
    from_left, from_right, late = tied(from_left, from_right, late)
    pieces += [from_left, from_right]
    return pieces, jnp.asarray(table, jnp.int32)[lax.axis_index(axis)], early, late


def gather_rows(block, near, far):
    return jnp.concatenate([block, far, near, swapped(far, "tensor", 1)], axis=0)


def scatter_near(keep, send):
    count = keep.shape[0] // 2
    came = swapped(send, "tensor", 1)
    other = (keep[count:].astype(f32) + came[count:].astype(f32)).astype(bf16)
    return keep[:count], came[:count], other


def tied(*arrays):
    return lax.optimization_barrier(arrays)


def summed_over(vec, axis):
    n = lax.axis_size(axis)
    bit = 1
    while bit < n:
        vec = vec + swapped(vec, axis, bit)
        bit *= 2
    return vec


def assemble(piece_refs, start_ref, first, out_ref):
    columns = pl.ds(first, out_ref.shape[1])
    for n, ref in enumerate(piece_refs):
        rows = ref.shape[0]
        out_ref[pl.ds(pl.multiple_of(start_ref[n], rows), rows), :] = ref[:, columns]


def row_stats(x):
    mean = jnp.mean(x, axis=-1, keepdims=True)
    center = x - mean
    return mean, lax.rsqrt(jnp.mean(center * center, axis=-1, keepdims=True) + norm_eps)


def normed_from(x_ref, stats_ref):
    return (x_ref[...].astype(f32) - stats_ref[:, 0:1]) * stats_ref[:, 1:2]


def ff_kernel(pieces, start_ref, x_ref, g_ref, stats_ref, b_ref, vec_ref, fc2_w, *refs):
    w_refs = refs[:pieces]
    out_ref, u_ref, grads_ref, small_ref = refs[pieces : pieces + 4]
    fc_w, fc_acc, fc2_acc = refs[pieces + 4 :]
    step = pl.program_id(0)
    ff = fc2_w.shape[1]

    @pl.when(step == 0)
    def _():
        assemble(w_refs, start_ref, 0, fc_w)
        fc_acc[...] = jnp.zeros_like(fc_acc)
        fc2_acc[...] = jnp.zeros_like(fc2_acc)
        small_ref[...] = jnp.zeros_like(small_ref)

    gain, shift = vec_ref[4:5, :], vec_ref[5:6, :]
    normed = normed_from(x_ref, stats_ref)
    normed_two = (normed * gain + shift).astype(bf16)
    pre = mm(normed_two, fc_w[...], 1, 0) + b_ref[...]
    cdf = 0.5 + 0.5 * lax.erf(pre * inv_sqrt_two)
    act = (pre * cdf).astype(bf16)
    slope = cdf + pre * (jnp.exp(-0.5 * pre * pre) * inv_sqrt_two_pi)
    out_ref[...] = mm(act, fc2_w[...], 1, 1).astype(bf16)
    g = g_ref[...]
    pre_grad = (mm(g, fc2_w[...], 1, 0) * slope).astype(bf16)
    two_grad = mm(pre_grad, fc_w[...], 1, 1)
    u_ref[...] = (two_grad * gain).astype(bf16)
    fc_acc[...] += mm(normed_two, pre_grad, 0, 0)
    fc2_acc[...] += mm(g, act, 0, 0)
    small_ref[0:1, :] += jnp.sum(two_grad * normed, axis=0, keepdims=True)
    small_ref[1:2, :] += jnp.sum(two_grad, axis=0, keepdims=True)
    small_ref[2:3, :] += jnp.sum(g.astype(f32), axis=0, keepdims=True)
    small_ref[3:4, :] += jnp.sum(pre_grad.astype(f32), axis=0, keepdims=True)

    @pl.when(step == pl.num_programs(0) - 1)
    def _():
        grads_ref[:, :ff] = fc_acc[...].astype(bf16)
        grads_ref[:, ff:] = fc2_acc[...].astype(bf16)


def feed_forward(starts, x, g, stats, b_fc, vec, fc2_w, pieces, ff):
    tokens, dim = x.shape
    rows = tokens // 4
    spec = pl.BlockSpec((rows, dim), lambda s, *_: (s, 0))
    whole = lambda shape: pl.BlockSpec(shape, lambda s, *_: (0, 0))
    return pl.pallas_call(
        functools.partial(ff_kernel, len(pieces)),
        grid_spec=pltpu.PrefetchScalarGridSpec(
            num_scalar_prefetch=1,
            grid=(4,),
            in_specs=[
                spec,
                spec,
                pl.BlockSpec((rows, 128), lambda s, *_: (s, 0)),
                whole((1, ff)),
                whole(vec.shape),
                whole(fc2_w.shape),
            ]
            + [whole(p.shape) for p in pieces],
            out_specs=[spec, spec, whole((dim, 2 * ff)), whole((8, dim))],
            scratch_shapes=[pltpu.VMEM((dim, ff), bf16)] + [pltpu.VMEM((dim, ff), f32)] * 2,
        ),
        out_shape=[
            shaped((tokens, dim), bf16),
            shaped((tokens, dim), bf16),
            shaped((dim, 2 * ff), bf16),
            shaped((8, dim), f32),
        ],
        compiler_params=params(),
        cost_estimate=cost(12 * tokens * dim * ff, 8 * tokens * dim + 8 * dim * ff, 2 * tokens * ff),
        name="feed_forward",
    )(starts, x, g, stats, b_fc, vec, fc2_w, *pieces)


def turned(x, cos_t, sin_t):
    half = ROT // 2
    out = []
    for h in range(x.shape[0] // HEAD_DIM):
        a = x[h * HEAD_DIM : h * HEAD_DIM + half]
        b = x[h * HEAD_DIM + half : h * HEAD_DIM + ROT]
        out += [a * cos_t - b * sin_t, b * cos_t + a * sin_t, x[h * HEAD_DIM + ROT : (h + 1) * HEAD_DIM]]
    return jnp.concatenate(out, axis=0)


def project_kernel(pieces, first, start_ref, place_ref, x_ref, b_ref, cos_ref, sin_ref, *refs):
    w_refs = refs[:pieces]
    q_ref, k_ref, v_ref, halo_ref, normed_ref, stats_ref, wt_ref, vec_ref, packed = refs[pieces:]
    feat = q_ref.shape[0]
    width = wt_ref.shape[0]

    @pl.when(pl.program_id(0) == 0)
    def _():
        assemble(w_refs, start_ref, first, packed)
        wt_ref[...] = packed[:, :width].astype(f32).T.astype(bf16)
        vec_ref[...] = packed[:, width:].astype(f32).T[:8]

    x = x_ref[...].astype(f32)
    mean, inv_std = row_stats(x)
    lane = lax.broadcasted_iota(jnp.int32, stats_ref.shape, 1)
    stats_ref[...] = jnp.where(lane == 0, mean, inv_std)
    normed_one = ((x - mean) * inv_std * vec_ref[2:3, :] + vec_ref[3:4, :]).astype(bf16)
    normed_ref[...] = normed_one
    proj = mm(wt_ref[: 3 * feat, :], normed_one, 1, 1) + b_ref[...]
    cos_t, sin_t = cos_ref[...], sin_ref[...]
    q_ref[...] = (turned(proj[:feat], cos_t, sin_t) * HEAD_DIM ** (-0.5)).astype(bf16)
    k_ref[...] = turned(proj[feat : 2 * feat], cos_t, sin_t).astype(bf16)
    v_ref[...] = proj[2 * feat :].astype(bf16)
    rows = k_ref.shape[1]
    halo = halo_ref.shape[1]
    place = place_ref[pl.program_id(0)]
    for n in range(4):
        begin = max(0, 4 * rows - halo - n * rows)
        if begin < rows:
            to = n * rows + begin - (4 * rows - halo)

            @pl.when(place == n)
            def _():
                halo_ref[:feat, to : to + rows - begin] = k_ref[:, begin:]
                halo_ref[feat:, to : to + rows - begin] = v_ref[:, begin:]


def project(starts, places, x, b_col, cos_t, sin_t, pieces, first, feat, halo):
    tokens, dim = x.shape
    rows = tokens // 4
    width = 4 * feat
    spec = pl.BlockSpec((rows, dim), lambda s, *_: (s, 0))
    placed = lambda r: pl.BlockSpec((r, rows), lambda s, start, place: (0, place[s]))
    whole = lambda shape: pl.BlockSpec(shape, lambda s, *_: (0, 0))
    return pl.pallas_call(
        functools.partial(project_kernel, len(pieces), first),
        grid_spec=pltpu.PrefetchScalarGridSpec(
            num_scalar_prefetch=2,
            grid=(4,),
            in_specs=[spec, whole(b_col.shape), placed(ROT // 2), placed(ROT // 2)]
            + [whole(p.shape) for p in pieces],
            out_specs=[placed(feat)] * 3
            + [
                whole((2 * feat, halo)),
                spec,
                pl.BlockSpec((rows, 128), lambda s, *_: (s, 0)),
                whole((width, dim)),
                whole((8, dim)),
            ],
            scratch_shapes=[pltpu.VMEM((dim, width + 128), bf16)],
        ),
        out_shape=[shaped((feat, tokens), bf16)] * 3
        + [
            shaped((2 * feat, halo), bf16),
            shaped((tokens, dim), bf16),
            shaped((tokens, 128), f32),
            shaped((width, dim), bf16),
            shaped((8, dim), f32),
        ],
        compiler_params=params(),
        cost_estimate=cost(6 * tokens * dim * feat, 6 * tokens * dim + 4 * dim * width),
        name="project",
    )(starts, places, x, b_col, cos_t, sin_t, *pieces)


def key_mask(chunk, lo_row, hi_row):
    idx = chunk * BLK + lax.broadcasted_iota(jnp.int32, (BLK, BLK), 0)
    return jnp.where((idx >= lo_row) & (idx <= hi_row), 0.0, big_negative)


def attn_fwd_kernel(heads, halo, first_ref, q_ref, k_ref, v_ref, left_ref, lo_ref, o_ref, lse_ref, keys, values):
    i = pl.program_id(0)
    first = first_ref[i]
    last = i + halo // BLK
    feat = k_ref.shape[0]

    @pl.when(i == 0)
    def _():
        keys[:, :halo] = left_ref[:feat, :]
        keys[:, halo:] = k_ref[...]
        values[:, :halo] = left_ref[feat:, :]
        values[:, halo:] = v_ref[...]

    lo_row = lo_ref[...]
    hi_row = halo + i * BLK + lax.broadcasted_iota(jnp.int32, (1, BLK), 1)

    def step(c, carry):
        cols = pl.ds(pl.multiple_of(c * BLK, BLK), BLK)
        mask = key_mask(c, lo_row, hi_row)
        hs = range(heads)
        feats = [pl.ds(h * HEAD_DIM, HEAD_DIM) for h in hs]
        s = [mm(keys[feats[h], cols], q_ref[feats[h], :], 0, 0) + mask for h in hs]
        tops = [jnp.maximum(carry[h][0], jnp.max(s[h], axis=0, keepdims=True)) for h in hs]
        p = [jnp.exp(s[h] - tops[h]) for h in hs]
        pv = [mm(values[feats[h], cols], p[h].astype(bf16), 1, 0) for h in hs]
        kept = [jnp.exp(carry[h][0] - tops[h]) for h in hs]
        return tuple(
            (
                tops[h],
                carry[h][1] * kept[h] + jnp.sum(p[h], axis=0, keepdims=True),
                carry[h][2] * kept[h] + pv[h],
            )
            for h in hs
        )

    start = tuple(
        (
            jnp.full((1, BLK), big_negative, f32),
            jnp.zeros((1, BLK), f32),
            jnp.zeros((HEAD_DIM, BLK), f32),
        )
        for _ in range(heads)
    )
    done = lax.fori_loop(first, last + 1, step, start)
    for h in range(heads):
        top, total, acc = done[h]
        o_ref[pl.ds(h * HEAD_DIM, HEAD_DIM), :] = (acc / total).astype(bf16)
        lse_ref[pl.ds(h, 1), :] = top + jnp.log(total)


def attention_forward(first, q, k, v, left, lo, halo):
    feat, tokens = q.shape
    heads = feat // HEAD_DIM
    col = lambda i, *_: (0, i)
    whole = lambda shape: pl.BlockSpec(shape, lambda i, *_: (0, 0))
    q_spec = pl.BlockSpec((feat, BLK), col)
    return pl.pallas_call(
        functools.partial(attn_fwd_kernel, heads, halo),
        grid_spec=pltpu.PrefetchScalarGridSpec(
            num_scalar_prefetch=1,
            grid=(tokens // BLK,),
            in_specs=[q_spec, whole(k.shape), whole(v.shape), whole(left.shape), pl.BlockSpec((1, BLK), col)],
            out_specs=[q_spec, pl.BlockSpec((8, BLK), col)],
            scratch_shapes=[pltpu.VMEM((feat, halo + tokens), bf16)] * 2,
        ),
        out_shape=[shaped((feat, tokens), bf16), shaped((8, tokens), f32)],
        compiler_params=params(),
        cost_estimate=cost(16 * feat * tokens * 1024, 8 * feat * tokens, heads * tokens * 1024),
        name="attention_forward",
    )(first, q, k, v, left, lo)


def attn_bwd_step(heads, c, base, q_ref, k_ref, v_ref, do_ref, lse_ref, lo_row, hi_row, deltas, dq_ref, dk_ref, dv_ref):
    cols = pl.ds(pl.multiple_of((c - base) * BLK, BLK), BLK)
    mask = key_mask(c, lo_row, hi_row)
    hs = range(heads)
    feats = [pl.ds(h * HEAD_DIM, HEAD_DIM) for h in hs]
    s = [mm(k_ref[feats[h], cols], q_ref[feats[h], :], 0, 0) + mask for h in hs]
    dp = [mm(v_ref[feats[h], cols], do_ref[feats[h], :], 0, 0) for h in hs]
    p = [jnp.exp(s[h] - lse_ref[pl.ds(h, 1), :]) for h in hs]
    ds = [(p[h] * (dp[h] - deltas[h])).astype(bf16) for h in hs]
    dv = [mm(do_ref[feats[h], :], p[h].astype(bf16), 1, 1) for h in hs]
    dk = [mm(q_ref[feats[h], :], ds[h], 1, 1) for h in hs]
    dq = [mm(k_ref[feats[h], cols], ds[h], 1, 0) for h in hs]
    for h in hs:
        dv_ref[feats[h], cols] += dv[h]
        dk_ref[feats[h], cols] += dk[h]
        dq_ref[feats[h], :] += dq[h]


def row_deltas(heads, o_ref, do_ref):
    deltas = []
    for h in range(heads):
        feats = pl.ds(h * HEAD_DIM, HEAD_DIM)
        prod = do_ref[feats, :].astype(f32) * o_ref[feats, :].astype(f32)
        deltas.append(jnp.sum(prod, axis=0, keepdims=True))
    return deltas


def halo_bwd_kernel(heads, halo, first_ref, q_ref, left_ref, lo_ref, o_ref, lse_ref, do_ref, dq_ref, back_ref, dk, dv):
    i = pl.program_id(0)
    feat = q_ref.shape[0]

    @pl.when(i == 0)
    def _():
        dk[...] = jnp.zeros_like(dk)
        dv[...] = jnp.zeros_like(dv)

    lo_row = lo_ref[...]
    hi_row = jnp.full((1, BLK), halo, jnp.int32)
    dq_ref[...] = jnp.zeros_like(dq_ref)
    deltas = row_deltas(heads, o_ref, do_ref)
    k_ref, v_ref = left_ref.at[:feat, :], left_ref.at[feat:, :]

    def step(c, carry):
        attn_bwd_step(
            heads, c, 0, q_ref, k_ref, v_ref, do_ref, lse_ref, lo_row, hi_row, deltas, dq_ref, dk, dv
        )
        return carry

    lax.fori_loop(first_ref[i], halo // BLK, step, 0)

    @pl.when(i == pl.num_programs(0) - 1)
    def _():
        back_ref[:feat, :] = dk[...].astype(bf16)
        back_ref[feat:, :] = dv[...].astype(bf16)


def own_bwd_kernel(
    heads, halo, first_ref, q_ref, k_ref, v_ref, lo_ref, o_ref, lse_ref, do_ref, part_ref, dq_ref, dk_ref, dv_ref
):
    i = pl.program_id(0)
    base = halo // BLK

    @pl.when(i == 0)
    def _():
        dk_ref[...] = jnp.zeros_like(dk_ref)
        dv_ref[...] = jnp.zeros_like(dv_ref)

    @pl.when(i < base)
    def _():
        dq_ref[...] = part_ref[...]

    @pl.when(i >= base)
    def _():
        dq_ref[...] = jnp.zeros_like(dq_ref)

    lo_row = lo_ref[...]
    hi_row = halo + i * BLK + lax.broadcasted_iota(jnp.int32, (1, BLK), 1)
    deltas = row_deltas(heads, o_ref, do_ref)

    def step(c, carry):
        attn_bwd_step(
            heads, c, base, q_ref, k_ref, v_ref, do_ref, lse_ref, lo_row, hi_row, deltas, dq_ref, dk_ref, dv_ref
        )
        return carry

    lax.fori_loop(jnp.maximum(first_ref[i], base), i + base + 1, step, 0)
    dq_ref[...] = dq_ref[...] * HEAD_DIM ** (-0.5)


def backward_left(first, q, left, lo, o, lse, do, halo):
    feat, tokens = q.shape
    heads = feat // HEAD_DIM
    col = lambda i, *_: (0, i)
    whole = lambda shape: pl.BlockSpec(shape, lambda i, *_: (0, 0))
    q_spec = pl.BlockSpec((feat, BLK), col)
    return pl.pallas_call(
        functools.partial(halo_bwd_kernel, heads, halo),
        grid_spec=pltpu.PrefetchScalarGridSpec(
            num_scalar_prefetch=1,
            grid=(halo // BLK,),
            in_specs=[
                q_spec,
                whole(left.shape),
                pl.BlockSpec((1, BLK), col),
                q_spec,
                pl.BlockSpec((8, BLK), col),
                q_spec,
            ],
            out_specs=[q_spec, whole(left.shape)],
            scratch_shapes=[pltpu.VMEM((feat, halo), f32)] * 2,
        ),
        out_shape=[shaped((feat, halo), f32), shaped(left.shape, bf16)],
        compiler_params=params(),
        cost_estimate=cost(40 * feat * halo * 512, 20 * feat * halo, heads * halo * 512),
        name="attention_backward_left",
    )(first, q, left, lo, o, lse, do)


def backward_own(first, q, k, v, lo, o, lse, do, dq_part, halo):
    feat, tokens = q.shape
    heads = feat // HEAD_DIM
    col = lambda i, *_: (0, i)
    whole = lambda shape: pl.BlockSpec(shape, lambda i, *_: (0, 0))
    q_spec = pl.BlockSpec((feat, BLK), col)
    part_spec = pl.BlockSpec((feat, BLK), lambda i, *_: (0, jnp.minimum(i, halo // BLK - 1)))
    return pl.pallas_call(
        functools.partial(own_bwd_kernel, heads, halo),
        grid_spec=pltpu.PrefetchScalarGridSpec(
            num_scalar_prefetch=1,
            grid=(tokens // BLK,),
            in_specs=[
                q_spec,
                whole(k.shape),
                whole(v.shape),
                pl.BlockSpec((1, BLK), col),
                q_spec,
                pl.BlockSpec((8, BLK), col),
                q_spec,
                part_spec,
            ],
            out_specs=[q_spec, whole(k.shape), whole(v.shape)],
        ),
        out_shape=[shaped((feat, tokens), f32)] * 3,
        compiler_params=params(),
        cost_estimate=cost(40 * feat * tokens * 1024, 20 * feat * tokens, heads * tokens * 1024),
        name="attention_backward_own",
    )(first, q, k, v, lo, o, lse, do, dq_part)


def keep_send_specs(rows, dim):
    keep = pl.BlockSpec((rows, dim), lambda s, *_: (jnp.minimum(s, 1), 0))
    send = pl.BlockSpec((rows, dim), lambda s, *_: (jnp.maximum(s - 2, 0), 0))
    return keep, send


def put_rows(keep_ref, send_ref, value):
    s = pl.program_id(0)

    @pl.when(s < 2)
    def _():
        keep_ref[...] = value

    @pl.when(s >= 2)
    def _():
        send_ref[...] = value


def put_chunks(chunk_ref, keep_ref, send_ref, value):
    parts = chunk_ref.shape[0] // 2
    size = keep_ref.shape[0] // parts
    for half, ref in enumerate((keep_ref, send_ref)):
        for n in range(parts):
            at = pl.ds(pl.multiple_of(chunk_ref[half * parts + n] * size, size), size)
            ref[n * size : (n + 1) * size, :] = value[at, :].astype(bf16)


def out_kernel(
    place_ref, chunk_ref, o_ref, ff_ref, g_ref, w_ref, keep_ref, send_ref, wkeep_ref, wsend_ref, do_ref, acc, acc_t
):
    s = pl.program_id(0)

    @pl.when(s == 0)
    def _():
        acc[...] = jnp.zeros_like(acc)

    total = mm(o_ref[...], w_ref[...], 0, 0) + ff_ref[...].astype(f32)
    put_rows(keep_ref, send_ref, total.astype(bf16))
    acc[...] += mm(o_ref[...], g_ref[...], 1, 0)
    do_ref[...] = mm(w_ref[...], g_ref[...], 1, 1).astype(bf16)

    @pl.when(s == pl.num_programs(0) - 1)
    def _():
        acc_t[...] = acc[...].T
        put_chunks(chunk_ref, wkeep_ref, wsend_ref, acc_t)


def branch_out(places, chunks, o, ff_out, g, wt):
    feat, tokens = o.shape
    dim = wt.shape[1]
    rows = tokens // 4
    keep, send = keep_send_specs(rows, dim)
    spec = pl.BlockSpec((rows, dim), lambda s, *_: (s, 0))
    placed = pl.BlockSpec((feat, rows), lambda s, place, chunk: (0, place[s]))
    whole = lambda shape: pl.BlockSpec(shape, lambda s, *_: (0, 0))
    return pl.pallas_call(
        out_kernel,
        grid_spec=pltpu.PrefetchScalarGridSpec(
            num_scalar_prefetch=2,
            grid=(4,),
            in_specs=[placed, spec, spec, pl.BlockSpec((feat, dim), lambda s, *_: (3, 0))],
            out_specs=[keep, send, whole((dim // 2, feat)), whole((dim // 2, feat)), placed],
            scratch_shapes=[pltpu.VMEM((feat, dim), f32), pltpu.VMEM((dim, feat), f32)],
        ),
        out_shape=[shaped((tokens // 2, dim), bf16)] * 2
        + [shaped((dim // 2, feat), bf16)] * 2
        + [shaped((feat, tokens), bf16)],
        compiler_params=params(),
        cost_estimate=cost(4 * feat * tokens * dim, 6 * tokens * dim),
        name="branch_out",
    )(places, chunks, o, ff_out, g, wt)


def input_grad_kernel(
    halo,
    place_ref,
    dq_ref,
    dk_ref,
    dv_ref,
    back_ref,
    x_ref,
    stats_ref,
    u2_ref,
    wt_ref,
    vec_ref,
    cos_ref,
    sin_ref,
    keep_ref,
    send_ref,
    grad_ref,
    small_ref,
    bias_ref,
    late,
):
    s = pl.program_id(0)
    feat, rows = dq_ref.shape
    tokens = late.shape[1]

    @pl.when(s == 0)
    def _():
        late[:, : tokens - halo] = jnp.zeros((2 * feat, tokens - halo), bf16)
        late[:, tokens - halo :] = back_ref[...]
        small_ref[...] = jnp.zeros_like(small_ref)
        bias_ref[...] = jnp.zeros_like(bias_ref)

    cols = pl.ds(pl.multiple_of(place_ref[s] * rows, rows), rows)
    cos_t, sin_t = cos_ref[...], -sin_ref[...]
    dq = turned(dq_ref[...], cos_t, sin_t)
    dk = turned(dk_ref[...] + late[:feat, cols].astype(f32), cos_t, sin_t)
    dv = dv_ref[...] + late[feat:, cols].astype(f32)
    grad = jnp.concatenate([dq, dk, dv], axis=0).astype(bf16)
    grad_ref[...] = grad
    bias_ref[...] += jnp.sum(grad.astype(f32), axis=1, keepdims=True)
    one_grad = mm(grad, wt_ref[: 3 * feat, :], 0, 0)
    put_rows(keep_ref, send_ref, (one_grad * vec_ref[2:3, :] + u2_ref[...].astype(f32)).astype(bf16))
    normed = normed_from(x_ref, stats_ref)
    small_ref[0:1, :] += jnp.sum(one_grad * normed, axis=0, keepdims=True)
    small_ref[1:2, :] += jnp.sum(one_grad, axis=0, keepdims=True)


def input_gradient(places, dq, dk, dv, back, x, stats, u2, wt, vec, cos_t, sin_t, halo):
    feat, tokens = dq.shape
    dim = x.shape[1]
    rows = tokens // 4
    spec = pl.BlockSpec((rows, dim), lambda s, *_: (s, 0))
    placed = lambda r: pl.BlockSpec((r, rows), lambda s, place: (0, place[s]))
    whole = lambda shape: pl.BlockSpec(shape, lambda s, *_: (0, 0))
    keep, send = keep_send_specs(rows, dim)
    return pl.pallas_call(
        functools.partial(input_grad_kernel, halo),
        grid_spec=pltpu.PrefetchScalarGridSpec(
            num_scalar_prefetch=1,
            grid=(4,),
            in_specs=[placed(feat)] * 3
            + [whole(back.shape), spec, pl.BlockSpec((rows, 128), lambda s, *_: (s, 0)), spec, whole(wt.shape)]
            + [whole(vec.shape)]
            + [placed(ROT // 2)] * 2,
            out_specs=[keep, send, placed(3 * feat), whole((8, dim)), whole((3 * feat, 1))],
            scratch_shapes=[pltpu.VMEM((2 * feat, tokens), bf16)],
        ),
        out_shape=[shaped((tokens // 2, dim), bf16)] * 2
        + [shaped((3 * feat, tokens), bf16), shaped((8, dim), f32), shaped((3 * feat, 1), f32)],
        compiler_params=params(),
        cost_estimate=cost(12 * feat * tokens * dim, 10 * tokens * dim),
        name="input_gradient",
    )(places, dq, dk, dv, back, x, stats, u2, wt, vec, cos_t, sin_t)


def weight_grad_kernel(place_ref, chunk_ref, grad_ref, normed_ref, wkeep_ref, wsend_ref, acc, acc_t):
    s = pl.program_id(0)

    @pl.when(s == 0)
    def _():
        acc[...] = jnp.zeros_like(acc)

    acc[...] += mm(grad_ref[...], normed_ref[...], 1, 0)

    @pl.when(s == pl.num_programs(0) - 1)
    def _():
        acc_t[...] = acc[...].T
        put_chunks(chunk_ref, wkeep_ref, wsend_ref, acc_t)


def weight_gradient(places, chunks, grad, normed, part, parts):
    width, tokens = grad.shape
    width = width // parts
    dim = normed.shape[1]
    rows = tokens // 4
    whole = lambda shape: pl.BlockSpec(shape, lambda s, *_: (0, 0))
    return pl.pallas_call(
        weight_grad_kernel,
        grid_spec=pltpu.PrefetchScalarGridSpec(
            num_scalar_prefetch=2,
            grid=(4,),
            in_specs=[
                pl.BlockSpec((width, rows), lambda s, place, chunk: (part, place[s])),
                pl.BlockSpec((rows, dim), lambda s, *_: (s, 0)),
            ],
            out_specs=[whole((dim // 2, width))] * 2,
            scratch_shapes=[pltpu.VMEM((width, dim), f32), pltpu.VMEM((dim, width), f32)],
        ),
        out_shape=[shaped((dim // 2, width), bf16)] * 2,
        compiler_params=params(),
        cost_estimate=cost(4 * width * tokens * dim, 4 * tokens * dim),
        name="weight_gradient",
    )(places, chunks, grad, normed)


def norm_back_kernel(own_ref, came_ref, far_ref, x_ref, stats_ref, g_ref, out_ref):
    both = own_ref[...].astype(f32) + came_ref[...].astype(f32) + far_ref[...].astype(f32)
    normed = normed_from(x_ref, stats_ref)
    inv_std = stats_ref[:, 1:2]
    grad = both - jnp.mean(both, axis=-1, keepdims=True)
    grad = grad - normed * jnp.mean(both * normed, axis=-1, keepdims=True)
    out_ref[...] = (g_ref[...].astype(f32) + inv_std * grad).astype(bf16)


def norm_back(own, came, far, x, stats, g):
    count, dim = x.shape
    rows = count // 2
    spec = pl.BlockSpec((rows, dim), lambda s: (s, 0))
    return pl.pallas_call(
        norm_back_kernel,
        grid=(2,),
        in_specs=[spec] * 4 + [pl.BlockSpec((rows, 128), lambda s: (s, 0)), spec],
        out_specs=spec,
        out_shape=shaped((count, dim), bf16),
        compiler_params=params(),
        cost_estimate=cost(20 * count * dim, 12 * count * dim),
        name="norm_back",
    )(own, came, far, x, stats, g)


def rope_tables(positions):
    freq_idx = jnp.arange(0, ROT, 2, dtype=f32)
    inverse = rope_base ** (-freq_idx / ROT)
    angles = inverse[:, None] * positions.astype(f32)[None, :]
    return jnp.cos(angles), jnp.sin(angles)


def late_chunks():
    n = lax.axis_size("dp")
    rank = lax.axis_index("dp")
    if n > 8:
        return jnp.arange(2, dtype=jnp.int32)
    mine = jnp.stack([rank ^ (2 * k) for k in range(n // 2)])
    return jnp.concatenate([mine, mine ^ 1]).astype(jnp.int32)


def late_sent(keep, send):
    n = lax.axis_size("dp")
    if n > 8:
        whole = jnp.concatenate([keep, send], axis=0)
        return None, lax.psum_scatter(whole, "dp", scatter_dimension=0, tiled=True).astype(f32)
    return keep, swapped(send, "dp", 1)


def late_sum(keep, came):
    return came if keep is None else keep.astype(f32) + came.astype(f32)


def late_near(keep, send):
    return late_sum(*late_sent(keep, send))


def late_far(total, dtype):
    n = lax.axis_size("dp")
    if n > 8:
        return total
    size = total.shape[0] * 2 // n
    low = total.astype(dtype)
    own = total[:size]
    for k in range(1, n // 2):
        own = own + swapped(low[k * size : (k + 1) * size], "dp", 2 * k).astype(f32)
    return own


def body(
    hidden_in,
    w_qkv,
    b_qkv,
    w_out,
    b_out,
    w_fc,
    b_fc,
    w_fc2,
    b_fc2,
    ln1_gain,
    ln1_bias,
    ln2_gain,
    ln2_bias,
    segment_ids,
    positions,
    cotangent,
):
    local_dim = w_qkv.shape[2]
    ff = w_fc.shape[1]
    own_dims = w_fc.shape[0]
    seq_len = positions.shape[0]
    halo = seq_len * 3 // 8
    qkv_dim = 3 * local_dim
    rank = lax.axis_index("tensor")
    places = jnp.stack([rank ^ at for at in SLOTS]).astype(jnp.int32)

    vectors = jnp.stack([b_out, b_fc2, ln1_gain, ln1_bias, ln2_gain, ln2_bias], axis=1)
    vectors = jnp.pad(vectors, ((0, 0), (0, 122)))
    block = jnp.concatenate(
        [
            w_fc,
            jnp.transpose(w_qkv, (1, 0, 2)).reshape(own_dims, qkv_dim),
            w_out.T,
            vectors,
        ],
        axis=1,
    )
    x_far, g_far = swapped(hidden_in, "tensor", 2), swapped(cotangent, "tensor", 2)
    x_near, g_near = swapped(hidden_in, "tensor", 1), swapped(cotangent, "tensor", 1)
    pieces, starts, x_far, g_far = ring_gather(block, "dp", x_far, g_far)
    fc2_w = lax.all_gather(w_fc2.T, "dp", axis=0, tiled=True)
    x_all = gather_rows(hidden_in, x_near, x_far)
    g_all = gather_rows(cotangent, g_near, g_far)

    cos_t, sin_t = rope_tables(positions)
    lo = halo + jnp.arange(seq_len, dtype=jnp.int32) - positions
    first = lo[::BLK] // BLK
    lo_row = lo.reshape(1, seq_len)

    q, k, v, right, normed_one, stats, wt, vec = project(
        starts,
        places,
        x_all,
        b_qkv.astype(f32).reshape(qkv_dim, 1),
        cos_t,
        sin_t,
        pieces,
        ff,
        local_dim,
        halo,
    )
    left = passed_along(right, "dp", 1)
    ff_out, u_two, ff_grads, ff_small = feed_forward(
        starts, x_all, g_all, stats, b_fc.astype(f32).reshape(1, ff), vec, fc2_w, pieces, ff
    )
    ff_own = lax.psum_scatter(ff_grads, "dp", scatter_dimension=0, tiled=True).astype(f32)
    q, ff_out = tied(q, ff_out)

    o, lse = attention_forward(first, q, k, v, left, lo_row, halo)
    chunks = late_chunks()
    out_keep, out_send, ow_keep, ow_send, do = branch_out(places, chunks, o, ff_out, g_all, wt)
    own_o, came_o, other_o = scatter_near(out_keep, out_send)
    ow_near = late_near(ow_keep, ow_send)
    dq_part, back = backward_left(first, q, left, lo_row, o, lse, do, halo)
    dq_part, back, other_o, ow_near = tied(dq_part, back, other_o, ow_near)
    far_o = swapped(other_o, "tensor", 2)
    back = passed_along(back, "dp", -1)
    ow_own = late_far(ow_near, bf16)
    dq, dk, dv = backward_own(first, q, k, v, lo_row, o, lse, do, dq_part, halo)
    back, dq, far_o, ow_own = tied(back, dq, far_o, ow_own)
    summed = own_o.astype(f32) + came_o.astype(f32) + far_o.astype(f32)
    layer_out = (hidden_in.astype(f32) + summed + vec[0] + vec[1]).astype(bf16)

    u_keep, u_send, proj_grad, one_small, qkv_bias = input_gradient(
        places, dq, dk, dv, back, x_all, stats, u_two, wt, vec, cos_t, sin_t, halo
    )
    own_u, came_u, other_u = scatter_near(u_keep, u_send)
    keep_a, send_a = weight_gradient(places, chunks, proj_grad, normed_one, 0, 2)
    proj_grad, other_u, send_a = tied(proj_grad, other_u, send_a)
    keep_a, came_a = late_sent(keep_a, send_a)
    keep_b, send_b = weight_gradient(places, chunks, proj_grad, normed_one, 1, 2)

    n = lax.axis_size("dp")
    dims = x_all.shape[1]
    mine = jnp.concatenate([one_small[:2], ff_small[:3]], axis=0).reshape(5, n, own_dims)
    mine = jnp.pad(jnp.transpose(mine, (1, 0, 2)), ((0, 0), (0, 0), (0, 128 - own_dims)))
    fc_rows = ff_small[3].reshape(-1, 128)
    qkv_rows = jnp.pad(qkv_bias[:, 0], (0, -qkv_dim % 128)).reshape(-1, 128)
    shared = jnp.concatenate([fc_rows, qkv_rows], axis=0)
    small = jnp.concatenate([mine, jnp.broadcast_to(shared, (n,) + shared.shape)], axis=1)
    send_b, small, came_a = tied(send_b, small, came_a)
    near_a = late_sum(keep_a, came_a)
    near_b = late_near(keep_b, send_b)
    if n > 8:
        small_near = lax.psum_scatter(small, "dp", scatter_dimension=0, tiled=True)
    else:
        small = jnp.take(small, chunks, axis=0)
        small_near = late_near(small[: n // 2], small[n // 2 :])
    far_u = swapped(other_u, "tensor", 2)
    late_a, far_u = tied(late_far(near_a, bf16), far_u)
    near_b, small_near = tied(near_b, small_near)
    late_b = late_far(near_b, bf16)
    small_own = late_far(small_near, f32)[0]
    late_own = jnp.concatenate([late_a, late_b], axis=1)
    late_own, ff_own = tied(late_own, ff_own)
    norm_grads = summed_over(small_own[:4], "tensor")[:, :own_dims]
    fc_count = fc_rows.shape[0]
    fc_b_total = small_own[5 : 5 + fc_count].reshape(-1)
    qkv_b_total = small_own[5 + fc_count :].reshape(-1)[:qkv_dim].reshape(3, local_dim)
    out_b_total = small_own[4, :own_dims]

    input_grad = norm_back(own_u, came_u, far_u, hidden_in, stats[: hidden_in.shape[0]], cotangent)
    return (
        layer_out,
        input_grad,
        jnp.transpose(late_own.reshape(own_dims, 3, local_dim), (1, 0, 2)),
        qkv_b_total,
        ow_own.T,
        out_b_total,
        ff_own[:, :ff],
        fc_b_total,
        ff_own[:, ff:].T,
        out_b_total,
        norm_grads[0],
        norm_grads[1],
        norm_grads[2],
        norm_grads[3],
    )


def solution(mesh):
    in_specs = (
        P(("dp", "tensor"), None),
        P(None, "dp", "tensor"),
        P(None, "tensor"),
        P("tensor", "dp"),
        P("dp"),
        P("dp", "tensor"),
        P("tensor"),
        P("tensor", "dp"),
        P("dp"),
        P("dp"),
        P("dp"),
        P("dp"),
        P("dp"),
        P("dp"),
        P("dp"),
        P(("dp", "tensor"), None),
    )
    out_specs = (
        P(("dp", "tensor"), None),
        P(("dp", "tensor"), None),
        P(None, "dp", "tensor"),
        P(None, "tensor"),
        P("tensor", "dp"),
        P("dp"),
        P("dp", "tensor"),
        P("tensor"),
        P("tensor", "dp"),
        P("dp"),
        P("dp"),
        P("dp"),
        P("dp"),
        P("dp"),
    )
    return jax.shard_map(body, mesh=mesh, in_specs=in_specs, out_specs=out_specs, check_vma=False)
```

```python
import functools

import jax
import jax.numpy as jnp
from jax import lax
from jax.experimental import pallas as pl
from jax.experimental.pallas import tpu as pltpu
from jax.sharding import PartitionSpec as P

HEAD_DIM = 64
ROT = 16
BLK = 256
SLOTS = (0, 2, 1, 3)

norm_eps = 1e-05
big_negative = -1e30
rope_base = 10000.0
inv_sqrt_two = 0.7071067811865476
inv_sqrt_two_pi = 0.3989422804014327

f32 = jnp.float32
bf16 = jnp.bfloat16


def mm(a, b, ca, cb):
    return lax.dot_general(a, b, (((ca,), (cb,)), ((), ())), preferred_element_type=f32)


def params(**kw):
    return pltpu.CompilerParams(vmem_limit_bytes=56 * 1024 * 1024, **kw)


def cost(flops, moved, exps=0):
    return pl.CostEstimate(flops=int(flops), bytes_accessed=int(moved), transcendentals=int(exps))


def shaped(shape, dtype):
    return jax.ShapeDtypeStruct(shape, dtype)


def passed_along(block, axis, distance):
    devices = range(lax.axis_size(axis))
    route = [(i - distance, i) for i in devices if i - distance in devices]
    return lax.ppermute(block, axis, route)


def swapped(block, axis, bit):
    route = [(i, i ^ bit) for i in range(lax.axis_size(axis))]
    return lax.ppermute(block, axis, route)


def ring_order(n):
    return list(range(0, n, 2)) + list(range(n - 1, 0, -2))


def ring_gather(block, axis, early, late):
    n = lax.axis_size(axis)
    rows = block.shape[0]
    if n > 8:
        return [lax.all_gather(block, axis, axis=0, tiled=True)], jnp.zeros((1,), jnp.int32), early, late
    ring = ring_order(n)
    ahead = [(ring[r], ring[(r + 1) % n]) for r in range(n)]
    behind = [(b, a) for a, b in ahead]
    table = []
    for device in range(n):
        at = ring.index(device)
        row = [device * rows]
        for step in range(1, n // 2):
            row.append(ring[(at - step) % n] * rows)
            row.append(ring[(at + step) % n] * rows)
        row.append(ring[(at + n // 2) % n] * rows)
        table.append(row)
    pieces = [block]
    from_left = from_right = block
    for step in range(1, n // 2):
        from_left = lax.ppermute(from_left, axis, ahead)
        from_right = lax.ppermute(from_right, axis, behind)
        if step == n // 2 - 1:
            from_left, from_right, early = tied(from_left, from_right, early)
        else:
            from_left, from_right = tied(from_left, from_right)
        pieces += [from_left, from_right]
    from_left, late = tied(lax.ppermute(from_left, axis, ahead), late)
    pieces.append(from_left)
    return pieces, jnp.asarray(table, jnp.int32)[lax.axis_index(axis)], early, late


def gather_rows(block, near, far):
    return [block, far, near, swapped(far, "tensor", 1)]


def scatter_near(keep, send):
    count = keep.shape[0] // 2
    came = swapped(send, "tensor", 1)
    other = (keep[count:].astype(f32) + came[count:].astype(f32)).astype(bf16)
    return keep, came, other


def tied(*arrays):
    return lax.optimization_barrier(arrays)


def summed_over(vec, axis):
    n = lax.axis_size(axis)
    bit = 1
    while bit < n:
        vec = vec + swapped(vec, axis, bit)
        bit *= 2
    return vec


def assemble(piece_refs, start_ref, first, out_ref):
    columns = pl.ds(first, out_ref.shape[1])
    for n, ref in enumerate(piece_refs):
        rows = ref.shape[0]
        out_ref[pl.ds(pl.multiple_of(start_ref[n], rows), rows), :] = ref[:, columns]


def take_rows(block_refs, out_ref):
    for n, ref in enumerate(block_refs):

        @pl.when(pl.program_id(0) == n)
        def _():
            out_ref[...] = ref[...]


def row_stats(x):
    mean = jnp.mean(x, axis=-1, keepdims=True)
    center = x - mean
    return mean, lax.rsqrt(jnp.mean(center * center, axis=-1, keepdims=True) + norm_eps)


def normed_from(x_ref, stats_ref):
    return (x_ref[...].astype(f32) - stats_ref[:, 0:1]) * stats_ref[:, 1:2]


def ff_kernel(pieces, start_ref, x_ref, stats_ref, b_ref, vec_ref, fc2_w, *refs):
    g_refs, w_refs = refs[:4], refs[4 : 4 + pieces]
    out_ref, u_ref, g_ref, grads_ref, small_ref, fc_w, fc_acc, fc2_acc = refs[4 + pieces :]
    take_rows(g_refs, g_ref)
    step = pl.program_id(0)
    ff = fc2_w.shape[1]

    @pl.when(step == 0)
    def _():
        assemble(w_refs, start_ref, 0, fc_w)
        fc_acc[...] = jnp.zeros_like(fc_acc)
        fc2_acc[...] = jnp.zeros_like(fc2_acc)
        small_ref[...] = jnp.zeros_like(small_ref)

    gain, shift = vec_ref[4:5, :], vec_ref[5:6, :]
    normed = normed_from(x_ref, stats_ref)
    normed_two = (normed * gain + shift).astype(bf16)
    pre = mm(normed_two, fc_w[...], 1, 0) + b_ref[...]
    cdf = 0.5 + 0.5 * lax.erf(pre * inv_sqrt_two)
    act = (pre * cdf).astype(bf16)
    slope = cdf + pre * (jnp.exp(-0.5 * pre * pre) * inv_sqrt_two_pi)
    out_ref[...] = mm(act, fc2_w[...], 1, 1).astype(bf16)
    g = g_ref[...]
    pre_grad = (mm(g, fc2_w[...], 1, 0) * slope).astype(bf16)
    two_grad = mm(pre_grad, fc_w[...], 1, 1)
    u_ref[...] = (two_grad * gain).astype(bf16)
    fc_acc[...] += mm(normed_two, pre_grad, 0, 0)
    fc2_acc[...] += mm(g, act, 0, 0)
    small_ref[0:1, :] += jnp.sum(two_grad * normed, axis=0, keepdims=True)
    small_ref[1:2, :] += jnp.sum(two_grad, axis=0, keepdims=True)
    small_ref[2:3, :] += jnp.sum(g.astype(f32), axis=0, keepdims=True)
    small_ref[3:4, :] += jnp.sum(pre_grad.astype(f32), axis=0, keepdims=True)

    @pl.when(step == pl.num_programs(0) - 1)
    def _():
        grads_ref[:, :ff] = fc_acc[...].astype(bf16)
        grads_ref[:, ff:] = fc2_acc[...].astype(bf16)


def feed_forward(starts, x, g, stats, b_fc, vec, fc2_w, pieces, ff):
    tokens, dim = x.shape
    rows = tokens // 4
    spec = pl.BlockSpec((rows, dim), lambda s, *_: (s, 0))
    whole = lambda shape: pl.BlockSpec(shape, lambda s, *_: (0, 0))
    return pl.pallas_call(
        functools.partial(ff_kernel, len(pieces)),
        grid_spec=pltpu.PrefetchScalarGridSpec(
            num_scalar_prefetch=1,
            grid=(4,),
            in_specs=[
                spec,
                pl.BlockSpec((rows, 128), lambda s, *_: (s, 0)),
                whole((1, ff)),
                whole(vec.shape),
                whole(fc2_w.shape),
            ]
            + [whole(p.shape) for p in g + pieces],
            out_specs=[spec, spec, spec, whole((dim, 2 * ff)), whole((8, dim))],
            scratch_shapes=[pltpu.VMEM((dim, ff), bf16)] + [pltpu.VMEM((dim, ff), f32)] * 2,
        ),
        out_shape=[
            shaped((tokens, dim), bf16),
            shaped((tokens, dim), bf16),
            shaped((tokens, dim), bf16),
            shaped((dim, 2 * ff), bf16),
            shaped((8, dim), f32),
        ],
        compiler_params=params(),
        cost_estimate=cost(12 * tokens * dim * ff, 8 * tokens * dim + 8 * dim * ff, 2 * tokens * ff),
        name="feed_forward",
    )(starts, x, stats, b_fc, vec, fc2_w, *g, *pieces)


def turned(x, cos_t, sin_t):
    half = ROT // 2
    out = []
    for h in range(x.shape[0] // HEAD_DIM):
        a = x[h * HEAD_DIM : h * HEAD_DIM + half]
        b = x[h * HEAD_DIM + half : h * HEAD_DIM + ROT]
        out += [a * cos_t - b * sin_t, b * cos_t + a * sin_t, x[h * HEAD_DIM + ROT : (h + 1) * HEAD_DIM]]
    return jnp.concatenate(out, axis=0)


def project_kernel(pieces, first, start_ref, place_ref, b_ref, cos_ref, sin_ref, *refs):
    x_refs, w_refs = refs[:4], refs[4 : 4 + pieces]
    (q_ref, k_ref, v_ref, halo_ref, x_ref, normed_ref, stats_ref, wt_ref, vec_ref, packed) = refs[4 + pieces :]
    take_rows(x_refs, x_ref)
    feat = q_ref.shape[0]
    width = wt_ref.shape[0]

    @pl.when(pl.program_id(0) == 0)
    def _():
        assemble(w_refs, start_ref, first, packed)
        wt_ref[...] = packed[:, :width].astype(f32).T.astype(bf16)
        vec_ref[...] = packed[:, width:].astype(f32).T[:8]

    x = x_ref[...].astype(f32)
    mean, inv_std = row_stats(x)
    lane = lax.broadcasted_iota(jnp.int32, stats_ref.shape, 1)
    stats_ref[...] = jnp.where(lane == 0, mean, inv_std)
    normed_one = ((x - mean) * inv_std * vec_ref[2:3, :] + vec_ref[3:4, :]).astype(bf16)
    normed_ref[...] = normed_one
    proj = mm(wt_ref[: 3 * feat, :], normed_one, 1, 1) + b_ref[...]
    cos_t, sin_t = cos_ref[...], sin_ref[...]
    q_ref[...] = (turned(proj[:feat], cos_t, sin_t) * HEAD_DIM ** (-0.5)).astype(bf16)
    k_ref[...] = turned(proj[feat : 2 * feat], cos_t, sin_t).astype(bf16)
    v_ref[...] = proj[2 * feat :].astype(bf16)
    rows = k_ref.shape[1]
    halo = halo_ref.shape[1]
    place = place_ref[pl.program_id(0)]
    for n in range(4):
        begin = max(0, 4 * rows - halo - n * rows)
        if begin < rows:
            to = n * rows + begin - (4 * rows - halo)

            @pl.when(place == n)
            def _():
                halo_ref[:feat, to : to + rows - begin] = k_ref[:, begin:]
                halo_ref[feat:, to : to + rows - begin] = v_ref[:, begin:]


def project(starts, places, x, b_col, cos_t, sin_t, pieces, first, feat, halo):
    rows, dim = x[0].shape
    tokens = 4 * rows
    width = 4 * feat
    spec = pl.BlockSpec((rows, dim), lambda s, *_: (s, 0))
    placed = lambda r: pl.BlockSpec((r, rows), lambda s, start, place: (0, place[s]))
    whole = lambda shape: pl.BlockSpec(shape, lambda s, *_: (0, 0))
    return pl.pallas_call(
        functools.partial(project_kernel, len(pieces), first),
        grid_spec=pltpu.PrefetchScalarGridSpec(
            num_scalar_prefetch=2,
            grid=(4,),
            in_specs=[whole(b_col.shape), placed(ROT // 2), placed(ROT // 2)]
            + [whole(p.shape) for p in x + pieces],
            out_specs=[placed(feat)] * 3
            + [
                whole((2 * feat, halo)),
                spec,
                spec,
                pl.BlockSpec((rows, 128), lambda s, *_: (s, 0)),
                whole((width, dim)),
                whole((8, dim)),
            ],
            scratch_shapes=[pltpu.VMEM((dim, width + 128), bf16)],
        ),
        out_shape=[shaped((feat, tokens), bf16)] * 3
        + [
            shaped((2 * feat, halo), bf16),
            shaped((tokens, dim), bf16),
            shaped((tokens, dim), bf16),
            shaped((tokens, 128), f32),
            shaped((width, dim), bf16),
            shaped((8, dim), f32),
        ],
        compiler_params=params(),
        cost_estimate=cost(6 * tokens * dim * feat, 6 * tokens * dim + 4 * dim * width),
        name="project",
    )(starts, places, b_col, cos_t, sin_t, *x, *pieces)


def key_mask(chunk, lo_row, hi_row):
    idx = chunk * BLK + lax.broadcasted_iota(jnp.int32, (BLK, BLK), 0)
    return jnp.where((idx >= lo_row) & (idx <= hi_row), 0.0, big_negative)


def attn_fwd_kernel(heads, halo, first_ref, q_ref, k_ref, v_ref, left_ref, lo_ref, o_ref, lse_ref, keys, values):
    i = pl.program_id(0)
    first = first_ref[i]
    last = i + halo // BLK
    feat = k_ref.shape[0]

    @pl.when(i == 0)
    def _():
        keys[:, :halo] = left_ref[:feat, :]
        keys[:, halo:] = k_ref[...]
        values[:, :halo] = left_ref[feat:, :]
        values[:, halo:] = v_ref[...]

    lo_row = lo_ref[...]
    hi_row = halo + i * BLK + lax.broadcasted_iota(jnp.int32, (1, BLK), 1)

    def step(c, carry):
        cols = pl.ds(pl.multiple_of(c * BLK, BLK), BLK)
        mask = key_mask(c, lo_row, hi_row)
        hs = range(heads)
        feats = [pl.ds(h * HEAD_DIM, HEAD_DIM) for h in hs]
        s = [mm(keys[feats[h], cols], q_ref[feats[h], :], 0, 0) + mask for h in hs]
        tops = [jnp.maximum(carry[h][0], jnp.max(s[h], axis=0, keepdims=True)) for h in hs]
        p = [jnp.exp(s[h] - tops[h]) for h in hs]
        pv = [mm(values[feats[h], cols], p[h].astype(bf16), 1, 0) for h in hs]
        kept = [jnp.exp(carry[h][0] - tops[h]) for h in hs]
        return tuple(
            (
                tops[h],
                carry[h][1] * kept[h] + jnp.sum(p[h], axis=0, keepdims=True),
                carry[h][2] * kept[h] + pv[h],
            )
            for h in hs
        )

    start = tuple(
        (
            jnp.full((1, BLK), big_negative, f32),
            jnp.zeros((1, BLK), f32),
            jnp.zeros((HEAD_DIM, BLK), f32),
        )
        for _ in range(heads)
    )
    done = lax.fori_loop(first, last + 1, step, start)
    for h in range(heads):
        top, total, acc = done[h]
        o_ref[pl.ds(h * HEAD_DIM, HEAD_DIM), :] = (acc / total).astype(bf16)
        lse_ref[pl.ds(h, 1), :] = top + jnp.log(total)


def attention_forward(first, q, k, v, left, lo, halo):
    feat, tokens = q.shape
    heads = feat // HEAD_DIM
    col = lambda i, *_: (0, i)
    whole = lambda shape: pl.BlockSpec(shape, lambda i, *_: (0, 0))
    q_spec = pl.BlockSpec((feat, BLK), col)
    return pl.pallas_call(
        functools.partial(attn_fwd_kernel, heads, halo),
        grid_spec=pltpu.PrefetchScalarGridSpec(
            num_scalar_prefetch=1,
            grid=(tokens // BLK,),
            in_specs=[q_spec, whole(k.shape), whole(v.shape), whole(left.shape), pl.BlockSpec((1, BLK), col)],
            out_specs=[q_spec, pl.BlockSpec((8, BLK), col)],
            scratch_shapes=[pltpu.VMEM((feat, halo + tokens), bf16)] * 2,
        ),
        out_shape=[shaped((feat, tokens), bf16), shaped((8, tokens), f32)],
        compiler_params=params(),
        cost_estimate=cost(16 * feat * tokens * 1024, 8 * feat * tokens, heads * tokens * 1024),
        name="attention_forward",
    )(first, q, k, v, left, lo)


def attn_bwd_step(heads, c, base, q_ref, k_ref, v_ref, do_ref, lse_ref, lo_row, hi_row, deltas, dq_ref, dk_ref, dv_ref):
    cols = pl.ds(pl.multiple_of((c - base) * BLK, BLK), BLK)
    mask = key_mask(c, lo_row, hi_row)
    hs = range(heads)
    feats = [pl.ds(h * HEAD_DIM, HEAD_DIM) for h in hs]
    s = [mm(k_ref[feats[h], cols], q_ref[feats[h], :], 0, 0) + mask for h in hs]
    dp = [mm(v_ref[feats[h], cols], do_ref[feats[h], :], 0, 0) for h in hs]
    p = [jnp.exp(s[h] - lse_ref[pl.ds(h, 1), :]) for h in hs]
    ds = [(p[h] * (dp[h] - deltas[h])).astype(bf16) for h in hs]
    dv = [mm(do_ref[feats[h], :], p[h].astype(bf16), 1, 1) for h in hs]
    dk = [mm(q_ref[feats[h], :], ds[h], 1, 1) for h in hs]
    dq = [mm(k_ref[feats[h], cols], ds[h], 1, 0) for h in hs]
    for h in hs:
        dv_ref[feats[h], cols] += dv[h]
        dk_ref[feats[h], cols] += dk[h]
        dq_ref[feats[h], :] += dq[h]


def row_deltas(heads, o_ref, do_ref):
    deltas = []
    for h in range(heads):
        feats = pl.ds(h * HEAD_DIM, HEAD_DIM)
        prod = do_ref[feats, :].astype(f32) * o_ref[feats, :].astype(f32)
        deltas.append(jnp.sum(prod, axis=0, keepdims=True))
    return deltas


def halo_bwd_kernel(heads, halo, first_ref, q_ref, left_ref, lo_ref, o_ref, lse_ref, do_ref, dq_ref, back_ref, dk, dv):
    i = pl.program_id(0)
    feat = q_ref.shape[0]

    @pl.when(i == 0)
    def _():
        dk[...] = jnp.zeros_like(dk)
        dv[...] = jnp.zeros_like(dv)

    lo_row = lo_ref[...]
    hi_row = jnp.full((1, BLK), halo, jnp.int32)
    dq_ref[...] = jnp.zeros_like(dq_ref)
    deltas = row_deltas(heads, o_ref, do_ref)
    k_ref, v_ref = left_ref.at[:feat, :], left_ref.at[feat:, :]

    def step(c, carry):
        attn_bwd_step(
            heads, c, 0, q_ref, k_ref, v_ref, do_ref, lse_ref, lo_row, hi_row, deltas, dq_ref, dk, dv
        )
        return carry

    lax.fori_loop(first_ref[i], halo // BLK, step, 0)

    @pl.when(i == pl.num_programs(0) - 1)
    def _():
        back_ref[:feat, :] = dk[...].astype(bf16)
        back_ref[feat:, :] = dv[...].astype(bf16)


def own_bwd_kernel(
    heads, halo, first_ref, q_ref, k_ref, v_ref, lo_ref, o_ref, lse_ref, do_ref, part_ref, dq_ref, dk_ref, dv_ref
):
    i = pl.program_id(0)
    base = halo // BLK

    @pl.when(i == 0)
    def _():
        dk_ref[...] = jnp.zeros_like(dk_ref)
        dv_ref[...] = jnp.zeros_like(dv_ref)

    @pl.when(i < base)
    def _():
        dq_ref[...] = part_ref[...]

    @pl.when(i >= base)
    def _():
        dq_ref[...] = jnp.zeros_like(dq_ref)

    lo_row = lo_ref[...]
    hi_row = halo + i * BLK + lax.broadcasted_iota(jnp.int32, (1, BLK), 1)
    deltas = row_deltas(heads, o_ref, do_ref)

    def step(c, carry):
        attn_bwd_step(
            heads, c, base, q_ref, k_ref, v_ref, do_ref, lse_ref, lo_row, hi_row, deltas, dq_ref, dk_ref, dv_ref
        )
        return carry

    lax.fori_loop(jnp.maximum(first_ref[i], base), i + base + 1, step, 0)
    dq_ref[...] = dq_ref[...] * HEAD_DIM ** (-0.5)


def backward_left(first, q, left, lo, o, lse, do, halo):
    feat, tokens = q.shape
    heads = feat // HEAD_DIM
    col = lambda i, *_: (0, i)
    whole = lambda shape: pl.BlockSpec(shape, lambda i, *_: (0, 0))
    q_spec = pl.BlockSpec((feat, BLK), col)
    return pl.pallas_call(
        functools.partial(halo_bwd_kernel, heads, halo),
        grid_spec=pltpu.PrefetchScalarGridSpec(
            num_scalar_prefetch=1,
            grid=(halo // BLK,),
            in_specs=[
                q_spec,
                whole(left.shape),
                pl.BlockSpec((1, BLK), col),
                q_spec,
                pl.BlockSpec((8, BLK), col),
                q_spec,
            ],
            out_specs=[q_spec, whole(left.shape)],
            scratch_shapes=[pltpu.VMEM((feat, halo), f32)] * 2,
        ),
        out_shape=[shaped((feat, halo), f32), shaped(left.shape, bf16)],
        compiler_params=params(),
        cost_estimate=cost(40 * feat * halo * 512, 20 * feat * halo, heads * halo * 512),
        name="attention_backward_left",
    )(first, q, left, lo, o, lse, do)


def backward_own(first, q, k, v, lo, o, lse, do, dq_part, halo):
    feat, tokens = q.shape
    heads = feat // HEAD_DIM
    col = lambda i, *_: (0, i)
    whole = lambda shape: pl.BlockSpec(shape, lambda i, *_: (0, 0))
    q_spec = pl.BlockSpec((feat, BLK), col)
    part_spec = pl.BlockSpec((feat, BLK), lambda i, *_: (0, jnp.minimum(i, halo // BLK - 1)))
    return pl.pallas_call(
        functools.partial(own_bwd_kernel, heads, halo),
        grid_spec=pltpu.PrefetchScalarGridSpec(
            num_scalar_prefetch=1,
            grid=(tokens // BLK,),
            in_specs=[
                q_spec,
                whole(k.shape),
                whole(v.shape),
                pl.BlockSpec((1, BLK), col),
                q_spec,
                pl.BlockSpec((8, BLK), col),
                q_spec,
                part_spec,
            ],
            out_specs=[q_spec, whole(k.shape), whole(v.shape)],
        ),
        out_shape=[shaped((feat, tokens), f32)] * 3,
        compiler_params=params(),
        cost_estimate=cost(40 * feat * tokens * 1024, 20 * feat * tokens, heads * tokens * 1024),
        name="attention_backward_own",
    )(first, q, k, v, lo, o, lse, do, dq_part)


def keep_send_specs(rows, dim):
    keep = pl.BlockSpec((rows, dim), lambda s, *_: (jnp.minimum(s, 1), 0))
    send = pl.BlockSpec((rows, dim), lambda s, *_: (jnp.maximum(s - 2, 0), 0))
    return keep, send


def put_rows(keep_ref, send_ref, value):
    s = pl.program_id(0)

    @pl.when(s < 2)
    def _():
        keep_ref[...] = value

    @pl.when(s >= 2)
    def _():
        send_ref[...] = value


def put_chunks(chunk_ref, keep_ref, send_ref, value):
    parts = chunk_ref.shape[0] // 2
    size = keep_ref.shape[0] // parts
    for half, ref in enumerate((keep_ref, send_ref)):
        for n in range(parts):
            at = pl.ds(pl.multiple_of(chunk_ref[half * parts + n] * size, size), size)
            ref[n * size : (n + 1) * size, :] = value[at, :].astype(bf16)


def out_kernel(
    place_ref, chunk_ref, o_ref, ff_ref, g_ref, w_ref, keep_ref, send_ref, wkeep_ref, wsend_ref, do_ref, acc, acc_t
):
    s = pl.program_id(0)

    @pl.when(s == 0)
    def _():
        acc[...] = jnp.zeros_like(acc)

    total = mm(o_ref[...], w_ref[...], 0, 0) + ff_ref[...].astype(f32)
    put_rows(keep_ref, send_ref, total.astype(bf16))
    acc[...] += mm(o_ref[...], g_ref[...], 1, 0)
    do_ref[...] = mm(w_ref[...], g_ref[...], 1, 1).astype(bf16)

    @pl.when(s == pl.num_programs(0) - 1)
    def _():
        acc_t[...] = acc[...].T
        put_chunks(chunk_ref, wkeep_ref, wsend_ref, acc_t)


def branch_out(places, chunks, o, ff_out, g, wt):
    feat, tokens = o.shape
    dim = wt.shape[1]
    rows = tokens // 4
    keep, send = keep_send_specs(rows, dim)
    spec = pl.BlockSpec((rows, dim), lambda s, *_: (s, 0))
    placed = pl.BlockSpec((feat, rows), lambda s, place, chunk: (0, place[s]))
    whole = lambda shape: pl.BlockSpec(shape, lambda s, *_: (0, 0))
    return pl.pallas_call(
        out_kernel,
        grid_spec=pltpu.PrefetchScalarGridSpec(
            num_scalar_prefetch=2,
            grid=(4,),
            in_specs=[placed, spec, spec, pl.BlockSpec((feat, dim), lambda s, *_: (3, 0))],
            out_specs=[keep, send, whole((dim // 2, feat)), whole((dim // 2, feat)), placed],
            scratch_shapes=[pltpu.VMEM((feat, dim), f32), pltpu.VMEM((dim, feat), f32)],
        ),
        out_shape=[shaped((tokens // 2, dim), bf16)] * 2
        + [shaped((dim // 2, feat), bf16)] * 2
        + [shaped((feat, tokens), bf16)],
        compiler_params=params(),
        cost_estimate=cost(4 * feat * tokens * dim, 6 * tokens * dim),
        name="branch_out",
    )(places, chunks, o, ff_out, g, wt)


def input_grad_kernel(
    halo,
    place_ref,
    dq_ref,
    dk_ref,
    dv_ref,
    back_ref,
    x_ref,
    stats_ref,
    u2_ref,
    wt_ref,
    vec_ref,
    cos_ref,
    sin_ref,
    keep_ref,
    send_ref,
    grad_ref,
    small_ref,
    bias_ref,
    late,
):
    s = pl.program_id(0)
    feat, rows = dq_ref.shape
    tokens = late.shape[1]

    @pl.when(s == 0)
    def _():
        late[:, : tokens - halo] = jnp.zeros((2 * feat, tokens - halo), bf16)
        late[:, tokens - halo :] = back_ref[...]
        small_ref[...] = jnp.zeros_like(small_ref)
        bias_ref[...] = jnp.zeros_like(bias_ref)

    cols = pl.ds(pl.multiple_of(place_ref[s] * rows, rows), rows)
    cos_t, sin_t = cos_ref[...], -sin_ref[...]
    dq = turned(dq_ref[...], cos_t, sin_t)
    dk = turned(dk_ref[...] + late[:feat, cols].astype(f32), cos_t, sin_t)
    dv = dv_ref[...] + late[feat:, cols].astype(f32)
    grad = jnp.concatenate([dq, dk, dv], axis=0).astype(bf16)
    grad_ref[...] = grad
    bias_ref[...] += jnp.sum(grad.astype(f32), axis=1, keepdims=True)
    one_grad = mm(grad, wt_ref[: 3 * feat, :], 0, 0)
    put_rows(keep_ref, send_ref, (one_grad * vec_ref[2:3, :] + u2_ref[...].astype(f32)).astype(bf16))
    normed = normed_from(x_ref, stats_ref)
    small_ref[0:1, :] += jnp.sum(one_grad * normed, axis=0, keepdims=True)
    small_ref[1:2, :] += jnp.sum(one_grad, axis=0, keepdims=True)


def input_gradient(places, dq, dk, dv, back, x, stats, u2, wt, vec, cos_t, sin_t, halo):
    feat, tokens = dq.shape
    dim = x.shape[1]
    rows = tokens // 4
    spec = pl.BlockSpec((rows, dim), lambda s, *_: (s, 0))
    placed = lambda r: pl.BlockSpec((r, rows), lambda s, place: (0, place[s]))
    whole = lambda shape: pl.BlockSpec(shape, lambda s, *_: (0, 0))
    keep, send = keep_send_specs(rows, dim)
    return pl.pallas_call(
        functools.partial(input_grad_kernel, halo),
        grid_spec=pltpu.PrefetchScalarGridSpec(
            num_scalar_prefetch=1,
            grid=(4,),
            in_specs=[placed(feat)] * 3
            + [whole(back.shape), spec, pl.BlockSpec((rows, 128), lambda s, *_: (s, 0)), spec, whole(wt.shape)]
            + [whole(vec.shape)]
            + [placed(ROT // 2)] * 2,
            out_specs=[keep, send, placed(3 * feat), whole((8, dim)), whole((3 * feat, 1))],
            scratch_shapes=[pltpu.VMEM((2 * feat, tokens), bf16)],
        ),
        out_shape=[shaped((tokens // 2, dim), bf16)] * 2
        + [shaped((3 * feat, tokens), bf16), shaped((8, dim), f32), shaped((3 * feat, 1), f32)],
        compiler_params=params(),
        cost_estimate=cost(12 * feat * tokens * dim, 10 * tokens * dim),
        name="input_gradient",
    )(places, dq, dk, dv, back, x, stats, u2, wt, vec, cos_t, sin_t)


def weight_grad_kernel(own_dims, place_ref, chunk_ref, grad_ref, normed_ref, *refs):
    small_refs, (wkeep_ref, wsend_ref, acc, acc_t) = refs[:-4], refs[-4:]
    s = pl.program_id(0)

    @pl.when(s == 0)
    def _():
        acc[...] = jnp.zeros_like(acc)

    width = grad_ref.shape[0]
    acc[:width, :] += mm(grad_ref[...], normed_ref[...], 1, 0)

    @pl.when(s == pl.num_programs(0) - 1)
    def _():
        if small_refs:
            one_ref, ff_ref, bias_ref = small_refs
            acc[256:258, :] = one_ref[0:2, :]
            acc[258:262, :] = ff_ref[0:4, :]
        acc_t[...] = acc[...].T
        if small_refs:
            columns = acc_t[:, 256:]
            lane = lax.broadcasted_iota(jnp.int32, (own_dims, 128), 1)
            shared = jnp.zeros((own_dims, 128), f32)
            count = columns.shape[0] // own_dims
            for n in range(count):
                part = columns[n * own_dims : (n + 1) * own_dims, 5:6]
                shared = jnp.where(lane == 8 + n, part, shared)
            for n in range(bias_ref.shape[0] // own_dims):
                part = bias_ref[n * own_dims : (n + 1) * own_dims, 0:1]
                shared = jnp.where(lane == 8 + count + n, part, shared)
            lane = lax.broadcasted_iota(jnp.int32, columns.shape, 1)
            acc_t[:, 256:] = jnp.where(lane < 5, columns, jnp.concatenate([shared] * count, axis=0))
        put_chunks(chunk_ref, wkeep_ref, wsend_ref, acc_t)


def weight_gradient(places, chunks, grad, normed, width, part, own_dims, small=()):
    tokens = grad.shape[1]
    dim = normed.shape[1]
    rows = tokens // 4
    out_width = 384 if small else width
    whole = lambda shape: pl.BlockSpec(shape, lambda s, *_: (0, 0))
    return pl.pallas_call(
        functools.partial(weight_grad_kernel, own_dims),
        grid_spec=pltpu.PrefetchScalarGridSpec(
            num_scalar_prefetch=2,
            grid=(4,),
            in_specs=[
                pl.BlockSpec((width, rows), lambda s, place, chunk: (part, place[s])),
                pl.BlockSpec((rows, dim), lambda s, *_: (s, 0)),
            ]
            + [whole(a.shape) for a in small],
            out_specs=[whole((dim // 2, out_width))] * 2,
            scratch_shapes=[pltpu.VMEM((out_width, dim), f32), pltpu.VMEM((dim, out_width), f32)],
        ),
        out_shape=[shaped((dim // 2, out_width), bf16)] * 2,
        compiler_params=params(),
        cost_estimate=cost(4 * width * tokens * dim, 4 * tokens * dim),
        name="weight_gradient",
    )(places, chunks, grad, normed, *small)


def norm_back_kernel(own_ref, came_ref, far_ref, x_ref, stats_ref, g_ref, out_ref):
    both = own_ref[...].astype(f32) + came_ref[...].astype(f32) + far_ref[...].astype(f32)
    normed = normed_from(x_ref, stats_ref)
    inv_std = stats_ref[:, 1:2]
    grad = both - jnp.mean(both, axis=-1, keepdims=True)
    grad = grad - normed * jnp.mean(both * normed, axis=-1, keepdims=True)
    out_ref[...] = (g_ref[...].astype(f32) + inv_std * grad).astype(bf16)


def norm_back(own, came, far, x, stats, g):
    count, dim = x.shape
    rows = count // 2
    spec = pl.BlockSpec((rows, dim), lambda s: (s, 0))
    return pl.pallas_call(
        norm_back_kernel,
        grid=(2,),
        in_specs=[spec, spec, spec, spec, pl.BlockSpec((rows, 128), lambda s: (s, 0)), spec],
        out_specs=spec,
        out_shape=shaped((count, dim), bf16),
        compiler_params=params(),
        cost_estimate=cost(20 * count * dim, 12 * count * dim),
        name="norm_back",
    )(own, came, far, x, stats, g)


def rope_tables(positions):
    freq_idx = jnp.arange(0, ROT, 2, dtype=f32)
    inverse = rope_base ** (-freq_idx / ROT)
    angles = inverse[:, None] * positions.astype(f32)[None, :]
    return jnp.cos(angles), jnp.sin(angles)


def late_chunks():
    n = lax.axis_size("dp")
    rank = lax.axis_index("dp")
    if n > 8:
        return jnp.arange(2, dtype=jnp.int32)
    mine = jnp.stack([rank ^ (2 * k) for k in range(n // 2)])
    return jnp.concatenate([mine, mine ^ 1]).astype(jnp.int32)


def late_sent(keep, send):
    n = lax.axis_size("dp")
    if n > 8:
        whole = jnp.concatenate([keep, send], axis=0)
        return None, lax.psum_scatter(whole, "dp", scatter_dimension=0, tiled=True).astype(f32)
    return keep, swapped(send, "dp", 1)


def late_sum(keep, came):
    return came if keep is None else keep.astype(f32) + came.astype(f32)


def late_near(keep, send):
    return late_sum(*late_sent(keep, send))


def late_far(total, dtype):
    n = lax.axis_size("dp")
    if n > 8:
        return total
    size = total.shape[0] * 2 // n
    low = total.astype(dtype)
    own = total[:size]
    for k in range(1, n // 2):
        own = own + swapped(low[k * size : (k + 1) * size], "dp", 2 * k).astype(f32)
    return own


def body(
    hidden_in,
    w_qkv,
    b_qkv,
    w_out,
    b_out,
    w_fc,
    b_fc,
    w_fc2,
    b_fc2,
    ln1_gain,
    ln1_bias,
    ln2_gain,
    ln2_bias,
    segment_ids,
    positions,
    cotangent,
):
    local_dim = w_qkv.shape[2]
    ff = w_fc.shape[1]
    own_dims = w_fc.shape[0]
    seq_len = positions.shape[0]
    halo = seq_len * 3 // 8
    qkv_dim = 3 * local_dim
    rank = lax.axis_index("tensor")
    places = jnp.stack([rank ^ at for at in SLOTS]).astype(jnp.int32)

    vectors = jnp.stack([b_out, b_fc2, ln1_gain, ln1_bias, ln2_gain, ln2_bias], axis=1)
    vectors = jnp.pad(vectors, ((0, 0), (0, 122)))
    block = jnp.concatenate(
        [
            w_fc,
            jnp.transpose(w_qkv, (1, 0, 2)).reshape(own_dims, qkv_dim),
            w_out.T,
            vectors,
        ],
        axis=1,
    )
    x_far, g_far = swapped(hidden_in, "tensor", 2), swapped(cotangent, "tensor", 2)
    x_near, g_near = swapped(hidden_in, "tensor", 1), swapped(cotangent, "tensor", 1)
    pieces, starts, x_far, g_far = ring_gather(block, "dp", x_far, g_far)
    fc2_w = lax.all_gather(w_fc2.T, "dp", axis=0, tiled=True)
    x_blocks = gather_rows(hidden_in, x_near, x_far)
    g_blocks = gather_rows(cotangent, g_near, g_far)

    cos_t, sin_t = rope_tables(positions)
    lo = halo + jnp.arange(seq_len, dtype=jnp.int32) - positions
    first = lo[::BLK] // BLK
    lo_row = lo.reshape(1, seq_len)

    q, k, v, right, x_all, normed_one, stats, wt, vec = project(
        starts,
        places,
        x_blocks,
        b_qkv.astype(f32).reshape(qkv_dim, 1),
        cos_t,
        sin_t,
        pieces,
        ff,
        local_dim,
        halo,
    )
    left = passed_along(right, "dp", 1)
    ff_out, u_two, g_all, ff_grads, ff_small = feed_forward(
        starts, x_all, g_blocks, stats, b_fc.astype(f32).reshape(1, ff), vec, fc2_w, pieces, ff
    )
    ff_own = lax.psum_scatter(ff_grads, "dp", scatter_dimension=0, tiled=True).astype(f32)
    q, ff_out = tied(q, ff_out)

    o, lse = attention_forward(first, q, k, v, left, lo_row, halo)
    chunks = late_chunks()
    out_keep, out_send, ow_keep, ow_send, do = branch_out(places, chunks, o, ff_out, g_all, wt)
    own_o, came_o, other_o = scatter_near(out_keep, out_send)
    ow_near = late_near(ow_keep, ow_send)
    dq_part, back = backward_left(first, q, left, lo_row, o, lse, do, halo)
    dq_part, back, other_o, ow_near = tied(dq_part, back, other_o, ow_near)
    far_o = swapped(other_o, "tensor", 2)
    back = passed_along(back, "dp", -1)
    ow_own = late_far(ow_near, bf16)
    dq, dk, dv = backward_own(first, q, k, v, lo_row, o, lse, do, dq_part, halo)
    back, dq, far_o, ow_own, ff_own = tied(back, dq, far_o, ow_own, ff_own)
    count = hidden_in.shape[0]
    summed = own_o[:count].astype(f32) + came_o[:count].astype(f32) + far_o.astype(f32)
    layer_out = (hidden_in.astype(f32) + summed + vec[0] + vec[1]).astype(bf16)

    u_keep, u_send, proj_grad, one_small, qkv_bias = input_gradient(
        places, dq, dk, dv, back, x_all, stats, u_two, wt, vec, cos_t, sin_t, halo
    )
    own_u, came_u, other_u = scatter_near(u_keep, u_send)
    keep_a, send_a = weight_gradient(places, chunks, proj_grad, normed_one, 2 * local_dim, 0, own_dims)
    proj_grad, other_u, send_a = tied(proj_grad, other_u, send_a)
    keep_a, came_a = late_sent(keep_a, send_a)
    keep_b, send_b = weight_gradient(
        places, chunks, proj_grad, normed_one, local_dim, 2, own_dims, (one_small, ff_small, qkv_bias)
    )
    send_b, came_a = tied(send_b, came_a)
    near_a = late_sum(keep_a, came_a)
    near_b = late_near(keep_b, send_b)
    far_u = swapped(other_u, "tensor", 2)
    late_a, far_u = tied(late_far(near_a, bf16), far_u)
    late_b = late_far(near_b, bf16)
    late_own = jnp.concatenate([late_a, late_b[:, :local_dim]], axis=1)

    vectors = late_b[:, 256:]
    norm_grads = summed_over(vectors, "tensor")[:, :4].T
    fc_count = ff // own_dims
    fc_b_total = vectors[:, 8 : 8 + fc_count].T.reshape(ff)
    qkv_b_total = vectors[:, 8 + fc_count : 8 + fc_count + qkv_dim // own_dims].T.reshape(3, local_dim)
    out_b_total = vectors[:, 4]

    input_grad = norm_back(own_u, came_u, far_u, hidden_in, stats, cotangent)
    return (
        layer_out,
        input_grad,
        jnp.transpose(late_own.reshape(own_dims, 3, local_dim), (1, 0, 2)),
        qkv_b_total,
        ow_own.T,
        out_b_total,
        ff_own[:, :ff],
        fc_b_total,
        ff_own[:, ff:].T,
        out_b_total,
        norm_grads[0],
        norm_grads[1],
        norm_grads[2],
        norm_grads[3],
    )


def solution(mesh):
    in_specs = (
        P(("dp", "tensor"), None),
        P(None, "dp", "tensor"),
        P(None, "tensor"),
        P("tensor", "dp"),
        P("dp"),
        P("dp", "tensor"),
        P("tensor"),
        P("tensor", "dp"),
        P("dp"),
        P("dp"),
        P("dp"),
        P("dp"),
        P("dp"),
        P("dp"),
        P("dp"),
        P(("dp", "tensor"), None),
    )
    out_specs = (
        P(("dp", "tensor"), None),
        P(("dp", "tensor"), None),
        P(None, "dp", "tensor"),
        P(None, "tensor"),
        P("tensor", "dp"),
        P("dp"),
        P("dp", "tensor"),
        P("tensor"),
        P("tensor", "dp"),
        P("dp"),
        P("dp"),
        P("dp"),
        P("dp"),
        P("dp"),
    )
    return jax.shard_map(body, mesh=mesh, in_specs=in_specs, out_specs=out_specs, check_vma=False)
```

```python
import functools

import jax
import jax.numpy as jnp
from jax import lax
from jax.experimental import pallas as pl
from jax.experimental.pallas import tpu as pltpu
from jax.sharding import PartitionSpec as P

HEAD_DIM = 64
ROT = 16
BLK = 256
SLOTS = (0, 2, 1, 3)

norm_eps = 1e-05
big_negative = -1e30
rope_base = 10000.0
inv_sqrt_two = 0.7071067811865476
inv_sqrt_two_pi = 0.3989422804014327

f32 = jnp.float32
bf16 = jnp.bfloat16


def mm(a, b, ca, cb):
    return lax.dot_general(a, b, (((ca,), (cb,)), ((), ())), preferred_element_type=f32)


def params(**kw):
    return pltpu.CompilerParams(vmem_limit_bytes=56 * 1024 * 1024, **kw)


def cost(flops, moved, exps=0):
    return pl.CostEstimate(flops=int(flops) // 16, bytes_accessed=int(moved) // 16, transcendentals=int(exps) // 16)


def shaped(shape, dtype):
    return jax.ShapeDtypeStruct(shape, dtype)


def passed_along(block, axis, distance):
    devices = range(lax.axis_size(axis))
    route = [(i - distance, i) for i in devices if i - distance in devices]
    return lax.ppermute(block, axis, route)


def swapped(block, axis, bit):
    route = [(i, i ^ bit) for i in range(lax.axis_size(axis))]
    return lax.ppermute(block, axis, route)


def ring_order(n):
    return list(range(0, n, 2)) + list(range(n - 1, 0, -2))


def ring_gather(block, axis, early):
    n = lax.axis_size(axis)
    rows = block.shape[0]
    if n > 8:
        return [lax.all_gather(block, axis, axis=0, tiled=True)], jnp.zeros((1,), jnp.int32), early
    ring = ring_order(n)
    ahead = [(ring[r], ring[(r + 1) % n]) for r in range(n)]
    behind = [(b, a) for a, b in ahead]
    table = []
    for device in range(n):
        at = ring.index(device)
        row = [device * rows]
        for step in range(1, n // 2):
            row.append(ring[(at - step) % n] * rows)
            row.append(ring[(at + step) % n] * rows)
        row.append(ring[(at + n // 2) % n] * rows)
        table.append(row)
    pieces = [block]
    from_left = from_right = block
    for step in range(1, n // 2):
        from_left = lax.ppermute(from_left, axis, ahead)
        from_right = lax.ppermute(from_right, axis, behind)
        if step == n // 2 - 1:
            from_left, from_right, early = tied(from_left, from_right, early)
        else:
            from_left, from_right = tied(from_left, from_right)
        pieces += [from_left, from_right]
    pieces.append(lax.ppermute(from_left, axis, ahead))
    return pieces, jnp.asarray(table, jnp.int32)[lax.axis_index(axis)], early


def gather_rows(block, near, far):
    return [block, far, near, swapped(far, "tensor", 1)]


def scatter_near(keep, send):
    count = keep.shape[0] // 2
    came = swapped(send, "tensor", 1)
    other = (keep[count:].astype(f32) + came[count:].astype(f32)).astype(bf16)
    return keep, came, other


def tied(*arrays):
    return lax.optimization_barrier(arrays)


def summed_over(vec, axis):
    n = lax.axis_size(axis)
    bit = 1
    while bit < n:
        vec = vec + swapped(vec, axis, bit)
        bit *= 2
    return vec


def assemble(piece_refs, start_ref, first, out_ref):
    columns = pl.ds(first, out_ref.shape[1])
    for n, ref in enumerate(piece_refs):
        rows = ref.shape[0]
        out_ref[pl.ds(pl.multiple_of(start_ref[n], rows), rows), :] = ref[:, columns]


def take_rows(block_refs, out_ref):
    for n, ref in enumerate(block_refs):

        @pl.when(pl.program_id(0) == n)
        def _():
            out_ref[...] = ref[...]


def row_stats(x):
    mean = jnp.mean(x, axis=-1, keepdims=True)
    center = x - mean
    return mean, lax.rsqrt(jnp.mean(center * center, axis=-1, keepdims=True) + norm_eps)


def normed_from(x_ref, stats_ref):
    return (x_ref[...].astype(f32) - stats_ref[:, 0:1]) * stats_ref[:, 1:2]


def ff_kernel(x_ref, stats_ref, b_ref, vec_ref, w_ref, *refs):
    g_refs, (out_ref, u_ref, g_ref, grads_ref, small_ref, fc_acc, fc2_acc) = refs[:4], refs[4:]
    take_rows(g_refs, g_ref)
    step = pl.program_id(0)
    ff = fc_acc.shape[1]
    fc_w, fc2_w = w_ref.at[:, :ff], w_ref.at[:, ff:]

    @pl.when(step == 0)
    def _():
        fc_acc[...] = jnp.zeros_like(fc_acc)
        fc2_acc[...] = jnp.zeros_like(fc2_acc)
        small_ref[...] = jnp.zeros_like(small_ref)

    gain, shift = vec_ref[4:5, :], vec_ref[5:6, :]
    normed = normed_from(x_ref, stats_ref)
    normed_two = (normed * gain + shift).astype(bf16)
    pre = mm(normed_two, fc_w[...], 1, 0) + b_ref[...]
    cdf = 0.5 + 0.5 * lax.erf(pre * inv_sqrt_two)
    act = (pre * cdf).astype(bf16)
    slope = cdf + pre * (jnp.exp(-0.5 * pre * pre) * inv_sqrt_two_pi)
    out_ref[...] = mm(act, fc2_w[...], 1, 1).astype(bf16)
    g = g_ref[...]
    pre_grad = (mm(g, fc2_w[...], 1, 0) * slope).astype(bf16)
    two_grad = mm(pre_grad, fc_w[...], 1, 1)
    u_ref[...] = (two_grad * gain).astype(bf16)
    fc_acc[...] += mm(normed_two, pre_grad, 0, 0)
    fc2_acc[...] += mm(g, act, 0, 0)
    small_ref[0:1, :] += jnp.sum(two_grad * normed, axis=0, keepdims=True)
    small_ref[1:2, :] += jnp.sum(two_grad, axis=0, keepdims=True)
    small_ref[2:3, :] += jnp.sum(g.astype(f32), axis=0, keepdims=True)
    small_ref[3:4, :] += jnp.sum(pre_grad.astype(f32), axis=0, keepdims=True)

    @pl.when(step == pl.num_programs(0) - 1)
    def _():
        grads_ref[:, :ff] = fc_acc[...].astype(bf16)
        grads_ref[:, ff:] = fc2_acc[...].astype(bf16)


def feed_forward(x, g, stats, b_fc, vec, w, ff):
    tokens, dim = x.shape
    rows = tokens // 4
    spec = pl.BlockSpec((rows, dim), lambda s, *_: (s, 0))
    whole = lambda shape: pl.BlockSpec(shape, lambda s, *_: (0, 0))
    return pl.pallas_call(
        ff_kernel,
        grid_spec=pltpu.PrefetchScalarGridSpec(
            num_scalar_prefetch=0,
            grid=(4,),
            in_specs=[
                spec,
                pl.BlockSpec((rows, 128), lambda s, *_: (s, 0)),
                whole((1, ff)),
                whole(vec.shape),
                whole(w.shape),
            ]
            + [whole(p.shape) for p in g],
            out_specs=[spec, spec, spec, whole((dim, 2 * ff)), whole((8, dim))],
            scratch_shapes=[pltpu.VMEM((dim, ff), f32)] * 2,
        ),
        out_shape=[
            shaped((tokens, dim), bf16),
            shaped((tokens, dim), bf16),
            shaped((tokens, dim), bf16),
            shaped((dim, 2 * ff), bf16),
            shaped((8, dim), f32),
        ],
        compiler_params=params(),
        cost_estimate=cost(12 * tokens * dim * ff, 8 * tokens * dim + 8 * dim * ff, 2 * tokens * ff),
        name="feed_forward",
    )(x, stats, b_fc, vec, w, *g)


def turned(x, cos_t, sin_t):
    half = ROT // 2
    out = []
    for h in range(x.shape[0] // HEAD_DIM):
        a = x[h * HEAD_DIM : h * HEAD_DIM + half]
        b = x[h * HEAD_DIM + half : h * HEAD_DIM + ROT]
        out += [a * cos_t - b * sin_t, b * cos_t + a * sin_t, x[h * HEAD_DIM + ROT : (h + 1) * HEAD_DIM]]
    return jnp.concatenate(out, axis=0)


def project_kernel(pieces, first, start_ref, place_ref, b_ref, cos_ref, sin_ref, *refs):
    x_refs, w_refs = refs[:4], refs[4 : 4 + pieces]
    (q_ref, k_ref, v_ref, halo_ref, x_ref, normed_ref, stats_ref, wt_ref, vec_ref, packed) = refs[4 + pieces :]
    take_rows(x_refs, x_ref)
    feat = q_ref.shape[0]
    width = wt_ref.shape[0]

    @pl.when(pl.program_id(0) == 0)
    def _():
        assemble(w_refs, start_ref, first, packed)
        wt_ref[...] = packed[:, :width].astype(f32).T.astype(bf16)
        vec_ref[...] = packed[:, width:].astype(f32).T[:8]

    x = x_ref[...].astype(f32)
    mean, inv_std = row_stats(x)
    lane = lax.broadcasted_iota(jnp.int32, stats_ref.shape, 1)
    stats_ref[...] = jnp.where(lane == 0, mean, inv_std)
    normed_one = ((x - mean) * inv_std * vec_ref[2:3, :] + vec_ref[3:4, :]).astype(bf16)
    normed_ref[...] = normed_one
    proj = mm(wt_ref[: 3 * feat, :], normed_one, 1, 1) + b_ref[...]
    cos_t, sin_t = cos_ref[...], sin_ref[...]
    q_ref[...] = (turned(proj[:feat], cos_t, sin_t) * HEAD_DIM ** (-0.5)).astype(bf16)
    k_ref[...] = turned(proj[feat : 2 * feat], cos_t, sin_t).astype(bf16)
    v_ref[...] = proj[2 * feat :].astype(bf16)
    rows = k_ref.shape[1]
    halo = halo_ref.shape[1]
    place = place_ref[pl.program_id(0)]
    for n in range(4):
        begin = max(0, 4 * rows - halo - n * rows)
        if begin < rows:
            to = n * rows + begin - (4 * rows - halo)

            @pl.when(place == n)
            def _():
                halo_ref[:feat, to : to + rows - begin] = k_ref[:, begin:]
                halo_ref[feat:, to : to + rows - begin] = v_ref[:, begin:]


def project(starts, places, x, b_col, cos_t, sin_t, pieces, first, feat, halo):
    rows, dim = x[0].shape
    tokens = 4 * rows
    width = 4 * feat
    spec = pl.BlockSpec((rows, dim), lambda s, *_: (s, 0))
    placed = lambda r: pl.BlockSpec((r, rows), lambda s, start, place: (0, place[s]))
    whole = lambda shape: pl.BlockSpec(shape, lambda s, *_: (0, 0))
    return pl.pallas_call(
        functools.partial(project_kernel, len(pieces), first),
        grid_spec=pltpu.PrefetchScalarGridSpec(
            num_scalar_prefetch=2,
            grid=(4,),
            in_specs=[whole(b_col.shape), placed(ROT // 2), placed(ROT // 2)]
            + [whole(p.shape) for p in x + pieces],
            out_specs=[placed(feat)] * 3
            + [
                whole((2 * feat, halo)),
                spec,
                spec,
                pl.BlockSpec((rows, 128), lambda s, *_: (s, 0)),
                whole((width, dim)),
                whole((8, dim)),
            ],
            scratch_shapes=[pltpu.VMEM((dim, width + 128), bf16)],
        ),
        out_shape=[shaped((feat, tokens), bf16)] * 3
        + [
            shaped((2 * feat, halo), bf16),
            shaped((tokens, dim), bf16),
            shaped((tokens, dim), bf16),
            shaped((tokens, 128), f32),
            shaped((width, dim), bf16),
            shaped((8, dim), f32),
        ],
        compiler_params=params(),
        cost_estimate=cost(6 * tokens * dim * feat, 6 * tokens * dim + 4 * dim * width),
        name="project",
    )(starts, places, b_col, cos_t, sin_t, *x, *pieces)


def key_mask(chunk, lo_row, hi_row):
    idx = chunk * BLK + lax.broadcasted_iota(jnp.int32, (BLK, BLK), 0)
    return jnp.where((idx >= lo_row) & (idx <= hi_row), 0.0, big_negative)


def attn_fwd_kernel(heads, halo, first_ref, q_ref, k_ref, v_ref, left_ref, lo_ref, o_ref, lse_ref, keys, values):
    i = pl.program_id(0)
    first = first_ref[i]
    last = i + halo // BLK
    feat = k_ref.shape[0]

    @pl.when(i == 0)
    def _():
        keys[:, :halo] = left_ref[:feat, :]
        keys[:, halo:] = k_ref[...]
        values[:, :halo] = left_ref[feat:, :]
        values[:, halo:] = v_ref[...]

    lo_row = lo_ref[...]
    hi_row = halo + i * BLK + lax.broadcasted_iota(jnp.int32, (1, BLK), 1)

    def step(c, carry):
        cols = pl.ds(pl.multiple_of(c * BLK, BLK), BLK)
        mask = key_mask(c, lo_row, hi_row)
        hs = range(heads)
        feats = [pl.ds(h * HEAD_DIM, HEAD_DIM) for h in hs]
        s = [mm(keys[feats[h], cols], q_ref[feats[h], :], 0, 0) + mask for h in hs]
        tops = [jnp.maximum(carry[h][0], jnp.max(s[h], axis=0, keepdims=True)) for h in hs]
        p = [jnp.exp(s[h] - tops[h]) for h in hs]
        pv = [mm(values[feats[h], cols], p[h].astype(bf16), 1, 0) for h in hs]
        kept = [jnp.exp(carry[h][0] - tops[h]) for h in hs]
        return tuple(
            (
                tops[h],
                carry[h][1] * kept[h] + jnp.sum(p[h], axis=0, keepdims=True),
                carry[h][2] * kept[h] + pv[h],
            )
            for h in hs
        )

    start = tuple(
        (
            jnp.full((1, BLK), big_negative, f32),
            jnp.zeros((1, BLK), f32),
            jnp.zeros((HEAD_DIM, BLK), f32),
        )
        for _ in range(heads)
    )
    done = lax.fori_loop(first, last + 1, step, start)
    for h in range(heads):
        top, total, acc = done[h]
        o_ref[pl.ds(h * HEAD_DIM, HEAD_DIM), :] = (acc / total).astype(bf16)
        lse_ref[pl.ds(h, 1), :] = top + jnp.log(total)


def attention_forward(first, q, k, v, left, lo, halo):
    feat, tokens = q.shape
    heads = feat // HEAD_DIM
    col = lambda i, *_: (0, i)
    whole = lambda shape: pl.BlockSpec(shape, lambda i, *_: (0, 0))
    q_spec = pl.BlockSpec((feat, BLK), col)
    return pl.pallas_call(
        functools.partial(attn_fwd_kernel, heads, halo),
        grid_spec=pltpu.PrefetchScalarGridSpec(
            num_scalar_prefetch=1,
            grid=(tokens // BLK,),
            in_specs=[q_spec, whole(k.shape), whole(v.shape), whole(left.shape), pl.BlockSpec((1, BLK), col)],
            out_specs=[q_spec, pl.BlockSpec((8, BLK), col)],
            scratch_shapes=[pltpu.VMEM((feat, halo + tokens), bf16)] * 2,
        ),
        out_shape=[shaped((feat, tokens), bf16), shaped((8, tokens), f32)],
        compiler_params=params(),
        cost_estimate=cost(16 * feat * tokens * 1024, 8 * feat * tokens, heads * tokens * 1024),
        name="attention_forward",
    )(first, q, k, v, left, lo)


def attn_bwd_step(heads, c, base, q_ref, k_ref, v_ref, do_ref, lse_ref, lo_row, hi_row, deltas, dq_ref, dk_ref, dv_ref):
    cols = pl.ds(pl.multiple_of((c - base) * BLK, BLK), BLK)
    mask = key_mask(c, lo_row, hi_row)
    hs = range(heads)
    feats = [pl.ds(h * HEAD_DIM, HEAD_DIM) for h in hs]
    s = [mm(k_ref[feats[h], cols], q_ref[feats[h], :], 0, 0) + mask for h in hs]
    dp = [mm(v_ref[feats[h], cols], do_ref[feats[h], :], 0, 0) for h in hs]
    p = [jnp.exp(s[h] - lse_ref[pl.ds(h, 1), :]) for h in hs]
    ds = [(p[h] * (dp[h] - deltas[h])).astype(bf16) for h in hs]
    dv = [mm(do_ref[feats[h], :], p[h].astype(bf16), 1, 1) for h in hs]
    dk = [mm(q_ref[feats[h], :], ds[h], 1, 1) for h in hs]
    dq = [mm(k_ref[feats[h], cols], ds[h], 1, 0) for h in hs]
    for h in hs:
        dv_ref[feats[h], cols] += dv[h]
        dk_ref[feats[h], cols] += dk[h]
        dq_ref[feats[h], :] += dq[h]


def row_deltas(heads, o_ref, do_ref):
    deltas = []
    for h in range(heads):
        feats = pl.ds(h * HEAD_DIM, HEAD_DIM)
        prod = do_ref[feats, :].astype(f32) * o_ref[feats, :].astype(f32)
        deltas.append(jnp.sum(prod, axis=0, keepdims=True))
    return deltas


def halo_bwd_kernel(heads, halo, first_ref, q_ref, left_ref, lo_ref, o_ref, lse_ref, do_ref, dq_ref, back_ref, dk, dv):
    i = pl.program_id(0)
    feat = q_ref.shape[0]

    @pl.when(i == 0)
    def _():
        dk[...] = jnp.zeros_like(dk)
        dv[...] = jnp.zeros_like(dv)

    lo_row = lo_ref[...]
    hi_row = jnp.full((1, BLK), halo, jnp.int32)
    dq_ref[...] = jnp.zeros_like(dq_ref)
    deltas = row_deltas(heads, o_ref, do_ref)
    k_ref, v_ref = left_ref.at[:feat, :], left_ref.at[feat:, :]

    def step(c, carry):
        attn_bwd_step(
            heads, c, 0, q_ref, k_ref, v_ref, do_ref, lse_ref, lo_row, hi_row, deltas, dq_ref, dk, dv
        )
        return carry

    lax.fori_loop(first_ref[i], halo // BLK, step, 0)

    @pl.when(i == pl.num_programs(0) - 1)
    def _():
        back_ref[:feat, :] = dk[...].astype(bf16)
        back_ref[feat:, :] = dv[...].astype(bf16)


def own_bwd_kernel(
    heads, halo, first_ref, q_ref, k_ref, v_ref, lo_ref, o_ref, lse_ref, do_ref, part_ref, dq_ref, dk_ref, dv_ref
):
    i = pl.program_id(0)
    base = halo // BLK

    @pl.when(i == 0)
    def _():
        dk_ref[...] = jnp.zeros_like(dk_ref)
        dv_ref[...] = jnp.zeros_like(dv_ref)

    @pl.when(i < base)
    def _():
        dq_ref[...] = part_ref[...]

    @pl.when(i >= base)
    def _():
        dq_ref[...] = jnp.zeros_like(dq_ref)

    lo_row = lo_ref[...]
    hi_row = halo + i * BLK + lax.broadcasted_iota(jnp.int32, (1, BLK), 1)
    deltas = row_deltas(heads, o_ref, do_ref)

    def step(c, carry):
        attn_bwd_step(
            heads, c, base, q_ref, k_ref, v_ref, do_ref, lse_ref, lo_row, hi_row, deltas, dq_ref, dk_ref, dv_ref
        )
        return carry

    lax.fori_loop(jnp.maximum(first_ref[i], base), i + base + 1, step, 0)
    dq_ref[...] = dq_ref[...] * HEAD_DIM ** (-0.5)


def backward_left(first, q, left, lo, o, lse, do, halo):
    feat, tokens = q.shape
    heads = feat // HEAD_DIM
    col = lambda i, *_: (0, i)
    whole = lambda shape: pl.BlockSpec(shape, lambda i, *_: (0, 0))
    q_spec = pl.BlockSpec((feat, BLK), col)
    return pl.pallas_call(
        functools.partial(halo_bwd_kernel, heads, halo),
        grid_spec=pltpu.PrefetchScalarGridSpec(
            num_scalar_prefetch=1,
            grid=(halo // BLK,),
            in_specs=[
                q_spec,
                whole(left.shape),
                pl.BlockSpec((1, BLK), col),
                q_spec,
                pl.BlockSpec((8, BLK), col),
                q_spec,
            ],
            out_specs=[q_spec, whole(left.shape)],
            scratch_shapes=[pltpu.VMEM((feat, halo), f32)] * 2,
        ),
        out_shape=[shaped((feat, halo), f32), shaped(left.shape, bf16)],
        compiler_params=params(),
        cost_estimate=cost(40 * feat * halo * 512, 20 * feat * halo, heads * halo * 512),
        name="attention_backward_left",
    )(first, q, left, lo, o, lse, do)


def backward_own(first, q, k, v, lo, o, lse, do, dq_part, halo):
    feat, tokens = q.shape
    heads = feat // HEAD_DIM
    col = lambda i, *_: (0, i)
    whole = lambda shape: pl.BlockSpec(shape, lambda i, *_: (0, 0))
    q_spec = pl.BlockSpec((feat, BLK), col)
    part_spec = pl.BlockSpec((feat, BLK), lambda i, *_: (0, jnp.minimum(i, halo // BLK - 1)))
    return pl.pallas_call(
        functools.partial(own_bwd_kernel, heads, halo),
        grid_spec=pltpu.PrefetchScalarGridSpec(
            num_scalar_prefetch=1,
            grid=(tokens // BLK,),
            in_specs=[
                q_spec,
                whole(k.shape),
                whole(v.shape),
                pl.BlockSpec((1, BLK), col),
                q_spec,
                pl.BlockSpec((8, BLK), col),
                q_spec,
                part_spec,
            ],
            out_specs=[q_spec, whole(k.shape), whole(v.shape)],
        ),
        out_shape=[shaped((feat, tokens), f32)] * 3,
        compiler_params=params(),
        cost_estimate=cost(40 * feat * tokens * 1024, 20 * feat * tokens, heads * tokens * 1024),
        name="attention_backward_own",
    )(first, q, k, v, lo, o, lse, do, dq_part)


def keep_send_specs(rows, dim):
    keep = pl.BlockSpec((rows, dim), lambda s, *_: (jnp.minimum(s, 1), 0))
    send = pl.BlockSpec((rows, dim), lambda s, *_: (jnp.maximum(s - 2, 0), 0))
    return keep, send


def put_rows(keep_ref, send_ref, value):
    s = pl.program_id(0)

    @pl.when(s < 2)
    def _():
        keep_ref[...] = value

    @pl.when(s >= 2)
    def _():
        send_ref[...] = value


def put_chunks(chunk_ref, keep_ref, send_ref, value):
    parts = chunk_ref.shape[0] // 2
    size = keep_ref.shape[0] // parts
    for half, ref in enumerate((keep_ref, send_ref)):
        for n in range(parts):
            at = pl.ds(pl.multiple_of(chunk_ref[half * parts + n] * size, size), size)
            ref[n * size : (n + 1) * size, :] = value[at, :].astype(bf16)


def out_kernel(
    place_ref, chunk_ref, o_ref, ff_ref, g_ref, w_ref, keep_ref, send_ref, wkeep_ref, wsend_ref, do_ref, acc, acc_t
):
    s = pl.program_id(0)

    @pl.when(s == 0)
    def _():
        acc[...] = jnp.zeros_like(acc)

    total = mm(o_ref[...], w_ref[...], 0, 0) + ff_ref[...].astype(f32)
    put_rows(keep_ref, send_ref, total.astype(bf16))
    acc[...] += mm(o_ref[...], g_ref[...], 1, 0)
    do_ref[...] = mm(w_ref[...], g_ref[...], 1, 1).astype(bf16)

    @pl.when(s == pl.num_programs(0) - 1)
    def _():
        acc_t[...] = acc[...].T
        put_chunks(chunk_ref, wkeep_ref, wsend_ref, acc_t)


def branch_out(places, chunks, o, ff_out, g, wt):
    feat, tokens = o.shape
    dim = wt.shape[1]
    rows = tokens // 4
    keep, send = keep_send_specs(rows, dim)
    spec = pl.BlockSpec((rows, dim), lambda s, *_: (s, 0))
    placed = pl.BlockSpec((feat, rows), lambda s, place, chunk: (0, place[s]))
    whole = lambda shape: pl.BlockSpec(shape, lambda s, *_: (0, 0))
    return pl.pallas_call(
        out_kernel,
        grid_spec=pltpu.PrefetchScalarGridSpec(
            num_scalar_prefetch=2,
            grid=(4,),
            in_specs=[placed, spec, spec, pl.BlockSpec((feat, dim), lambda s, *_: (3, 0))],
            out_specs=[keep, send, whole((dim // 2, feat)), whole((dim // 2, feat)), placed],
            scratch_shapes=[pltpu.VMEM((feat, dim), f32), pltpu.VMEM((dim, feat), f32)],
        ),
        out_shape=[shaped((tokens // 2, dim), bf16)] * 2
        + [shaped((dim // 2, feat), bf16)] * 2
        + [shaped((feat, tokens), bf16)],
        compiler_params=params(),
        cost_estimate=cost(4 * feat * tokens * dim, 6 * tokens * dim),
        name="branch_out",
    )(places, chunks, o, ff_out, g, wt)


def input_grad_kernel(
    halo,
    place_ref,
    dq_ref,
    dk_ref,
    dv_ref,
    back_ref,
    x_ref,
    stats_ref,
    u2_ref,
    wt_ref,
    vec_ref,
    cos_ref,
    sin_ref,
    keep_ref,
    send_ref,
    grad_ref,
    small_ref,
    bias_ref,
    late,
):
    s = pl.program_id(0)
    feat, rows = dq_ref.shape
    tokens = late.shape[1]

    @pl.when(s == 0)
    def _():
        late[:, : tokens - halo] = jnp.zeros((2 * feat, tokens - halo), bf16)
        late[:, tokens - halo :] = back_ref[...]
        small_ref[...] = jnp.zeros_like(small_ref)
        bias_ref[...] = jnp.zeros_like(bias_ref)

    cols = pl.ds(pl.multiple_of(place_ref[s] * rows, rows), rows)
    cos_t, sin_t = cos_ref[...], -sin_ref[...]
    dq = turned(dq_ref[...], cos_t, sin_t)
    dk = turned(dk_ref[...] + late[:feat, cols].astype(f32), cos_t, sin_t)
    dv = dv_ref[...] + late[feat:, cols].astype(f32)
    grad = jnp.concatenate([dq, dk, dv], axis=0).astype(bf16)
    grad_ref[...] = grad
    bias_ref[...] += jnp.sum(grad.astype(f32), axis=1, keepdims=True)
    one_grad = mm(grad, wt_ref[: 3 * feat, :], 0, 0)
    put_rows(keep_ref, send_ref, (one_grad * vec_ref[2:3, :] + u2_ref[...].astype(f32)).astype(bf16))
    normed = normed_from(x_ref, stats_ref)
    small_ref[0:1, :] += jnp.sum(one_grad * normed, axis=0, keepdims=True)
    small_ref[1:2, :] += jnp.sum(one_grad, axis=0, keepdims=True)


def input_gradient(places, dq, dk, dv, back, x, stats, u2, wt, vec, cos_t, sin_t, halo):
    feat, tokens = dq.shape
    dim = x.shape[1]
    rows = tokens // 4
    spec = pl.BlockSpec((rows, dim), lambda s, *_: (s, 0))
    placed = lambda r: pl.BlockSpec((r, rows), lambda s, place: (0, place[s]))
    whole = lambda shape: pl.BlockSpec(shape, lambda s, *_: (0, 0))
    keep, send = keep_send_specs(rows, dim)
    return pl.pallas_call(
        functools.partial(input_grad_kernel, halo),
        grid_spec=pltpu.PrefetchScalarGridSpec(
            num_scalar_prefetch=1,
            grid=(4,),
            in_specs=[placed(feat)] * 3
            + [whole(back.shape), spec, pl.BlockSpec((rows, 128), lambda s, *_: (s, 0)), spec, whole(wt.shape)]
            + [whole(vec.shape)]
            + [placed(ROT // 2)] * 2,
            out_specs=[keep, send, placed(3 * feat), whole((8, dim)), whole((3 * feat, 1))],
            scratch_shapes=[pltpu.VMEM((2 * feat, tokens), bf16)],
        ),
        out_shape=[shaped((tokens // 2, dim), bf16)] * 2
        + [shaped((3 * feat, tokens), bf16), shaped((8, dim), f32), shaped((3 * feat, 1), f32)],
        compiler_params=params(),
        cost_estimate=cost(12 * feat * tokens * dim, 10 * tokens * dim),
        name="input_gradient",
    )(places, dq, dk, dv, back, x, stats, u2, wt, vec, cos_t, sin_t)


def weight_grad_kernel(own_dims, place_ref, chunk_ref, grad_ref, normed_ref, *refs):
    small_refs, (wkeep_ref, wsend_ref, acc, acc_t) = refs[:-4], refs[-4:]
    s = pl.program_id(0)

    @pl.when(s == 0)
    def _():
        acc[...] = jnp.zeros_like(acc)

    width = grad_ref.shape[0]
    acc[:width, :] += mm(grad_ref[...], normed_ref[...], 1, 0)

    @pl.when(s == pl.num_programs(0) - 1)
    def _():
        if small_refs:
            one_ref, ff_ref, bias_ref = small_refs
            acc[256:258, :] = one_ref[0:2, :]
            acc[258:262, :] = ff_ref[0:4, :]
        acc_t[...] = acc[...].T
        if small_refs:
            columns = acc_t[:, 256:]
            lane = lax.broadcasted_iota(jnp.int32, (own_dims, 128), 1)
            shared = jnp.zeros((own_dims, 128), f32)
            count = columns.shape[0] // own_dims
            for n in range(count):
                part = columns[n * own_dims : (n + 1) * own_dims, 5:6]
                shared = jnp.where(lane == 8 + n, part, shared)
            for n in range(bias_ref.shape[0] // own_dims):
                part = bias_ref[n * own_dims : (n + 1) * own_dims, 0:1]
                shared = jnp.where(lane == 8 + count + n, part, shared)
            lane = lax.broadcasted_iota(jnp.int32, columns.shape, 1)
            acc_t[:, 256:] = jnp.where(lane < 5, columns, jnp.concatenate([shared] * count, axis=0))
        put_chunks(chunk_ref, wkeep_ref, wsend_ref, acc_t)


def weight_gradient(places, chunks, grad, normed, width, part, own_dims, small=()):
    tokens = grad.shape[1]
    dim = normed.shape[1]
    rows = tokens // 4
    out_width = 384 if small else width
    whole = lambda shape: pl.BlockSpec(shape, lambda s, *_: (0, 0))
    return pl.pallas_call(
        functools.partial(weight_grad_kernel, own_dims),
        grid_spec=pltpu.PrefetchScalarGridSpec(
            num_scalar_prefetch=2,
            grid=(4,),
            in_specs=[
                pl.BlockSpec((width, rows), lambda s, place, chunk: (part, place[s])),
                pl.BlockSpec((rows, dim), lambda s, *_: (s, 0)),
            ]
            + [whole(a.shape) for a in small],
            out_specs=[whole((dim // 2, out_width))] * 2,
            scratch_shapes=[pltpu.VMEM((out_width, dim), f32), pltpu.VMEM((dim, out_width), f32)],
        ),
        out_shape=[shaped((dim // 2, out_width), bf16)] * 2,
        compiler_params=params(),
        cost_estimate=cost(4 * width * tokens * dim, 4 * tokens * dim),
        name="weight_gradient",
    )(places, chunks, grad, normed, *small)


def norm_back_kernel(own_ref, came_ref, far_ref, x_ref, stats_ref, g_ref, out_ref):
    both = own_ref[...].astype(f32) + came_ref[...].astype(f32) + far_ref[...].astype(f32)
    normed = normed_from(x_ref, stats_ref)
    inv_std = stats_ref[:, 1:2]
    grad = both - jnp.mean(both, axis=-1, keepdims=True)
    grad = grad - normed * jnp.mean(both * normed, axis=-1, keepdims=True)
    out_ref[...] = (g_ref[...].astype(f32) + inv_std * grad).astype(bf16)


def norm_back(own, came, far, x, stats, g):
    count, dim = x.shape
    rows = count // 2
    spec = pl.BlockSpec((rows, dim), lambda s: (s, 0))
    return pl.pallas_call(
        norm_back_kernel,
        grid=(2,),
        in_specs=[spec, spec, spec, spec, pl.BlockSpec((rows, 128), lambda s: (s, 0)), spec],
        out_specs=spec,
        out_shape=shaped((count, dim), bf16),
        compiler_params=params(),
        cost_estimate=cost(20 * count * dim, 12 * count * dim),
        name="norm_back",
    )(own, came, far, x, stats, g)


def rope_tables(positions):
    freq_idx = jnp.arange(0, ROT, 2, dtype=f32)
    inverse = rope_base ** (-freq_idx / ROT)
    angles = inverse[:, None] * positions.astype(f32)[None, :]
    return jnp.cos(angles), jnp.sin(angles)


def late_chunks():
    n = lax.axis_size("dp")
    rank = lax.axis_index("dp")
    if n > 8:
        return jnp.arange(2, dtype=jnp.int32)
    mine = jnp.stack([rank ^ (2 * k) for k in range(n // 2)])
    return jnp.concatenate([mine, mine ^ 1]).astype(jnp.int32)


def late_sent(keep, send):
    n = lax.axis_size("dp")
    if n > 8:
        whole = jnp.concatenate([keep, send], axis=0)
        return None, lax.psum_scatter(whole, "dp", scatter_dimension=0, tiled=True).astype(f32)
    return keep, swapped(send, "dp", 1)


def late_sum(keep, came):
    return came if keep is None else keep.astype(f32) + came.astype(f32)


def late_near(keep, send):
    return late_sum(*late_sent(keep, send))


def late_far(total, dtype):
    n = lax.axis_size("dp")
    if n > 8:
        return total
    size = total.shape[0] * 2 // n
    low = total.astype(dtype)
    own = total[:size]
    for k in range(1, n // 2):
        own = own + swapped(low[k * size : (k + 1) * size], "dp", 2 * k).astype(f32)
    return own


def body(
    hidden_in,
    w_qkv,
    b_qkv,
    w_out,
    b_out,
    w_fc,
    b_fc,
    w_fc2,
    b_fc2,
    ln1_gain,
    ln1_bias,
    ln2_gain,
    ln2_bias,
    segment_ids,
    positions,
    cotangent,
):
    local_dim = w_qkv.shape[2]
    ff = w_fc.shape[1]
    own_dims = w_fc.shape[0]
    seq_len = positions.shape[0]
    halo = seq_len * 3 // 8
    qkv_dim = 3 * local_dim
    rank = lax.axis_index("tensor")
    places = jnp.stack([rank ^ at for at in SLOTS]).astype(jnp.int32)

    vectors = jnp.stack([b_out, b_fc2, ln1_gain, ln1_bias, ln2_gain, ln2_bias], axis=1)
    vectors = jnp.pad(vectors, ((0, 0), (0, 122)))
    block = jnp.concatenate(
        [
            jnp.transpose(w_qkv, (1, 0, 2)).reshape(own_dims, qkv_dim),
            w_out.T,
            vectors,
        ],
        axis=1,
    )
    x_far, g_far = swapped(hidden_in, "tensor", 2), swapped(cotangent, "tensor", 2)
    x_near, g_near = swapped(hidden_in, "tensor", 1), swapped(cotangent, "tensor", 1)
    pieces, starts, x_far = ring_gather(block, "dp", x_far)
    ff_w = lax.all_gather(jnp.concatenate([w_fc, w_fc2.T], axis=1), "dp", axis=0, tiled=True)
    x_blocks = gather_rows(hidden_in, x_near, x_far)

    cos_t, sin_t = rope_tables(positions)
    lo = halo + jnp.arange(seq_len, dtype=jnp.int32) - positions
    first = lo[::BLK] // BLK
    lo_row = lo.reshape(1, seq_len)

    q, k, v, right, x_all, normed_one, stats, wt, vec = project(
        starts,
        places,
        x_blocks,
        b_qkv.astype(f32).reshape(qkv_dim, 1),
        cos_t,
        sin_t,
        pieces,
        0,
        local_dim,
        halo,
    )
    right, g_far = tied(right, g_far)
    left = passed_along(right, "dp", 1)
    g_blocks = gather_rows(cotangent, g_near, g_far)
    ff_out, u_two, g_all, ff_grads, ff_small = feed_forward(
        x_all, g_blocks, stats, b_fc.astype(f32).reshape(1, ff), vec, ff_w, ff
    )
    ff_sum = lax.psum_scatter(ff_grads, "dp", scatter_dimension=0, tiled=True)
    q, ff_out = tied(q, ff_out)

    o, lse = attention_forward(first, q, k, v, left, lo_row, halo)
    chunks = late_chunks()
    out_keep, out_send, ow_keep, ow_send, do = branch_out(places, chunks, o, ff_out, g_all, wt)
    own_o, came_o, other_o = scatter_near(out_keep, out_send)
    ow_near = late_near(ow_keep, ow_send)
    dq_part, back = backward_left(first, q, left, lo_row, o, lse, do, halo)
    dq_part, back, other_o, ow_near = tied(dq_part, back, other_o, ow_near)
    far_o = swapped(other_o, "tensor", 2)
    back = passed_along(back, "dp", -1)
    ow_own = late_far(ow_near, bf16)
    dq, dk, dv = backward_own(first, q, k, v, lo_row, o, lse, do, dq_part, halo)
    back, dq, far_o, ow_own = tied(back, dq, far_o, ow_own)
    count = hidden_in.shape[0]
    summed = own_o[:count].astype(f32) + came_o[:count].astype(f32) + far_o.astype(f32)
    layer_out = (hidden_in.astype(f32) + summed + vec[0] + vec[1]).astype(bf16)

    u_keep, u_send, proj_grad, one_small, qkv_bias = input_gradient(
        places, dq, dk, dv, back, x_all, stats, u_two, wt, vec, cos_t, sin_t, halo
    )
    own_u, came_u, other_u = scatter_near(u_keep, u_send)
    proj_grad, ff_sum = tied(proj_grad, ff_sum)
    keep_a, send_a = weight_gradient(places, chunks, proj_grad, normed_one, 2 * local_dim, 0, own_dims)
    proj_grad, other_u, send_a = tied(proj_grad, other_u, send_a)
    keep_a, came_a = late_sent(keep_a, send_a)
    keep_b, send_b = weight_gradient(
        places, chunks, proj_grad, normed_one, local_dim, 2, own_dims, (one_small, ff_small, qkv_bias)
    )
    send_b, came_a = tied(send_b, came_a)
    near_a = late_sum(keep_a, came_a)
    near_b = late_near(keep_b, send_b)
    far_u = swapped(other_u, "tensor", 2)
    late_a, far_u = tied(late_far(near_a, bf16), far_u)
    late_b = late_far(near_b, bf16)
    late_own = jnp.concatenate([late_a, late_b[:, :local_dim]], axis=1)

    late_b, ff_sum = tied(late_b, ff_sum)
    ff_own = ff_sum.astype(f32)
    vectors = late_b[:, 256:]
    norm_grads = summed_over(vectors, "tensor")[:, :4].T
    fc_count = ff // own_dims
    fc_b_total = vectors[:, 8 : 8 + fc_count].T.reshape(ff)
    qkv_b_total = vectors[:, 8 + fc_count : 8 + fc_count + qkv_dim // own_dims].T.reshape(3, local_dim)
    out_b_total = vectors[:, 4]

    input_grad = norm_back(own_u, came_u, far_u, hidden_in, stats, cotangent)
    return (
        layer_out,
        input_grad,
        jnp.transpose(late_own.reshape(own_dims, 3, local_dim), (1, 0, 2)),
        qkv_b_total,
        ow_own.T,
        out_b_total,
        ff_own[:, :ff],
        fc_b_total,
        ff_own[:, ff:].T,
        out_b_total,
        norm_grads[0],
        norm_grads[1],
        norm_grads[2],
        norm_grads[3],
    )


def solution(mesh):
    in_specs = (
        P(("dp", "tensor"), None),
        P(None, "dp", "tensor"),
        P(None, "tensor"),
        P("tensor", "dp"),
        P("dp"),
        P("dp", "tensor"),
        P("tensor"),
        P("tensor", "dp"),
        P("dp"),
        P("dp"),
        P("dp"),
        P("dp"),
        P("dp"),
        P("dp"),
        P("dp"),
        P(("dp", "tensor"), None),
    )
    out_specs = (
        P(("dp", "tensor"), None),
        P(("dp", "tensor"), None),
        P(None, "dp", "tensor"),
        P(None, "tensor"),
        P("tensor", "dp"),
        P("dp"),
        P("dp", "tensor"),
        P("tensor"),
        P("tensor", "dp"),
        P("dp"),
        P("dp"),
        P("dp"),
        P("dp"),
        P("dp"),
    )
    return jax.shard_map(body, mesh=mesh, in_specs=in_specs, out_specs=out_specs, check_vma=False)
```

```python
import functools

import jax
import jax.numpy as jnp
from jax import lax
from jax.experimental import pallas as pl
from jax.experimental.pallas import tpu as pltpu
from jax.sharding import PartitionSpec as P

HEAD_DIM = 64
ROT = 16
BLK = 256
SLOTS = (0, 2, 1, 3)

norm_eps = 1e-05
big_negative = -1e30
rope_base = 10000.0
inv_sqrt_two = 0.7071067811865476
inv_sqrt_two_pi = 0.3989422804014327

f32 = jnp.float32
bf16 = jnp.bfloat16


def mm(a, b, ca, cb):
    return lax.dot_general(a, b, (((ca,), (cb,)), ((), ())), preferred_element_type=f32)


def params(**kw):
    return pltpu.CompilerParams(vmem_limit_bytes=56 * 1024 * 1024, **kw)


def cost(flops, moved, exps=0):
    return pl.CostEstimate(flops=int(flops) // 16, bytes_accessed=int(moved) // 16, transcendentals=int(exps) // 16)


def shaped(shape, dtype):
    return jax.ShapeDtypeStruct(shape, dtype)


def passed_along(block, axis, distance):
    devices = range(lax.axis_size(axis))
    route = [(i - distance, i) for i in devices if i - distance in devices]
    return lax.ppermute(block, axis, route)


def swapped(block, axis, bit):
    route = [(i, i ^ bit) for i in range(lax.axis_size(axis))]
    return lax.ppermute(block, axis, route)


def ring_order(n):
    return list(range(0, n, 2)) + list(range(n - 1, 0, -2))


def ring_gather(block, axis, early):
    n = lax.axis_size(axis)
    rows = block.shape[0]
    if n > 8:
        return [lax.all_gather(block, axis, axis=0, tiled=True)], jnp.zeros((1,), jnp.int32), early
    ring = ring_order(n)
    ahead = [(ring[r], ring[(r + 1) % n]) for r in range(n)]
    behind = [(b, a) for a, b in ahead]
    table = []
    for device in range(n):
        at = ring.index(device)
        row = [device * rows]
        for step in range(1, n // 2):
            row.append(ring[(at - step) % n] * rows)
            row.append(ring[(at + step) % n] * rows)
        row.append(ring[(at + n // 2) % n] * rows)
        table.append(row)
    pieces = [block]
    from_left = from_right = block
    for step in range(1, n // 2):
        from_left = lax.ppermute(from_left, axis, ahead)
        from_right = lax.ppermute(from_right, axis, behind)
        if step == n // 2 - 1:
            from_left, from_right, early = tied(from_left, from_right, early)
        else:
            from_left, from_right = tied(from_left, from_right)
        pieces += [from_left, from_right]
    pieces.append(lax.ppermute(from_left, axis, ahead))
    return pieces, jnp.asarray(table, jnp.int32)[lax.axis_index(axis)], early


def gather_rows(block, near, far):
    return [block, far, near, swapped(far, "tensor", 1)]


def scatter_near(keep, send):
    count = keep.shape[0] // 2
    came = swapped(send, "tensor", 1)
    other = (keep[count:].astype(f32) + came[count:].astype(f32)).astype(bf16)
    return keep, came, other


def tied(*arrays):
    return lax.optimization_barrier(arrays)


def summed_over(vec, axis):
    n = lax.axis_size(axis)
    bit = 1
    while bit < n:
        vec = vec + swapped(vec, axis, bit)
        bit *= 2
    return vec


def assemble(piece_refs, start_ref, first, out_ref):
    columns = pl.ds(first, out_ref.shape[1])
    for n, ref in enumerate(piece_refs):
        rows = ref.shape[0]
        out_ref[pl.ds(pl.multiple_of(start_ref[n], rows), rows), :] = ref[:, columns]


def take_rows(block_refs, out_ref):
    for n, ref in enumerate(block_refs):

        @pl.when(pl.program_id(0) == n)
        def _():
            out_ref[...] = ref[...]


def row_stats(x):
    mean = jnp.mean(x, axis=-1, keepdims=True)
    center = x - mean
    return mean, lax.rsqrt(jnp.mean(center * center, axis=-1, keepdims=True) + norm_eps)


def normed_from(x_ref, stats_ref):
    return (x_ref[...].astype(f32) - stats_ref[:, 0:1]) * stats_ref[:, 1:2]


def ff_kernel(x_ref, stats_ref, b_ref, vec_ref, w_ref, *refs):
    g_refs, (out_ref, u_ref, g_ref, grads_ref, small_ref, fc_acc, fc2_acc) = refs[:4], refs[4:]
    take_rows(g_refs, g_ref)
    step = pl.program_id(0)
    ff = fc_acc.shape[1]
    fc_w, fc2_w = w_ref.at[:, :ff], w_ref.at[:, ff:]

    @pl.when(step == 0)
    def _():
        fc_acc[...] = jnp.zeros_like(fc_acc)
        fc2_acc[...] = jnp.zeros_like(fc2_acc)
        small_ref[...] = jnp.zeros_like(small_ref)

    gain, shift = vec_ref[4:5, :], vec_ref[5:6, :]
    normed = normed_from(x_ref, stats_ref)
    normed_two = (normed * gain + shift).astype(bf16)
    pre = mm(normed_two, fc_w[...], 1, 0) + b_ref[...]
    cdf = 0.5 + 0.5 * lax.erf(pre * inv_sqrt_two)
    act = (pre * cdf).astype(bf16)
    slope = cdf + pre * (jnp.exp(-0.5 * pre * pre) * inv_sqrt_two_pi)
    out_ref[...] = mm(act, fc2_w[...], 1, 1).astype(bf16)
    g = g_ref[...]
    pre_grad = (mm(g, fc2_w[...], 1, 0) * slope).astype(bf16)
    two_grad = mm(pre_grad, fc_w[...], 1, 1)
    u_ref[...] = (two_grad * gain).astype(bf16)
    fc_acc[...] += mm(normed_two, pre_grad, 0, 0)
    fc2_acc[...] += mm(g, act, 0, 0)
    small_ref[0:1, :] += jnp.sum(two_grad * normed, axis=0, keepdims=True)
    small_ref[1:2, :] += jnp.sum(two_grad, axis=0, keepdims=True)
    small_ref[2:3, :] += jnp.sum(g.astype(f32), axis=0, keepdims=True)
    small_ref[3:4, :] += jnp.sum(pre_grad.astype(f32), axis=0, keepdims=True)

    @pl.when(step == pl.num_programs(0) - 1)
    def _():
        grads_ref[:, :ff] = fc_acc[...].astype(bf16)
        grads_ref[:, ff:] = fc2_acc[...].astype(bf16)


def feed_forward(x, g, stats, b_fc, vec, w, ff):
    tokens, dim = x.shape
    rows = tokens // 4
    spec = pl.BlockSpec((rows, dim), lambda s, *_: (s, 0))
    whole = lambda shape: pl.BlockSpec(shape, lambda s, *_: (0, 0))
    return pl.pallas_call(
        ff_kernel,
        grid_spec=pltpu.PrefetchScalarGridSpec(
            num_scalar_prefetch=0,
            grid=(4,),
            in_specs=[
                spec,
                pl.BlockSpec((rows, 128), lambda s, *_: (s, 0)),
                whole((1, ff)),
                whole(vec.shape),
                whole(w.shape),
            ]
            + [whole(p.shape) for p in g],
            out_specs=[spec, spec, spec, whole((dim, 2 * ff)), whole((8, dim))],
            scratch_shapes=[pltpu.VMEM((dim, ff), f32)] * 2,
        ),
        out_shape=[
            shaped((tokens, dim), bf16),
            shaped((tokens, dim), bf16),
            shaped((tokens, dim), bf16),
            shaped((dim, 2 * ff), bf16),
            shaped((8, dim), f32),
        ],
        compiler_params=params(),
        cost_estimate=cost(12 * tokens * dim * ff, 8 * tokens * dim + 8 * dim * ff, 2 * tokens * ff),
        name="feed_forward",
    )(x, stats, b_fc, vec, w, *g)


def turned(x, cos_t, sin_t):
    half = ROT // 2
    out = []
    for h in range(x.shape[0] // HEAD_DIM):
        a = x[h * HEAD_DIM : h * HEAD_DIM + half]
        b = x[h * HEAD_DIM + half : h * HEAD_DIM + ROT]
        out += [a * cos_t - b * sin_t, b * cos_t + a * sin_t, x[h * HEAD_DIM + ROT : (h + 1) * HEAD_DIM]]
    return jnp.concatenate(out, axis=0)


def project_kernel(pieces, first, start_ref, place_ref, b_ref, cos_ref, sin_ref, *refs):
    x_refs, w_refs = refs[:4], refs[4 : 4 + pieces]
    (q_ref, k_ref, v_ref, halo_ref, x_ref, normed_ref, stats_ref, wt_ref, vec_ref, packed) = refs[4 + pieces :]
    take_rows(x_refs, x_ref)
    feat = q_ref.shape[0]
    width = wt_ref.shape[0]

    @pl.when(pl.program_id(0) == 0)
    def _():
        assemble(w_refs, start_ref, first, packed)
        wt_ref[...] = packed[:, :width].astype(f32).T.astype(bf16)
        vec_ref[...] = packed[:, width:].astype(f32).T[:8]

    x = x_ref[...].astype(f32)
    mean, inv_std = row_stats(x)
    lane = lax.broadcasted_iota(jnp.int32, stats_ref.shape, 1)
    stats_ref[...] = jnp.where(lane == 0, mean, inv_std)
    normed_one = ((x - mean) * inv_std * vec_ref[2:3, :] + vec_ref[3:4, :]).astype(bf16)
    normed_ref[...] = normed_one
    proj = mm(wt_ref[: 3 * feat, :], normed_one, 1, 1) + b_ref[...]
    cos_t, sin_t = cos_ref[...], sin_ref[...]
    q_ref[...] = (turned(proj[:feat], cos_t, sin_t) * HEAD_DIM ** (-0.5)).astype(bf16)
    k_ref[...] = turned(proj[feat : 2 * feat], cos_t, sin_t).astype(bf16)
    v_ref[...] = proj[2 * feat :].astype(bf16)
    rows = k_ref.shape[1]
    halo = halo_ref.shape[1]
    place = place_ref[pl.program_id(0)]
    for n in range(4):
        begin = max(0, 4 * rows - halo - n * rows)
        if begin < rows:
            to = n * rows + begin - (4 * rows - halo)

            @pl.when(place == n)
            def _():
                halo_ref[:feat, to : to + rows - begin] = k_ref[:, begin:]
                halo_ref[feat:, to : to + rows - begin] = v_ref[:, begin:]


def project(starts, places, x, b_col, cos_t, sin_t, pieces, first, feat, halo):
    rows, dim = x[0].shape
    tokens = 4 * rows
    width = 4 * feat
    spec = pl.BlockSpec((rows, dim), lambda s, *_: (s, 0))
    placed = lambda r: pl.BlockSpec((r, rows), lambda s, start, place: (0, place[s]))
    whole = lambda shape: pl.BlockSpec(shape, lambda s, *_: (0, 0))
    return pl.pallas_call(
        functools.partial(project_kernel, len(pieces), first),
        grid_spec=pltpu.PrefetchScalarGridSpec(
            num_scalar_prefetch=2,
            grid=(4,),
            in_specs=[whole(b_col.shape), placed(ROT // 2), placed(ROT // 2)]
            + [whole(p.shape) for p in x + pieces],
            out_specs=[placed(feat)] * 3
            + [
                whole((2 * feat, halo)),
                spec,
                spec,
                pl.BlockSpec((rows, 128), lambda s, *_: (s, 0)),
                whole((width, dim)),
                whole((8, dim)),
            ],
            scratch_shapes=[pltpu.VMEM((dim, width + 128), bf16)],
        ),
        out_shape=[shaped((feat, tokens), bf16)] * 3
        + [
            shaped((2 * feat, halo), bf16),
            shaped((tokens, dim), bf16),
            shaped((tokens, dim), bf16),
            shaped((tokens, 128), f32),
            shaped((width, dim), bf16),
            shaped((8, dim), f32),
        ],
        compiler_params=params(),
        cost_estimate=cost(6 * tokens * dim * feat, 6 * tokens * dim + 4 * dim * width),
        name="project",
    )(starts, places, b_col, cos_t, sin_t, *x, *pieces)


def key_mask(chunk, lo_row, hi_row):
    idx = chunk * BLK + lax.broadcasted_iota(jnp.int32, (BLK, BLK), 0)
    return jnp.where((idx >= lo_row) & (idx <= hi_row), 0.0, big_negative)


def attn_fwd_kernel(heads, halo, first_ref, q_ref, k_ref, v_ref, left_ref, lo_ref, o_ref, lse_ref, keys, values):
    i = pl.program_id(0)
    first = first_ref[i]
    last = i + halo // BLK
    feat = k_ref.shape[0]

    @pl.when(i == 0)
    def _():
        keys[:, :halo] = left_ref[:feat, :]
        keys[:, halo:] = k_ref[...]
        values[:, :halo] = left_ref[feat:, :]
        values[:, halo:] = v_ref[...]

    lo_row = lo_ref[...]
    hi_row = halo + i * BLK + lax.broadcasted_iota(jnp.int32, (1, BLK), 1)

    def step(c, carry):
        cols = pl.ds(pl.multiple_of(c * BLK, BLK), BLK)
        mask = key_mask(c, lo_row, hi_row)
        hs = range(heads)
        feats = [pl.ds(h * HEAD_DIM, HEAD_DIM) for h in hs]
        s = [mm(keys[feats[h], cols], q_ref[feats[h], :], 0, 0) + mask for h in hs]
        tops = [jnp.maximum(carry[h][0], jnp.max(s[h], axis=0, keepdims=True)) for h in hs]
        p = [jnp.exp(s[h] - tops[h]) for h in hs]
        pv = [mm(values[feats[h], cols], p[h].astype(bf16), 1, 0) for h in hs]
        kept = [jnp.exp(carry[h][0] - tops[h]) for h in hs]
        return tuple(
            (
                tops[h],
                carry[h][1] * kept[h] + jnp.sum(p[h], axis=0, keepdims=True),
                carry[h][2] * kept[h] + pv[h],
            )
            for h in hs
        )

    start = tuple(
        (
            jnp.full((1, BLK), big_negative, f32),
            jnp.zeros((1, BLK), f32),
            jnp.zeros((HEAD_DIM, BLK), f32),
        )
        for _ in range(heads)
    )
    done = lax.fori_loop(first, last + 1, step, start)
    for h in range(heads):
        top, total, acc = done[h]
        o_ref[pl.ds(h * HEAD_DIM, HEAD_DIM), :] = (acc / total).astype(bf16)
        lse_ref[pl.ds(h, 1), :] = top + jnp.log(total)


def attention_forward(first, q, k, v, left, lo, halo):
    feat, tokens = q.shape
    heads = feat // HEAD_DIM
    col = lambda i, *_: (0, i)
    whole = lambda shape: pl.BlockSpec(shape, lambda i, *_: (0, 0))
    q_spec = pl.BlockSpec((feat, BLK), col)
    return pl.pallas_call(
        functools.partial(attn_fwd_kernel, heads, halo),
        grid_spec=pltpu.PrefetchScalarGridSpec(
            num_scalar_prefetch=1,
            grid=(tokens // BLK,),
            in_specs=[q_spec, whole(k.shape), whole(v.shape), whole(left.shape), pl.BlockSpec((1, BLK), col)],
            out_specs=[q_spec, pl.BlockSpec((8, BLK), col)],
            scratch_shapes=[pltpu.VMEM((feat, halo + tokens), bf16)] * 2,
        ),
        out_shape=[shaped((feat, tokens), bf16), shaped((8, tokens), f32)],
        compiler_params=params(),
        cost_estimate=cost(16 * feat * tokens * 1024, 8 * feat * tokens, heads * tokens * 1024),
        name="attention_forward",
    )(first, q, k, v, left, lo)


def attn_bwd_step(heads, c, base, q_ref, k_ref, v_ref, do_ref, lse_ref, lo_row, hi_row, deltas, dq_ref, dk_ref, dv_ref):
    cols = pl.ds(pl.multiple_of((c - base) * BLK, BLK), BLK)
    mask = key_mask(c, lo_row, hi_row)
    hs = range(heads)
    feats = [pl.ds(h * HEAD_DIM, HEAD_DIM) for h in hs]
    s = [mm(k_ref[feats[h], cols], q_ref[feats[h], :], 0, 0) + mask for h in hs]
    dp = [mm(v_ref[feats[h], cols], do_ref[feats[h], :], 0, 0) for h in hs]
    p = [jnp.exp(s[h] - lse_ref[pl.ds(h, 1), :]) for h in hs]
    ds = [(p[h] * (dp[h] - deltas[h])).astype(bf16) for h in hs]
    dv = [mm(do_ref[feats[h], :], p[h].astype(bf16), 1, 1) for h in hs]
    dk = [mm(q_ref[feats[h], :], ds[h], 1, 1) for h in hs]
    dq = [mm(k_ref[feats[h], cols], ds[h], 1, 0) for h in hs]
    for h in hs:
        dv_ref[feats[h], cols] += dv[h]
        dk_ref[feats[h], cols] += dk[h]
        dq_ref[feats[h], :] += dq[h]


def row_deltas(heads, o_ref, do_ref):
    deltas = []
    for h in range(heads):
        feats = pl.ds(h * HEAD_DIM, HEAD_DIM)
        prod = do_ref[feats, :].astype(f32) * o_ref[feats, :].astype(f32)
        deltas.append(jnp.sum(prod, axis=0, keepdims=True))
    return deltas


def halo_bwd_kernel(heads, halo, first_ref, q_ref, left_ref, lo_ref, o_ref, lse_ref, do_ref, dq_ref, back_ref, dk, dv):
    i = pl.program_id(0)
    feat = q_ref.shape[0]

    @pl.when(i == 0)
    def _():
        dk[...] = jnp.zeros_like(dk)
        dv[...] = jnp.zeros_like(dv)

    lo_row = lo_ref[...]
    hi_row = jnp.full((1, BLK), halo, jnp.int32)
    dq_ref[...] = jnp.zeros_like(dq_ref)
    deltas = row_deltas(heads, o_ref, do_ref)
    k_ref, v_ref = left_ref.at[:feat, :], left_ref.at[feat:, :]

    def step(c, carry):
        attn_bwd_step(
            heads, c, 0, q_ref, k_ref, v_ref, do_ref, lse_ref, lo_row, hi_row, deltas, dq_ref, dk, dv
        )
        return carry

    lax.fori_loop(first_ref[i], halo // BLK, step, 0)

    @pl.when(i == pl.num_programs(0) - 1)
    def _():
        back_ref[:feat, :] = dk[...].astype(bf16)
        back_ref[feat:, :] = dv[...].astype(bf16)


def own_bwd_kernel(
    heads, halo, first_ref, q_ref, k_ref, v_ref, lo_ref, o_ref, lse_ref, do_ref, part_ref, dq_ref, dk_ref, dv_ref
):
    i = pl.program_id(0)
    base = halo // BLK

    @pl.when(i == 0)
    def _():
        dk_ref[...] = jnp.zeros_like(dk_ref)
        dv_ref[...] = jnp.zeros_like(dv_ref)

    @pl.when(i < base)
    def _():
        dq_ref[...] = part_ref[...]

    @pl.when(i >= base)
    def _():
        dq_ref[...] = jnp.zeros_like(dq_ref)

    lo_row = lo_ref[...]
    hi_row = halo + i * BLK + lax.broadcasted_iota(jnp.int32, (1, BLK), 1)
    deltas = row_deltas(heads, o_ref, do_ref)

    def step(c, carry):
        attn_bwd_step(
            heads, c, base, q_ref, k_ref, v_ref, do_ref, lse_ref, lo_row, hi_row, deltas, dq_ref, dk_ref, dv_ref
        )
        return carry

    lax.fori_loop(jnp.maximum(first_ref[i], base), i + base + 1, step, 0)
    dq_ref[...] = dq_ref[...] * HEAD_DIM ** (-0.5)


def backward_left(first, q, left, lo, o, lse, do, halo):
    feat, tokens = q.shape
    heads = feat // HEAD_DIM
    col = lambda i, *_: (0, i)
    whole = lambda shape: pl.BlockSpec(shape, lambda i, *_: (0, 0))
    q_spec = pl.BlockSpec((feat, BLK), col)
    return pl.pallas_call(
        functools.partial(halo_bwd_kernel, heads, halo),
        grid_spec=pltpu.PrefetchScalarGridSpec(
            num_scalar_prefetch=1,
            grid=(halo // BLK,),
            in_specs=[
                q_spec,
                whole(left.shape),
                pl.BlockSpec((1, BLK), col),
                q_spec,
                pl.BlockSpec((8, BLK), col),
                q_spec,
            ],
            out_specs=[q_spec, whole(left.shape)],
            scratch_shapes=[pltpu.VMEM((feat, halo), f32)] * 2,
        ),
        out_shape=[shaped((feat, halo), f32), shaped(left.shape, bf16)],
        compiler_params=params(),
        cost_estimate=cost(40 * feat * halo * 512, 20 * feat * halo, heads * halo * 512),
        name="attention_backward_left",
    )(first, q, left, lo, o, lse, do)


def backward_own(first, q, k, v, lo, o, lse, do, dq_part, halo):
    feat, tokens = q.shape
    heads = feat // HEAD_DIM
    col = lambda i, *_: (0, i)
    whole = lambda shape: pl.BlockSpec(shape, lambda i, *_: (0, 0))
    q_spec = pl.BlockSpec((feat, BLK), col)
    part_spec = pl.BlockSpec((feat, BLK), lambda i, *_: (0, jnp.minimum(i, halo // BLK - 1)))
    return pl.pallas_call(
        functools.partial(own_bwd_kernel, heads, halo),
        grid_spec=pltpu.PrefetchScalarGridSpec(
            num_scalar_prefetch=1,
            grid=(tokens // BLK,),
            in_specs=[
                q_spec,
                whole(k.shape),
                whole(v.shape),
                pl.BlockSpec((1, BLK), col),
                q_spec,
                pl.BlockSpec((8, BLK), col),
                q_spec,
                part_spec,
            ],
            out_specs=[q_spec, whole(k.shape), whole(v.shape)],
        ),
        out_shape=[shaped((feat, tokens), f32)] * 3,
        compiler_params=params(),
        cost_estimate=cost(40 * feat * tokens * 1024, 20 * feat * tokens, heads * tokens * 1024),
        name="attention_backward_own",
    )(first, q, k, v, lo, o, lse, do, dq_part)


def keep_send_specs(rows, dim):
    keep = pl.BlockSpec((rows, dim), lambda s, *_: (jnp.minimum(s, 1), 0))
    send = pl.BlockSpec((rows, dim), lambda s, *_: (jnp.maximum(s - 2, 0), 0))
    return keep, send


def put_rows(keep_ref, send_ref, value):
    s = pl.program_id(0)

    @pl.when(s < 2)
    def _():
        keep_ref[...] = value

    @pl.when(s >= 2)
    def _():
        send_ref[...] = value


def put_chunks(chunk_ref, keep_ref, send_ref, value):
    parts = chunk_ref.shape[0] // 2
    size = keep_ref.shape[0] // parts
    for half, ref in enumerate((keep_ref, send_ref)):
        for n in range(parts):
            at = pl.ds(pl.multiple_of(chunk_ref[half * parts + n] * size, size), size)
            ref[n * size : (n + 1) * size, :] = value[at, :].astype(bf16)


def out_kernel(place_ref, o_ref, ff_ref, g_ref, w_ref, keep_ref, send_ref, do_ref):
    total = mm(o_ref[...], w_ref[...], 0, 0) + ff_ref[...].astype(f32)
    put_rows(keep_ref, send_ref, total.astype(bf16))
    do_ref[...] = mm(w_ref[...], g_ref[...], 1, 1).astype(bf16)


def branch_out(places, o, ff_out, g, wt):
    feat, tokens = o.shape
    dim = wt.shape[1]
    rows = tokens // 4
    keep, send = keep_send_specs(rows, dim)
    spec = pl.BlockSpec((rows, dim), lambda s, *_: (s, 0))
    placed = pl.BlockSpec((feat, rows), lambda s, place: (0, place[s]))
    return pl.pallas_call(
        out_kernel,
        grid_spec=pltpu.PrefetchScalarGridSpec(
            num_scalar_prefetch=1,
            grid=(4,),
            in_specs=[placed, spec, spec, pl.BlockSpec((feat, dim), lambda s, *_: (3, 0))],
            out_specs=[keep, send, placed],
        ),
        out_shape=[shaped((tokens // 2, dim), bf16)] * 2 + [shaped((feat, tokens), bf16)],
        compiler_params=params(),
        cost_estimate=cost(4 * feat * tokens * dim, 6 * tokens * dim),
        name="branch_out",
    )(places, o, ff_out, g, wt)


def input_grad_kernel(
    halo,
    place_ref,
    dq_ref,
    dk_ref,
    dv_ref,
    back_ref,
    x_ref,
    stats_ref,
    u2_ref,
    wt_ref,
    vec_ref,
    cos_ref,
    sin_ref,
    keep_ref,
    send_ref,
    grad_ref,
    small_ref,
    bias_ref,
    late,
):
    s = pl.program_id(0)
    feat, rows = dq_ref.shape
    tokens = late.shape[1]

    @pl.when(s == 0)
    def _():
        late[:, : tokens - halo] = jnp.zeros((2 * feat, tokens - halo), bf16)
        late[:, tokens - halo :] = back_ref[...]
        small_ref[...] = jnp.zeros_like(small_ref)
        bias_ref[...] = jnp.zeros_like(bias_ref)

    cols = pl.ds(pl.multiple_of(place_ref[s] * rows, rows), rows)
    cos_t, sin_t = cos_ref[...], -sin_ref[...]
    dq = turned(dq_ref[...], cos_t, sin_t)
    dk = turned(dk_ref[...] + late[:feat, cols].astype(f32), cos_t, sin_t)
    dv = dv_ref[...] + late[feat:, cols].astype(f32)
    grad = jnp.concatenate([dq, dk, dv], axis=0).astype(bf16)
    grad_ref[...] = grad
    bias_ref[...] += jnp.sum(grad.astype(f32), axis=1, keepdims=True)
    one_grad = mm(grad, wt_ref[: 3 * feat, :], 0, 0)
    put_rows(keep_ref, send_ref, (one_grad * vec_ref[2:3, :] + u2_ref[...].astype(f32)).astype(bf16))
    normed = normed_from(x_ref, stats_ref)
    small_ref[0:1, :] += jnp.sum(one_grad * normed, axis=0, keepdims=True)
    small_ref[1:2, :] += jnp.sum(one_grad, axis=0, keepdims=True)


def input_gradient(places, dq, dk, dv, back, x, stats, u2, wt, vec, cos_t, sin_t, halo):
    feat, tokens = dq.shape
    dim = x.shape[1]
    rows = tokens // 4
    spec = pl.BlockSpec((rows, dim), lambda s, *_: (s, 0))
    placed = lambda r: pl.BlockSpec((r, rows), lambda s, place: (0, place[s]))
    whole = lambda shape: pl.BlockSpec(shape, lambda s, *_: (0, 0))
    keep, send = keep_send_specs(rows, dim)
    return pl.pallas_call(
        functools.partial(input_grad_kernel, halo),
        grid_spec=pltpu.PrefetchScalarGridSpec(
            num_scalar_prefetch=1,
            grid=(4,),
            in_specs=[placed(feat)] * 3
            + [whole(back.shape), spec, pl.BlockSpec((rows, 128), lambda s, *_: (s, 0)), spec, whole(wt.shape)]
            + [whole(vec.shape)]
            + [placed(ROT // 2)] * 2,
            out_specs=[keep, send, placed(3 * feat), whole((8, dim)), whole((3 * feat, 1))],
            scratch_shapes=[pltpu.VMEM((2 * feat, tokens), bf16)],
        ),
        out_shape=[shaped((tokens // 2, dim), bf16)] * 2
        + [shaped((3 * feat, tokens), bf16), shaped((8, dim), f32), shaped((3 * feat, 1), f32)],
        compiler_params=params(),
        cost_estimate=cost(12 * feat * tokens * dim, 10 * tokens * dim),
        name="input_gradient",
    )(places, dq, dk, dv, back, x, stats, u2, wt, vec, cos_t, sin_t)


def weight_grad_kernel(own_dims, place_ref, chunk_ref, grad_ref, normed_ref, *refs):
    more_refs, (wkeep_ref, wsend_ref, acc, acc_t) = refs[:-4], refs[-4:]
    s = pl.program_id(0)

    @pl.when(s == 0)
    def _():
        acc[...] = jnp.zeros_like(acc)

    width = grad_ref.shape[0]
    base = 2 * width
    acc[:width, :] += mm(grad_ref[...], normed_ref[...], 1, 0)
    if more_refs:
        o_ref, g_ref, one_ref, ff_ref, bias_ref = more_refs
        acc[width:base, :] += mm(o_ref[...], g_ref[...], 1, 0)

    @pl.when(s == pl.num_programs(0) - 1)
    def _():
        if more_refs:
            acc[base : base + 2, :] = one_ref[0:2, :]
            acc[base + 2 : base + 6, :] = ff_ref[0:4, :]
        acc_t[...] = acc[...].T
        if more_refs:
            columns = acc_t[:, base:]
            lane = lax.broadcasted_iota(jnp.int32, (own_dims, 128), 1)
            shared = jnp.zeros((own_dims, 128), f32)
            count = columns.shape[0] // own_dims
            for n in range(count):
                part = columns[n * own_dims : (n + 1) * own_dims, 5:6]
                shared = jnp.where(lane == 8 + n, part, shared)
            for n in range(bias_ref.shape[0] // own_dims):
                part = bias_ref[n * own_dims : (n + 1) * own_dims, 0:1]
                shared = jnp.where(lane == 8 + count + n, part, shared)
            lane = lax.broadcasted_iota(jnp.int32, columns.shape, 1)
            acc_t[:, base:] = jnp.where(lane < 5, columns, jnp.concatenate([shared] * count, axis=0))
        put_chunks(chunk_ref, wkeep_ref, wsend_ref, acc_t)


def weight_gradient(places, chunks, grad, normed, width, part, own_dims, o=None, g=None, small=()):
    tokens = grad.shape[1]
    dim = normed.shape[1]
    rows = tokens // 4
    out_width = 2 * width + 128 if small else width
    column = lambda part: pl.BlockSpec((width, rows), lambda s, place, chunk: (part, place[s]))
    spec = pl.BlockSpec((rows, dim), lambda s, *_: (s, 0))
    more = (o, g, *small) if small else ()
    whole = lambda shape: pl.BlockSpec(shape, lambda s, *_: (0, 0))
    return pl.pallas_call(
        functools.partial(weight_grad_kernel, own_dims),
        grid_spec=pltpu.PrefetchScalarGridSpec(
            num_scalar_prefetch=2,
            grid=(4,),
            in_specs=[column(part), spec]
            + ([column(0), spec] if small else [])
            + [whole(a.shape) for a in small],
            out_specs=[whole((dim // 2, out_width))] * 2,
            scratch_shapes=[pltpu.VMEM((out_width, dim), f32), pltpu.VMEM((dim, out_width), f32)],
        ),
        out_shape=[shaped((dim // 2, out_width), bf16)] * 2,
        compiler_params=params(),
        cost_estimate=cost(4 * width * tokens * dim, 4 * tokens * dim),
        name="weight_gradient",
    )(places, chunks, grad, normed, *more)


def norm_back_kernel(own_ref, came_ref, far_ref, x_ref, stats_ref, g_ref, out_ref):
    both = own_ref[...].astype(f32) + came_ref[...].astype(f32) + far_ref[...].astype(f32)
    normed = normed_from(x_ref, stats_ref)
    inv_std = stats_ref[:, 1:2]
    grad = both - jnp.mean(both, axis=-1, keepdims=True)
    grad = grad - normed * jnp.mean(both * normed, axis=-1, keepdims=True)
    out_ref[...] = (g_ref[...].astype(f32) + inv_std * grad).astype(bf16)


def norm_back(own, came, far, x, stats, g):
    count, dim = x.shape
    rows = count // 2
    spec = pl.BlockSpec((rows, dim), lambda s: (s, 0))
    return pl.pallas_call(
        norm_back_kernel,
        grid=(2,),
        in_specs=[spec, spec, spec, spec, pl.BlockSpec((rows, 128), lambda s: (s, 0)), spec],
        out_specs=spec,
        out_shape=shaped((count, dim), bf16),
        compiler_params=params(),
        cost_estimate=cost(20 * count * dim, 12 * count * dim),
        name="norm_back",
    )(own, came, far, x, stats, g)


def rope_tables(positions):
    freq_idx = jnp.arange(0, ROT, 2, dtype=f32)
    inverse = rope_base ** (-freq_idx / ROT)
    angles = inverse[:, None] * positions.astype(f32)[None, :]
    return jnp.cos(angles), jnp.sin(angles)


def late_chunks():
    n = lax.axis_size("dp")
    rank = lax.axis_index("dp")
    if n > 8:
        return jnp.arange(2, dtype=jnp.int32)
    mine = jnp.stack([rank ^ (2 * k) for k in range(n // 2)])
    return jnp.concatenate([mine, mine ^ 1]).astype(jnp.int32)


def late_sent(keep, send):
    n = lax.axis_size("dp")
    if n > 8:
        whole = jnp.concatenate([keep, send], axis=0)
        return None, lax.psum_scatter(whole, "dp", scatter_dimension=0, tiled=True).astype(f32)
    return keep, swapped(send, "dp", 1)


def late_sum(keep, came):
    return came if keep is None else keep.astype(f32) + came.astype(f32)


def late_near(keep, send):
    return late_sum(*late_sent(keep, send))


def late_far(total, dtype):
    n = lax.axis_size("dp")
    if n > 8:
        return total
    size = total.shape[0] * 2 // n
    low = total.astype(dtype)
    own = total[:size]
    for k in range(1, n // 2):
        own = own + swapped(low[k * size : (k + 1) * size], "dp", 2 * k).astype(f32)
    return own


def body(
    hidden_in,
    w_qkv,
    b_qkv,
    w_out,
    b_out,
    w_fc,
    b_fc,
    w_fc2,
    b_fc2,
    ln1_gain,
    ln1_bias,
    ln2_gain,
    ln2_bias,
    segment_ids,
    positions,
    cotangent,
):
    local_dim = w_qkv.shape[2]
    ff = w_fc.shape[1]
    own_dims = w_fc.shape[0]
    seq_len = positions.shape[0]
    halo = seq_len * 3 // 8
    qkv_dim = 3 * local_dim
    rank = lax.axis_index("tensor")
    places = jnp.stack([rank ^ at for at in SLOTS]).astype(jnp.int32)

    vectors = jnp.stack([b_out, b_fc2, ln1_gain, ln1_bias, ln2_gain, ln2_bias], axis=1)
    vectors = jnp.pad(vectors, ((0, 0), (0, 122)))
    block = jnp.concatenate(
        [
            jnp.transpose(w_qkv, (1, 0, 2)).reshape(own_dims, qkv_dim),
            w_out.T,
            vectors,
        ],
        axis=1,
    )
    x_far, g_far = swapped(hidden_in, "tensor", 2), swapped(cotangent, "tensor", 2)
    x_near, g_near = swapped(hidden_in, "tensor", 1), swapped(cotangent, "tensor", 1)
    pieces, starts, x_far = ring_gather(block, "dp", x_far)
    ff_w = lax.all_gather(jnp.concatenate([w_fc, w_fc2.T], axis=1), "dp", axis=0, tiled=True)
    x_blocks = gather_rows(hidden_in, x_near, x_far)

    cos_t, sin_t = rope_tables(positions)
    lo = halo + jnp.arange(seq_len, dtype=jnp.int32) - positions
    first = lo[::BLK] // BLK
    lo_row = lo.reshape(1, seq_len)

    q, k, v, right, x_all, normed_one, stats, wt, vec = project(
        starts,
        places,
        x_blocks,
        b_qkv.astype(f32).reshape(qkv_dim, 1),
        cos_t,
        sin_t,
        pieces,
        0,
        local_dim,
        halo,
    )
    right, g_far = tied(right, g_far)
    left = passed_along(right, "dp", 1)
    g_blocks = gather_rows(cotangent, g_near, g_far)
    ff_out, u_two, g_all, ff_grads, ff_small = feed_forward(
        x_all, g_blocks, stats, b_fc.astype(f32).reshape(1, ff), vec, ff_w, ff
    )
    ff_sum = lax.psum_scatter(ff_grads, "dp", scatter_dimension=0, tiled=True)
    q, ff_out = tied(q, ff_out)

    o, lse = attention_forward(first, q, k, v, left, lo_row, halo)
    chunks = late_chunks()
    out_keep, out_send, do = branch_out(places, o, ff_out, g_all, wt)
    own_o, came_o, other_o = scatter_near(out_keep, out_send)
    dq_part, back = backward_left(first, q, left, lo_row, o, lse, do, halo)
    dq_part, back, other_o = tied(dq_part, back, other_o)
    far_o = swapped(other_o, "tensor", 2)
    back = passed_along(back, "dp", -1)
    dq, dk, dv = backward_own(first, q, k, v, lo_row, o, lse, do, dq_part, halo)
    back, dq, far_o = tied(back, dq, far_o)
    count = hidden_in.shape[0]
    summed = own_o[:count].astype(f32) + came_o[:count].astype(f32) + far_o.astype(f32)
    layer_out = (hidden_in.astype(f32) + summed + vec[0] + vec[1]).astype(bf16)

    u_keep, u_send, proj_grad, one_small, qkv_bias = input_gradient(
        places, dq, dk, dv, back, x_all, stats, u_two, wt, vec, cos_t, sin_t, halo
    )
    own_u, came_u, other_u = scatter_near(u_keep, u_send)
    proj_grad, ff_sum = tied(proj_grad, ff_sum)
    keep_a, send_a = weight_gradient(places, chunks, proj_grad, normed_one, 2 * local_dim, 0, own_dims)
    proj_grad, other_u, send_a = tied(proj_grad, other_u, send_a)
    keep_a, came_a = late_sent(keep_a, send_a)
    keep_b, send_b = weight_gradient(
        places,
        chunks,
        proj_grad,
        normed_one,
        local_dim,
        2,
        own_dims,
        o,
        g_all,
        (one_small, ff_small, qkv_bias),
    )
    send_b, came_a = tied(send_b, came_a)
    near_a = late_sum(keep_a, came_a)
    near_b = late_near(keep_b, send_b)
    far_u = swapped(other_u, "tensor", 2)
    late_a, far_u = tied(late_far(near_a, bf16), far_u)
    late_b = late_far(near_b, bf16)
    late_own = jnp.concatenate([late_a, late_b[:, :local_dim]], axis=1)

    input_grad = norm_back(own_u, came_u, far_u, hidden_in, stats, cotangent)
    late_b, ff_sum, input_grad = tied(late_b, ff_sum, input_grad)
    ff_own = ff_sum.astype(f32)
    vectors = late_b[:, 2 * local_dim :]
    norm_grads = summed_over(vectors, "tensor")[:, :4].T
    fc_count = ff // own_dims
    fc_b_total = vectors[:, 8 : 8 + fc_count].T.reshape(ff)
    qkv_b_total = vectors[:, 8 + fc_count : 8 + fc_count + qkv_dim // own_dims].T.reshape(3, local_dim)
    out_b_total = vectors[:, 4]

    return (
        layer_out,
        input_grad,
        jnp.transpose(late_own.reshape(own_dims, 3, local_dim), (1, 0, 2)),
        qkv_b_total,
        late_b[:, local_dim : 2 * local_dim].T,
        out_b_total,
        ff_own[:, :ff],
        fc_b_total,
        ff_own[:, ff:].T,
        out_b_total,
        norm_grads[0],
        norm_grads[1],
        norm_grads[2],
        norm_grads[3],
    )


def solution(mesh):
    in_specs = (
        P(("dp", "tensor"), None),
        P(None, "dp", "tensor"),
        P(None, "tensor"),
        P("tensor", "dp"),
        P("dp"),
        P("dp", "tensor"),
        P("tensor"),
        P("tensor", "dp"),
        P("dp"),
        P("dp"),
        P("dp"),
        P("dp"),
        P("dp"),
        P("dp"),
        P("dp"),
        P(("dp", "tensor"), None),
    )
    out_specs = (
        P(("dp", "tensor"), None),
        P(("dp", "tensor"), None),
        P(None, "dp", "tensor"),
        P(None, "tensor"),
        P("tensor", "dp"),
        P("dp"),
        P("dp", "tensor"),
        P("tensor"),
        P("tensor", "dp"),
        P("dp"),
        P("dp"),
        P("dp"),
        P("dp"),
        P("dp"),
    )
    return jax.shard_map(body, mesh=mesh, in_specs=in_specs, out_specs=out_specs, check_vma=False)
```

```python
import functools

import jax
import jax.numpy as jnp
from jax import lax
from jax.experimental import pallas as pl
from jax.experimental.pallas import tpu as pltpu
from jax.sharding import PartitionSpec as P

HEAD_DIM = 64
ROT = 16
BLK = 256
SLOTS = (0, 2, 1, 3)

norm_eps = 1e-05
big_negative = -1e30
rope_base = 10000.0
inv_sqrt_two = 0.7071067811865476
inv_sqrt_two_pi = 0.3989422804014327

f32 = jnp.float32
bf16 = jnp.bfloat16


def mm(a, b, ca, cb):
    return lax.dot_general(a, b, (((ca,), (cb,)), ((), ())), preferred_element_type=f32)


def params(**kw):
    return pltpu.CompilerParams(vmem_limit_bytes=56 * 1024 * 1024, **kw)


def cost(flops, moved, exps=0):
    return pl.CostEstimate(flops=int(flops) // 16, bytes_accessed=int(moved) // 16, transcendentals=int(exps) // 16)


def shaped(shape, dtype):
    return jax.ShapeDtypeStruct(shape, dtype)


def passed_along(block, axis, distance):
    devices = range(lax.axis_size(axis))
    route = [(i - distance, i) for i in devices if i - distance in devices]
    return lax.ppermute(block, axis, route)


def swapped(block, axis, bit):
    route = [(i, i ^ bit) for i in range(lax.axis_size(axis))]
    return lax.ppermute(block, axis, route)


def ring_order(n):
    return list(range(0, n, 2)) + list(range(n - 1, 0, -2))


def ring_gather(block, axis, early):
    n = lax.axis_size(axis)
    rows = block.shape[0]
    if n > 8:
        return [lax.all_gather(block, axis, axis=0, tiled=True)], jnp.zeros((1,), jnp.int32), early
    ring = ring_order(n)
    ahead = [(ring[r], ring[(r + 1) % n]) for r in range(n)]
    behind = [(b, a) for a, b in ahead]
    table = []
    for device in range(n):
        at = ring.index(device)
        row = [device * rows]
        for step in range(1, n // 2):
            row.append(ring[(at - step) % n] * rows)
            row.append(ring[(at + step) % n] * rows)
        row.append(ring[(at + n // 2) % n] * rows)
        table.append(row)
    pieces = [block]
    from_left = from_right = block
    for step in range(1, n // 2):
        from_left = lax.ppermute(from_left, axis, ahead)
        from_right = lax.ppermute(from_right, axis, behind)
        if step == n // 2 - 1:
            from_left, from_right, early = tied(from_left, from_right, early)
        else:
            from_left, from_right = tied(from_left, from_right)
        pieces += [from_left, from_right]
    pieces.append(lax.ppermute(from_left, axis, ahead))
    return pieces, jnp.asarray(table, jnp.int32)[lax.axis_index(axis)], early


def gather_rows(block, near, far):
    return [block, far, near, swapped(far, "tensor", 1)]


def scatter_near(keep, send):
    count = keep.shape[0] // 2
    came = swapped(send, "tensor", 1)
    other = (keep[count:].astype(f32) + came[count:].astype(f32)).astype(bf16)
    return keep, came, other


def tied(*arrays):
    return lax.optimization_barrier(arrays)


def summed_over(vec, axis):
    n = lax.axis_size(axis)
    bit = 1
    while bit < n:
        vec = vec + swapped(vec, axis, bit)
        bit *= 2
    return vec


def assemble(piece_refs, start_ref, first, out_ref):
    columns = pl.ds(first, out_ref.shape[1])
    for n, ref in enumerate(piece_refs):
        rows = ref.shape[0]
        out_ref[pl.ds(pl.multiple_of(start_ref[n], rows), rows), :] = ref[:, columns]


def take_rows(block_refs, out_ref):
    for n, ref in enumerate(block_refs):

        @pl.when(pl.program_id(0) == n)
        def _():
            out_ref[...] = ref[...]


def row_stats(x):
    mean = jnp.mean(x, axis=-1, keepdims=True)
    center = x - mean
    return mean, lax.rsqrt(jnp.mean(center * center, axis=-1, keepdims=True) + norm_eps)


def normed_from(x_ref, stats_ref):
    return (x_ref[...].astype(f32) - stats_ref[:, 0:1]) * stats_ref[:, 1:2]


def ff_kernel(x_ref, stats_ref, b_ref, vec_ref, w_ref, *refs):
    g_refs, (out_ref, u_ref, g_ref, grads_ref, small_ref, fc_acc, fc2_acc) = refs[:4], refs[4:]
    take_rows(g_refs, g_ref)
    step = pl.program_id(0)
    ff = fc_acc.shape[1]
    fc_w, fc2_w = w_ref.at[:, :ff], w_ref.at[:, ff:]

    @pl.when(step == 0)
    def _():
        fc_acc[...] = jnp.zeros_like(fc_acc)
        fc2_acc[...] = jnp.zeros_like(fc2_acc)
        small_ref[...] = jnp.zeros_like(small_ref)

    gain, shift = vec_ref[4:5, :], vec_ref[5:6, :]
    normed = normed_from(x_ref, stats_ref)
    normed_two = (normed * gain + shift).astype(bf16)
    pre = mm(normed_two, fc_w[...], 1, 0) + b_ref[...]
    cdf = 0.5 + 0.5 * lax.erf(pre * inv_sqrt_two)
    act = (pre * cdf).astype(bf16)
    slope = cdf + pre * (jnp.exp(-0.5 * pre * pre) * inv_sqrt_two_pi)
    out_ref[...] = mm(act, fc2_w[...], 1, 1).astype(bf16)
    g = g_ref[...]
    pre_grad = (mm(g, fc2_w[...], 1, 0) * slope).astype(bf16)
    two_grad = mm(pre_grad, fc_w[...], 1, 1)
    u_ref[...] = (two_grad * gain).astype(bf16)
    fc_acc[...] += mm(normed_two, pre_grad, 0, 0)
    fc2_acc[...] += mm(g, act, 0, 0)
    small_ref[0:1, :] += jnp.sum(two_grad * normed, axis=0, keepdims=True)
    small_ref[1:2, :] += jnp.sum(two_grad, axis=0, keepdims=True)
    small_ref[2:3, :] += jnp.sum(g.astype(f32), axis=0, keepdims=True)
    small_ref[3:4, :] += jnp.sum(pre_grad.astype(f32), axis=0, keepdims=True)

    @pl.when(step == pl.num_programs(0) - 1)
    def _():
        grads_ref[:, :ff] = fc_acc[...].astype(bf16)
        grads_ref[:, ff:] = fc2_acc[...].astype(bf16)


def feed_forward(x, g, stats, b_fc, vec, w, ff):
    tokens, dim = x.shape
    rows = tokens // 4
    spec = pl.BlockSpec((rows, dim), lambda s, *_: (s, 0))
    whole = lambda shape: pl.BlockSpec(shape, lambda s, *_: (0, 0))
    return pl.pallas_call(
        ff_kernel,
        grid_spec=pltpu.PrefetchScalarGridSpec(
            num_scalar_prefetch=0,
            grid=(4,),
            in_specs=[
                spec,
                pl.BlockSpec((rows, 128), lambda s, *_: (s, 0)),
                whole((1, ff)),
                whole(vec.shape),
                whole(w.shape),
            ]
            + [whole(p.shape) for p in g],
            out_specs=[spec, spec, spec, whole((dim, 2 * ff)), whole((8, dim))],
            scratch_shapes=[pltpu.VMEM((dim, ff), f32)] * 2,
        ),
        out_shape=[
            shaped((tokens, dim), bf16),
            shaped((tokens, dim), bf16),
            shaped((tokens, dim), bf16),
            shaped((dim, 2 * ff), bf16),
            shaped((8, dim), f32),
        ],
        compiler_params=params(),
        cost_estimate=cost(12 * tokens * dim * ff, 8 * tokens * dim + 8 * dim * ff, 2 * tokens * ff),
        name="feed_forward",
    )(x, stats, b_fc, vec, w, *g)


def turned(x, cos_t, sin_t):
    half = ROT // 2
    out = []
    for h in range(x.shape[0] // HEAD_DIM):
        a = x[h * HEAD_DIM : h * HEAD_DIM + half]
        b = x[h * HEAD_DIM + half : h * HEAD_DIM + ROT]
        out += [a * cos_t - b * sin_t, b * cos_t + a * sin_t, x[h * HEAD_DIM + ROT : (h + 1) * HEAD_DIM]]
    return jnp.concatenate(out, axis=0)


def project_kernel(pieces, first, start_ref, place_ref, b_ref, cos_ref, sin_ref, *refs):
    x_refs, w_refs = refs[:4], refs[4 : 4 + pieces]
    (q_ref, k_ref, v_ref, halo_ref, x_ref, normed_ref, stats_ref, wt_ref, vec_ref, packed) = refs[4 + pieces :]
    take_rows(x_refs, x_ref)
    feat = q_ref.shape[0]
    width = wt_ref.shape[0]

    @pl.when(pl.program_id(0) == 0)
    def _():
        assemble(w_refs, start_ref, first, packed)
        wt_ref[...] = packed[:, :width].astype(f32).T.astype(bf16)
        vec_ref[...] = packed[:, width:].astype(f32).T[:8]

    x = x_ref[...].astype(f32)
    mean, inv_std = row_stats(x)
    lane = lax.broadcasted_iota(jnp.int32, stats_ref.shape, 1)
    stats_ref[...] = jnp.where(lane == 0, mean, inv_std)
    normed_one = ((x - mean) * inv_std * vec_ref[2:3, :] + vec_ref[3:4, :]).astype(bf16)
    normed_ref[...] = normed_one
    proj = mm(wt_ref[: 3 * feat, :], normed_one, 1, 1) + b_ref[...]
    cos_t, sin_t = cos_ref[...], sin_ref[...]
    q_ref[...] = (turned(proj[:feat], cos_t, sin_t) * HEAD_DIM ** (-0.5)).astype(bf16)
    k_ref[...] = turned(proj[feat : 2 * feat], cos_t, sin_t).astype(bf16)
    v_ref[...] = proj[2 * feat :].astype(bf16)
    rows = k_ref.shape[1]
    halo = halo_ref.shape[1]
    place = place_ref[pl.program_id(0)]
    for n in range(4):
        begin = max(0, 4 * rows - halo - n * rows)
        if begin < rows:
            to = n * rows + begin - (4 * rows - halo)

            @pl.when(place == n)
            def _():
                halo_ref[:feat, to : to + rows - begin] = k_ref[:, begin:]
                halo_ref[feat:, to : to + rows - begin] = v_ref[:, begin:]


def project(starts, places, x, b_col, cos_t, sin_t, pieces, first, feat, halo):
    rows, dim = x[0].shape
    tokens = 4 * rows
    width = 4 * feat
    spec = pl.BlockSpec((rows, dim), lambda s, *_: (s, 0))
    placed = lambda r: pl.BlockSpec((r, rows), lambda s, start, place: (0, place[s]))
    whole = lambda shape: pl.BlockSpec(shape, lambda s, *_: (0, 0))
    return pl.pallas_call(
        functools.partial(project_kernel, len(pieces), first),
        grid_spec=pltpu.PrefetchScalarGridSpec(
            num_scalar_prefetch=2,
            grid=(4,),
            in_specs=[whole(b_col.shape), placed(ROT // 2), placed(ROT // 2)]
            + [whole(p.shape) for p in x + pieces],
            out_specs=[placed(feat)] * 3
            + [
                whole((2 * feat, halo)),
                spec,
                spec,
                pl.BlockSpec((rows, 128), lambda s, *_: (s, 0)),
                whole((width, dim)),
                whole((8, dim)),
            ],
            scratch_shapes=[pltpu.VMEM((dim, width + 128), bf16)],
        ),
        out_shape=[shaped((feat, tokens), bf16)] * 3
        + [
            shaped((2 * feat, halo), bf16),
            shaped((tokens, dim), bf16),
            shaped((tokens, dim), bf16),
            shaped((tokens, 128), f32),
            shaped((width, dim), bf16),
            shaped((8, dim), f32),
        ],
        compiler_params=params(),
        cost_estimate=cost(6 * tokens * dim * feat, 6 * tokens * dim + 4 * dim * width),
        name="project",
    )(starts, places, b_col, cos_t, sin_t, *x, *pieces)


def key_mask(chunk, lo_row, hi_row):
    idx = chunk * BLK + lax.broadcasted_iota(jnp.int32, (BLK, BLK), 0)
    return jnp.where((idx >= lo_row) & (idx <= hi_row), 0.0, big_negative)


def over_chunks(begin, end, step, carry):
    pairs = (end - begin) // 2
    carry = lax.fori_loop(0, pairs, lambda n, c: step([begin + 2 * n, begin + 2 * n + 1], c), carry)
    return lax.fori_loop(begin + 2 * pairs, end, lambda n, c: step([n], c), carry)


def attn_fwd_kernel(heads, halo, first_ref, q_ref, k_ref, v_ref, left_ref, lo_ref, o_ref, lse_ref, keys, values):
    i = pl.program_id(0)
    first = first_ref[i]
    last = i + halo // BLK
    feat = k_ref.shape[0]

    @pl.when(i == 0)
    def _():
        keys[:, :halo] = left_ref[:feat, :]
        keys[:, halo:] = k_ref[...]
        values[:, :halo] = left_ref[feat:, :]
        values[:, halo:] = v_ref[...]

    lo_row = lo_ref[...]
    hi_row = halo + i * BLK + lax.broadcasted_iota(jnp.int32, (1, BLK), 1)

    def step(chunks, carry):
        hs, js = range(heads), range(len(chunks))
        feats = [pl.ds(h * HEAD_DIM, HEAD_DIM) for h in hs]
        cols = [pl.ds(pl.multiple_of(c * BLK, BLK), BLK) for c in chunks]
        mask = [key_mask(c, lo_row, hi_row) for c in chunks]
        s = [[mm(keys[feats[h], cols[j]], q_ref[feats[h], :], 0, 0) + mask[j] for j in js] for h in hs]
        tops = [carry[h][0] for h in hs]
        for j in js:
            tops = [jnp.maximum(tops[h], jnp.max(s[h][j], axis=0, keepdims=True)) for h in hs]
        p = [[jnp.exp(s[h][j] - tops[h]) for j in js] for h in hs]
        pv = [[mm(values[feats[h], cols[j]], p[h][j].astype(bf16), 1, 0) for j in js] for h in hs]
        kept = [jnp.exp(carry[h][0] - tops[h]) for h in hs]
        return tuple(
            (
                tops[h],
                carry[h][1] * kept[h] + sum(jnp.sum(p[h][j], axis=0, keepdims=True) for j in js),
                carry[h][2] * kept[h] + sum(pv[h]),
            )
            for h in hs
        )

    start = tuple(
        (
            jnp.full((1, BLK), big_negative, f32),
            jnp.zeros((1, BLK), f32),
            jnp.zeros((HEAD_DIM, BLK), f32),
        )
        for _ in range(heads)
    )
    done = over_chunks(first, last + 1, step, start)
    for h in range(heads):
        top, total, acc = done[h]
        o_ref[pl.ds(h * HEAD_DIM, HEAD_DIM), :] = (acc / total).astype(bf16)
        lse_ref[pl.ds(h, 1), :] = top + jnp.log(total)


def attention_forward(first, q, k, v, left, lo, halo):
    feat, tokens = q.shape
    heads = feat // HEAD_DIM
    col = lambda i, *_: (0, i)
    whole = lambda shape: pl.BlockSpec(shape, lambda i, *_: (0, 0))
    q_spec = pl.BlockSpec((feat, BLK), col)
    return pl.pallas_call(
        functools.partial(attn_fwd_kernel, heads, halo),
        grid_spec=pltpu.PrefetchScalarGridSpec(
            num_scalar_prefetch=1,
            grid=(tokens // BLK,),
            in_specs=[q_spec, whole(k.shape), whole(v.shape), whole(left.shape), pl.BlockSpec((1, BLK), col)],
            out_specs=[q_spec, pl.BlockSpec((8, BLK), col)],
            scratch_shapes=[pltpu.VMEM((feat, halo + tokens), bf16)] * 2,
        ),
        out_shape=[shaped((feat, tokens), bf16), shaped((8, tokens), f32)],
        compiler_params=params(),
        cost_estimate=cost(16 * feat * tokens * 1024, 8 * feat * tokens, heads * tokens * 1024),
        name="attention_forward",
    )(first, q, k, v, left, lo)


def attn_bwd_step(
    heads, chunks, base, q_ref, k_ref, v_ref, do_ref, lse_ref, lo_row, hi_row, deltas, dq_ref, dk_ref, dv_ref
):
    hs, js = range(heads), range(len(chunks))
    feats = [pl.ds(h * HEAD_DIM, HEAD_DIM) for h in hs]
    cols = [pl.ds(pl.multiple_of((c - base) * BLK, BLK), BLK) for c in chunks]
    mask = [key_mask(c, lo_row, hi_row) for c in chunks]
    both = [(h, j) for h in hs for j in js]
    s = [mm(k_ref[feats[h], cols[j]], q_ref[feats[h], :], 0, 0) + mask[j] for h, j in both]
    dp = [mm(v_ref[feats[h], cols[j]], do_ref[feats[h], :], 0, 0) for h, j in both]
    p = [jnp.exp(s[n] - lse_ref[pl.ds(h, 1), :]) for n, (h, j) in enumerate(both)]
    ds = [(p[n] * (dp[n] - deltas[h])).astype(bf16) for n, (h, j) in enumerate(both)]
    dv = [mm(do_ref[feats[h], :], p[n].astype(bf16), 1, 1) for n, (h, j) in enumerate(both)]
    dk = [mm(q_ref[feats[h], :], ds[n], 1, 1) for n, (h, j) in enumerate(both)]
    dq = [mm(k_ref[feats[h], cols[j]], ds[n], 1, 0) for n, (h, j) in enumerate(both)]
    for n, (h, j) in enumerate(both):
        dv_ref[feats[h], cols[j]] += dv[n]
        dk_ref[feats[h], cols[j]] += dk[n]
    for h in hs:
        dq_ref[feats[h], :] += sum(dq[n] for n, (at, j) in enumerate(both) if at == h)


def row_deltas(heads, o_ref, do_ref):
    deltas = []
    for h in range(heads):
        feats = pl.ds(h * HEAD_DIM, HEAD_DIM)
        prod = do_ref[feats, :].astype(f32) * o_ref[feats, :].astype(f32)
        deltas.append(jnp.sum(prod, axis=0, keepdims=True))
    return deltas


def halo_bwd_kernel(heads, halo, first_ref, q_ref, left_ref, lo_ref, o_ref, lse_ref, do_ref, dq_ref, back_ref, dk, dv):
    i = pl.program_id(0)
    feat = q_ref.shape[0]

    @pl.when(i == 0)
    def _():
        dk[...] = jnp.zeros_like(dk)
        dv[...] = jnp.zeros_like(dv)

    lo_row = lo_ref[...]
    hi_row = jnp.full((1, BLK), halo, jnp.int32)
    dq_ref[...] = jnp.zeros_like(dq_ref)
    deltas = row_deltas(heads, o_ref, do_ref)
    k_ref, v_ref = left_ref.at[:feat, :], left_ref.at[feat:, :]

    def step(c, carry):
        attn_bwd_step(
            heads, c, 0, q_ref, k_ref, v_ref, do_ref, lse_ref, lo_row, hi_row, deltas, dq_ref, dk, dv
        )
        return carry

    over_chunks(jnp.minimum(first_ref[i], halo // BLK), halo // BLK, step, 0)

    @pl.when(i == pl.num_programs(0) - 1)
    def _():
        back_ref[:feat, :] = dk[...].astype(bf16)
        back_ref[feat:, :] = dv[...].astype(bf16)


def own_bwd_kernel(
    heads, halo, first_ref, q_ref, k_ref, v_ref, lo_ref, o_ref, lse_ref, do_ref, part_ref, dq_ref, dk_ref, dv_ref
):
    i = pl.program_id(0)
    base = halo // BLK

    @pl.when(i == 0)
    def _():
        dk_ref[...] = jnp.zeros_like(dk_ref)
        dv_ref[...] = jnp.zeros_like(dv_ref)

    @pl.when(i < base)
    def _():
        dq_ref[...] = part_ref[...]

    @pl.when(i >= base)
    def _():
        dq_ref[...] = jnp.zeros_like(dq_ref)

    lo_row = lo_ref[...]
    hi_row = halo + i * BLK + lax.broadcasted_iota(jnp.int32, (1, BLK), 1)
    deltas = row_deltas(heads, o_ref, do_ref)

    def step(c, carry):
        attn_bwd_step(
            heads, c, base, q_ref, k_ref, v_ref, do_ref, lse_ref, lo_row, hi_row, deltas, dq_ref, dk_ref, dv_ref
        )
        return carry

    over_chunks(jnp.maximum(first_ref[i], base), i + base + 1, step, 0)
    dq_ref[...] = dq_ref[...] * HEAD_DIM ** (-0.5)


def backward_left(first, q, left, lo, o, lse, do, halo):
    feat, tokens = q.shape
    heads = feat // HEAD_DIM
    col = lambda i, *_: (0, i)
    whole = lambda shape: pl.BlockSpec(shape, lambda i, *_: (0, 0))
    q_spec = pl.BlockSpec((feat, BLK), col)
    return pl.pallas_call(
        functools.partial(halo_bwd_kernel, heads, halo),
        grid_spec=pltpu.PrefetchScalarGridSpec(
            num_scalar_prefetch=1,
            grid=(halo // BLK,),
            in_specs=[
                q_spec,
                whole(left.shape),
                pl.BlockSpec((1, BLK), col),
                q_spec,
                pl.BlockSpec((8, BLK), col),
                q_spec,
            ],
            out_specs=[q_spec, whole(left.shape)],
            scratch_shapes=[pltpu.VMEM((feat, halo), f32)] * 2,
        ),
        out_shape=[shaped((feat, halo), f32), shaped(left.shape, bf16)],
        compiler_params=params(),
        cost_estimate=cost(40 * feat * halo * 512, 20 * feat * halo, heads * halo * 512),
        name="attention_backward_left",
    )(first, q, left, lo, o, lse, do)


def backward_own(first, q, k, v, lo, o, lse, do, dq_part, halo):
    feat, tokens = q.shape
    heads = feat // HEAD_DIM
    col = lambda i, *_: (0, i)
    whole = lambda shape: pl.BlockSpec(shape, lambda i, *_: (0, 0))
    q_spec = pl.BlockSpec((feat, BLK), col)
    part_spec = pl.BlockSpec((feat, BLK), lambda i, *_: (0, jnp.minimum(i, halo // BLK - 1)))
    return pl.pallas_call(
        functools.partial(own_bwd_kernel, heads, halo),
        grid_spec=pltpu.PrefetchScalarGridSpec(
            num_scalar_prefetch=1,
            grid=(tokens // BLK,),
            in_specs=[
                q_spec,
                whole(k.shape),
                whole(v.shape),
                pl.BlockSpec((1, BLK), col),
                q_spec,
                pl.BlockSpec((8, BLK), col),
                q_spec,
                part_spec,
            ],
            out_specs=[q_spec, whole(k.shape), whole(v.shape)],
        ),
        out_shape=[shaped((feat, tokens), f32)] * 3,
        compiler_params=params(),
        cost_estimate=cost(40 * feat * tokens * 1024, 20 * feat * tokens, heads * tokens * 1024),
        name="attention_backward_own",
    )(first, q, k, v, lo, o, lse, do, dq_part)


def keep_send_specs(rows, dim):
    keep = pl.BlockSpec((rows, dim), lambda s, *_: (jnp.minimum(s, 1), 0))
    send = pl.BlockSpec((rows, dim), lambda s, *_: (jnp.maximum(s - 2, 0), 0))
    return keep, send


def put_rows(keep_ref, send_ref, value):
    s = pl.program_id(0)

    @pl.when(s < 2)
    def _():
        keep_ref[...] = value

    @pl.when(s >= 2)
    def _():
        send_ref[...] = value


def put_chunks(chunk_ref, keep_ref, send_ref, value):
    parts = chunk_ref.shape[0] // 2
    size = keep_ref.shape[0] // parts
    for half, ref in enumerate((keep_ref, send_ref)):
        for n in range(parts):
            at = pl.ds(pl.multiple_of(chunk_ref[half * parts + n] * size, size), size)
            ref[n * size : (n + 1) * size, :] = value[at, :].astype(bf16)


def out_kernel(place_ref, o_ref, ff_ref, g_ref, w_ref, keep_ref, send_ref, do_ref):
    total = mm(o_ref[...], w_ref[...], 0, 0) + ff_ref[...].astype(f32)
    put_rows(keep_ref, send_ref, total.astype(bf16))
    do_ref[...] = mm(w_ref[...], g_ref[...], 1, 1).astype(bf16)


def branch_out(places, o, ff_out, g, wt):
    feat, tokens = o.shape
    dim = wt.shape[1]
    rows = tokens // 4
    keep, send = keep_send_specs(rows, dim)
    spec = pl.BlockSpec((rows, dim), lambda s, *_: (s, 0))
    placed = pl.BlockSpec((feat, rows), lambda s, place: (0, place[s]))
    return pl.pallas_call(
        out_kernel,
        grid_spec=pltpu.PrefetchScalarGridSpec(
            num_scalar_prefetch=1,
            grid=(4,),
            in_specs=[placed, spec, spec, pl.BlockSpec((feat, dim), lambda s, *_: (3, 0))],
            out_specs=[keep, send, placed],
        ),
        out_shape=[shaped((tokens // 2, dim), bf16)] * 2 + [shaped((feat, tokens), bf16)],
        compiler_params=params(),
        cost_estimate=cost(4 * feat * tokens * dim, 6 * tokens * dim),
        name="branch_out",
    )(places, o, ff_out, g, wt)


def input_grad_kernel(
    halo,
    place_ref,
    dq_ref,
    dk_ref,
    dv_ref,
    back_ref,
    x_ref,
    stats_ref,
    u2_ref,
    wt_ref,
    vec_ref,
    cos_ref,
    sin_ref,
    keep_ref,
    send_ref,
    grad_ref,
    small_ref,
    bias_ref,
    late,
):
    s = pl.program_id(0)
    feat, rows = dq_ref.shape
    tokens = late.shape[1]

    @pl.when(s == 0)
    def _():
        late[:, : tokens - halo] = jnp.zeros((2 * feat, tokens - halo), bf16)
        late[:, tokens - halo :] = back_ref[...]
        small_ref[...] = jnp.zeros_like(small_ref)
        bias_ref[...] = jnp.zeros_like(bias_ref)

    cols = pl.ds(pl.multiple_of(place_ref[s] * rows, rows), rows)
    cos_t, sin_t = cos_ref[...], -sin_ref[...]
    dq = turned(dq_ref[...], cos_t, sin_t)
    dk = turned(dk_ref[...] + late[:feat, cols].astype(f32), cos_t, sin_t)
    dv = dv_ref[...] + late[feat:, cols].astype(f32)
    grad = jnp.concatenate([dq, dk, dv], axis=0).astype(bf16)
    grad_ref[...] = grad
    bias_ref[...] += jnp.sum(grad.astype(f32), axis=1, keepdims=True)
    one_grad = mm(grad, wt_ref[: 3 * feat, :], 0, 0)
    put_rows(keep_ref, send_ref, (one_grad * vec_ref[2:3, :] + u2_ref[...].astype(f32)).astype(bf16))
    normed = normed_from(x_ref, stats_ref)
    small_ref[0:1, :] += jnp.sum(one_grad * normed, axis=0, keepdims=True)
    small_ref[1:2, :] += jnp.sum(one_grad, axis=0, keepdims=True)


def input_gradient(places, dq, dk, dv, back, x, stats, u2, wt, vec, cos_t, sin_t, halo):
    feat, tokens = dq.shape
    dim = x.shape[1]
    rows = tokens // 4
    spec = pl.BlockSpec((rows, dim), lambda s, *_: (s, 0))
    placed = lambda r: pl.BlockSpec((r, rows), lambda s, place: (0, place[s]))
    whole = lambda shape: pl.BlockSpec(shape, lambda s, *_: (0, 0))
    keep, send = keep_send_specs(rows, dim)
    return pl.pallas_call(
        functools.partial(input_grad_kernel, halo),
        grid_spec=pltpu.PrefetchScalarGridSpec(
            num_scalar_prefetch=1,
            grid=(4,),
            in_specs=[placed(feat)] * 3
            + [whole(back.shape), spec, pl.BlockSpec((rows, 128), lambda s, *_: (s, 0)), spec, whole(wt.shape)]
            + [whole(vec.shape)]
            + [placed(ROT // 2)] * 2,
            out_specs=[keep, send, placed(3 * feat), whole((8, dim)), whole((3 * feat, 1))],
            scratch_shapes=[pltpu.VMEM((2 * feat, tokens), bf16)],
        ),
        out_shape=[shaped((tokens // 2, dim), bf16)] * 2
        + [shaped((3 * feat, tokens), bf16), shaped((8, dim), f32), shaped((3 * feat, 1), f32)],
        compiler_params=params(),
        cost_estimate=cost(12 * feat * tokens * dim, 10 * tokens * dim),
        name="input_gradient",
    )(places, dq, dk, dv, back, x, stats, u2, wt, vec, cos_t, sin_t)


def weight_grad_kernel(own_dims, place_ref, chunk_ref, grad_ref, normed_ref, *refs):
    more_refs, (wkeep_ref, wsend_ref, acc, acc_t) = refs[:-4], refs[-4:]
    s = pl.program_id(0)

    @pl.when(s == 0)
    def _():
        acc[...] = jnp.zeros_like(acc)

    width = grad_ref.shape[0]
    base = 2 * width
    acc[:width, :] += mm(grad_ref[...], normed_ref[...], 1, 0)
    if more_refs:
        o_ref, g_ref, one_ref, ff_ref, bias_ref = more_refs
        acc[width:base, :] += mm(o_ref[...], g_ref[...], 1, 0)

    @pl.when(s == pl.num_programs(0) - 1)
    def _():
        if more_refs:
            acc[base : base + 2, :] = one_ref[0:2, :]
            acc[base + 2 : base + 6, :] = ff_ref[0:4, :]
        acc_t[...] = acc[...].T
        if more_refs:
            columns = acc_t[:, base:]
            lane = lax.broadcasted_iota(jnp.int32, (own_dims, 128), 1)
            shared = jnp.zeros((own_dims, 128), f32)
            count = columns.shape[0] // own_dims
            for n in range(count):
                part = columns[n * own_dims : (n + 1) * own_dims, 5:6]
                shared = jnp.where(lane == 8 + n, part, shared)
            for n in range(bias_ref.shape[0] // own_dims):
                part = bias_ref[n * own_dims : (n + 1) * own_dims, 0:1]
                shared = jnp.where(lane == 8 + count + n, part, shared)
            lane = lax.broadcasted_iota(jnp.int32, columns.shape, 1)
            acc_t[:, base:] = jnp.where(lane < 5, columns, jnp.concatenate([shared] * count, axis=0))
        put_chunks(chunk_ref, wkeep_ref, wsend_ref, acc_t)


def weight_gradient(places, chunks, grad, normed, width, part, own_dims, o=None, g=None, small=()):
    tokens = grad.shape[1]
    dim = normed.shape[1]
    rows = tokens // 4
    out_width = 2 * width + 128 if small else width
    column = lambda part: pl.BlockSpec((width, rows), lambda s, place, chunk: (part, place[s]))
    spec = pl.BlockSpec((rows, dim), lambda s, *_: (s, 0))
    more = (o, g, *small) if small else ()
    whole = lambda shape: pl.BlockSpec(shape, lambda s, *_: (0, 0))
    return pl.pallas_call(
        functools.partial(weight_grad_kernel, own_dims),
        grid_spec=pltpu.PrefetchScalarGridSpec(
            num_scalar_prefetch=2,
            grid=(4,),
            in_specs=[column(part), spec]
            + ([column(0), spec] if small else [])
            + [whole(a.shape) for a in small],
            out_specs=[whole((dim // 2, out_width))] * 2,
            scratch_shapes=[pltpu.VMEM((out_width, dim), f32), pltpu.VMEM((dim, out_width), f32)],
        ),
        out_shape=[shaped((dim // 2, out_width), bf16)] * 2,
        compiler_params=params(),
        cost_estimate=cost(4 * width * tokens * dim, 4 * tokens * dim),
        name="weight_gradient",
    )(places, chunks, grad, normed, *more)


def norm_back_kernel(own_ref, came_ref, far_ref, x_ref, stats_ref, g_ref, out_ref):
    both = own_ref[...].astype(f32) + came_ref[...].astype(f32) + far_ref[...].astype(f32)
    normed = normed_from(x_ref, stats_ref)
    inv_std = stats_ref[:, 1:2]
    grad = both - jnp.mean(both, axis=-1, keepdims=True)
    grad = grad - normed * jnp.mean(both * normed, axis=-1, keepdims=True)
    out_ref[...] = (g_ref[...].astype(f32) + inv_std * grad).astype(bf16)


def norm_back(own, came, far, x, stats, g):
    count, dim = x.shape
    rows = count // 2
    spec = pl.BlockSpec((rows, dim), lambda s: (s, 0))
    return pl.pallas_call(
        norm_back_kernel,
        grid=(2,),
        in_specs=[spec, spec, spec, spec, pl.BlockSpec((rows, 128), lambda s: (s, 0)), spec],
        out_specs=spec,
        out_shape=shaped((count, dim), bf16),
        compiler_params=params(),
        cost_estimate=cost(20 * count * dim, 12 * count * dim),
        name="norm_back",
    )(own, came, far, x, stats, g)


def rope_tables(positions):
    freq_idx = jnp.arange(0, ROT, 2, dtype=f32)
    inverse = rope_base ** (-freq_idx / ROT)
    angles = inverse[:, None] * positions.astype(f32)[None, :]
    return jnp.cos(angles), jnp.sin(angles)


def late_chunks():
    n = lax.axis_size("dp")
    rank = lax.axis_index("dp")
    if n > 8:
        return jnp.arange(2, dtype=jnp.int32)
    mine = jnp.stack([rank ^ (2 * k) for k in range(n // 2)])
    return jnp.concatenate([mine, mine ^ 1]).astype(jnp.int32)


def late_sent(keep, send):
    n = lax.axis_size("dp")
    if n > 8:
        whole = jnp.concatenate([keep, send], axis=0)
        return None, lax.psum_scatter(whole, "dp", scatter_dimension=0, tiled=True).astype(f32)
    return keep, swapped(send, "dp", 1)


def late_sum(keep, came):
    return came if keep is None else keep.astype(f32) + came.astype(f32)


def late_near(keep, send):
    return late_sum(*late_sent(keep, send))


def late_far(total, dtype):
    n = lax.axis_size("dp")
    if n > 8:
        return total
    size = total.shape[0] * 2 // n
    low = total.astype(dtype)
    own = total[:size]
    for k in range(1, n // 2):
        own = own + swapped(low[k * size : (k + 1) * size], "dp", 2 * k).astype(f32)
    return own


def body(
    hidden_in,
    w_qkv,
    b_qkv,
    w_out,
    b_out,
    w_fc,
    b_fc,
    w_fc2,
    b_fc2,
    ln1_gain,
    ln1_bias,
    ln2_gain,
    ln2_bias,
    segment_ids,
    positions,
    cotangent,
):
    local_dim = w_qkv.shape[2]
    ff = w_fc.shape[1]
    own_dims = w_fc.shape[0]
    seq_len = positions.shape[0]
    halo = seq_len * 3 // 8
    qkv_dim = 3 * local_dim
    rank = lax.axis_index("tensor")
    places = jnp.stack([rank ^ at for at in SLOTS]).astype(jnp.int32)

    vectors = jnp.stack([b_out, b_fc2, ln1_gain, ln1_bias, ln2_gain, ln2_bias], axis=1)
    vectors = jnp.pad(vectors, ((0, 0), (0, 122)))
    block = jnp.concatenate(
        [
            jnp.transpose(w_qkv, (1, 0, 2)).reshape(own_dims, qkv_dim),
            w_out.T,
            vectors,
        ],
        axis=1,
    )
    x_far, g_far = swapped(hidden_in, "tensor", 2), swapped(cotangent, "tensor", 2)
    x_near, g_near = swapped(hidden_in, "tensor", 1), swapped(cotangent, "tensor", 1)
    pieces, starts, x_far = ring_gather(block, "dp", x_far)
    ff_w = lax.all_gather(jnp.concatenate([w_fc, w_fc2.T], axis=1), "dp", axis=0, tiled=True)
    x_blocks = gather_rows(hidden_in, x_near, x_far)

    cos_t, sin_t = rope_tables(positions)
    lo = halo + jnp.arange(seq_len, dtype=jnp.int32) - positions
    first = lo[::BLK] // BLK
    lo_row = lo.reshape(1, seq_len)

    q, k, v, right, x_all, normed_one, stats, wt, vec = project(
        starts,
        places,
        x_blocks,
        b_qkv.astype(f32).reshape(qkv_dim, 1),
        cos_t,
        sin_t,
        pieces,
        0,
        local_dim,
        halo,
    )
    right, g_far = tied(right, g_far)
    left = passed_along(right, "dp", 1)
    g_blocks = gather_rows(cotangent, g_near, g_far)
    ff_out, u_two, g_all, ff_grads, ff_small = feed_forward(
        x_all, g_blocks, stats, b_fc.astype(f32).reshape(1, ff), vec, ff_w, ff
    )
    ff_sum = lax.psum_scatter(ff_grads, "dp", scatter_dimension=0, tiled=True)
    q, ff_out = tied(q, ff_out)

    o, lse = attention_forward(first, q, k, v, left, lo_row, halo)
    chunks = late_chunks()
    out_keep, out_send, do = branch_out(places, o, ff_out, g_all, wt)
    own_o, came_o, other_o = scatter_near(out_keep, out_send)
    dq_part, back = backward_left(first, q, left, lo_row, o, lse, do, halo)
    dq_part, back, other_o = tied(dq_part, back, other_o)
    far_o = swapped(other_o, "tensor", 2)
    back = passed_along(back, "dp", -1)
    dq, dk, dv = backward_own(first, q, k, v, lo_row, o, lse, do, dq_part, halo)
    back, dq, far_o = tied(back, dq, far_o)
    count = hidden_in.shape[0]
    summed = own_o[:count].astype(f32) + came_o[:count].astype(f32) + far_o.astype(f32)
    layer_out = (hidden_in.astype(f32) + summed + vec[0] + vec[1]).astype(bf16)

    u_keep, u_send, proj_grad, one_small, qkv_bias = input_gradient(
        places, dq, dk, dv, back, x_all, stats, u_two, wt, vec, cos_t, sin_t, halo
    )
    own_u, came_u, other_u = scatter_near(u_keep, u_send)
    proj_grad, ff_sum = tied(proj_grad, ff_sum)
    keep_a, send_a = weight_gradient(places, chunks, proj_grad, normed_one, 2 * local_dim, 0, own_dims)
    proj_grad, other_u, send_a = tied(proj_grad, other_u, send_a)
    keep_a, came_a = late_sent(keep_a, send_a)
    keep_b, send_b = weight_gradient(
        places,
        chunks,
        proj_grad,
        normed_one,
        local_dim,
        2,
        own_dims,
        o,
        g_all,
        (one_small, ff_small, qkv_bias),
    )
    send_b, came_a = tied(send_b, came_a)
    near_a = late_sum(keep_a, came_a)
    near_b = late_near(keep_b, send_b)
    far_u = swapped(other_u, "tensor", 2)
    late_a, far_u = tied(late_far(near_a, bf16), far_u)
    late_b = late_far(near_b, bf16)
    late_own = jnp.concatenate([late_a, late_b[:, :local_dim]], axis=1)

    input_grad = norm_back(own_u, came_u, far_u, hidden_in, stats, cotangent)
    late_b, ff_sum, input_grad = tied(late_b, ff_sum, input_grad)
    ff_own = ff_sum.astype(f32)
    vectors = late_b[:, 2 * local_dim :]
    norm_grads = summed_over(vectors, "tensor")[:, :4].T
    fc_count = ff // own_dims
    fc_b_total = vectors[:, 8 : 8 + fc_count].T.reshape(ff)
    qkv_b_total = vectors[:, 8 + fc_count : 8 + fc_count + qkv_dim // own_dims].T.reshape(3, local_dim)
    out_b_total = vectors[:, 4]

    return (
        layer_out,
        input_grad,
        jnp.transpose(late_own.reshape(own_dims, 3, local_dim), (1, 0, 2)),
        qkv_b_total,
        late_b[:, local_dim : 2 * local_dim].T,
        out_b_total,
        ff_own[:, :ff],
        fc_b_total,
        ff_own[:, ff:].T,
        out_b_total,
        norm_grads[0],
        norm_grads[1],
        norm_grads[2],
        norm_grads[3],
    )


def solution(mesh):
    in_specs = (
        P(("dp", "tensor"), None),
        P(None, "dp", "tensor"),
        P(None, "tensor"),
        P("tensor", "dp"),
        P("dp"),
        P("dp", "tensor"),
        P("tensor"),
        P("tensor", "dp"),
        P("dp"),
        P("dp"),
        P("dp"),
        P("dp"),
        P("dp"),
        P("dp"),
        P("dp"),
        P(("dp", "tensor"), None),
    )
    out_specs = (
        P(("dp", "tensor"), None),
        P(("dp", "tensor"), None),
        P(None, "dp", "tensor"),
        P(None, "tensor"),
        P("tensor", "dp"),
        P("dp"),
        P("dp", "tensor"),
        P("tensor"),
        P("tensor", "dp"),
        P("dp"),
        P("dp"),
        P("dp"),
        P("dp"),
        P("dp"),
    )
    return jax.shard_map(body, mesh=mesh, in_specs=in_specs, out_specs=out_specs, check_vma=False)
```
